128 devices in a mesh: rep: 8 (over z, y_lo), sp: 16 (over y_hi, x, core).
Axes of the slice: x: 4, y: 4 (y_hi: 2, y_lo: 2; y = y_hi * 2 + y_lo), z: 4, core: 2. Of those that a mesh axis runs over, the one named last changes fastest.
Arguments:
- features: bfloat16 [8, 48, 72, 2048], P('rep', 'sp'), may hold values from -6 to 6
- atrous_weight: bfloat16 [27, 2048, 256], P(None, None, 'sp'), may hold values from -0.046875 to 0.046875
- point_weight: bfloat16 [2048, 256], P(None, 'sp'), may hold values from -0.125 to 0.125
- proj_weight: bfloat16 [1024, 256], replicated, may hold values from -0.1875 to 0.1875
- cotangent: bfloat16 [8, 48, 72, 256], P('rep', 'sp'), may hold values from -6 to 6
Outputs:
- projected: bfloat16 [8, 48, 72, 256], P('rep', 'sp')
- input_grad: bfloat16 [8, 48, 72, 2048], P('rep', 'sp')
- grad_point: float32 [2048, 256], P('sp')
- grad_atrous: float32 [27, 2048, 256], P(None, 'sp')
- grad_proj: float32 [1024, 256], replicated
The draws below stay inside these ranges and needn't reach their ends.
All inputs are finite; a program needn't handle non-finite values.
Results may differ from the reference program's by a relative error of at most 0.02.
Values may be sent and summed in bfloat16 or wider, within the bound.
No kernel may reach another device: no remote copies, remote signals or barrier semaphores. Data moves between devices by JAX's collectives and lax.ppermute only.
A program may use at most 192 MiB of HBM per device.

```python
import jax
import jax.numpy as jnp
from jax import lax

C = 2048
F = 256
F2 = 256
FIRST_DILATION = 6
SECOND_DILATION = 12
THIRD_DILATION = 18
H = 48
W = 72
BATCH = 8


def level_of(rng, extent, cuts, least, largest):
    def one(position, parts):
        draws = jax.random.uniform(jax.random.fold_in(jax.random.fold_in(rng, 6), position), (parts,), jnp.float32, least / len(cuts), largest / len(cuts))
        return jnp.repeat(jnp.exp(draws), extent[position] // parts).reshape((-1,) + (1,) * (len(extent) - position - 1))

    gain = one(*cuts[0])
    for cut in cuts[1:]:
        gain = gain * one(*cut)
    return gain


def noise(rng, extent, deviation, most, pieces=(), dtype=jnp.bfloat16):
    array = deviation * jax.random.normal(rng, extent, jnp.float32)
    if pieces:
        array = array * level_of(rng, extent, pieces, -0.22, 0.18)
    return jnp.clip(array, -most, most).astype(dtype)


def setup_inputs(seed: int = 0) -> dict:
    key_list = jax.random.split(jax.random.key(seed), 6)
    return {
        "features": noise(key_list[0], (BATCH, H, W, C), 1.0, 6.0, ((0, 8), (1, 16))),
        "atrous_weight": noise(key_list[1], (27, C, F), (9 * C) ** -0.5, 0.046875, ((2, 16),)),
        "point_weight": noise(key_list[2], (C, F), C ** -0.5, 0.125, ((1, 16),)),
        "proj_weight": noise(key_list[3], (4 * F, F2), (4 * F) ** -0.5, 0.1875),
        "cotangent": noise(key_list[4], (BATCH, H, W, F2), 1.0, 6.0, ((0, 8), (1, 16))),
    }


def shifted(field, off_row, off_col):
    ar = abs(off_row)
    ac = abs(off_col)
    padded = jnp.pad(field, ((ar, ar), (ac, ac), (0, 0)))
    return padded[ar + off_row:ar + off_row + field.shape[0], ac + off_col:ac + off_col + field.shape[1]]


def slope_of(value):
    sig = jax.nn.sigmoid(value)
    return sig + value * sig * (1.0 - sig)


def tap_list():
    kernel_taps = []
    for group_members, dilation_rate in enumerate((FIRST_DILATION, SECOND_DILATION, THIRD_DILATION)):
        for kernel_row in (-1, 0, 1):
            for kernel_column in (-1, 0, 1):
                kernel_taps.append((group_members, kernel_row * dilation_rate, kernel_column * dilation_rate))
    return kernel_taps


def flat_dot(left, right):
    return jnp.dot(left.reshape(-1, left.shape[-1]).T, right.reshape(-1, right.shape[-1]), preferred_element_type=jnp.float32)


def reference(features, atrous_weight, point_weight, proj_weight, cotangent):
    kernel_taps = tap_list()

    def sample(carry, inputs):
        grad_p, grad_a, grad_j = carry
        xs, cots = inputs
        pres = [jnp.dot(xs, point_weight, preferred_element_type=jnp.float32)]
        for group_members in range(3):
            total = jnp.zeros((H, W, F), jnp.float32)
            for t, (g, output_row, output_column) in enumerate(kernel_taps):
                if g == group_members:
                    total = total + jnp.dot(shifted(xs, output_row, output_column), atrous_weight[t], preferred_element_type=jnp.float32)
            pres.append(total)
        pre_low = jnp.concatenate(pres, -1).astype(jnp.bfloat16)
        pre_wide = pre_low.astype(jnp.float32)
        acts = jax.nn.silu(pre_wide).astype(jnp.bfloat16)
        out_pre = jnp.dot(acts, proj_weight, preferred_element_type=jnp.float32)
        projected = jax.nn.silu(out_pre).astype(jnp.bfloat16)
        dout = (cots.astype(jnp.float32) * slope_of(out_pre)).astype(jnp.bfloat16)
        grad_j = grad_j + flat_dot(acts, dout)
        dacts = jnp.dot(dout, proj_weight.T, preferred_element_type=jnp.float32)
        dacts = (dacts * slope_of(pre_wide)).astype(jnp.bfloat16)
        dpre = [dacts[..., j * F:(j + 1) * F] for j in range(4)]
        grad_p = grad_p + flat_dot(xs, dpre[0])
        tap_grads = []
        back = jnp.dot(dpre[0], point_weight.T, preferred_element_type=jnp.float32)
        for t, (g, output_row, output_column) in enumerate(kernel_taps):
            tap_grads.append(flat_dot(shifted(xs, output_row, output_column), dpre[g + 1]))
            back = back + shifted(jnp.dot(dpre[g + 1], atrous_weight[t].T, preferred_element_type=jnp.float32), -output_row, -output_column)
        grad_a = grad_a + jnp.stack(tap_grads, 0)
        return (grad_p, grad_a, grad_j), (projected, back.astype(jnp.bfloat16))

    init = (jnp.zeros((C, F), jnp.float32), jnp.zeros((27, C, F), jnp.float32), jnp.zeros((4 * F, F2), jnp.float32))
    (grad_p, grad_a, grad_j), (projected, input_grad) = lax.scan(sample, init, (features, cotangent))
    return projected, input_grad, grad_p / BATCH, grad_a / BATCH, grad_j / BATCH
```

```python
import functools

import jax
import jax.numpy as jnp
import numpy as np
from jax import lax
from jax.experimental import pallas as pl
from jax.experimental.pallas import tpu as pltpu
from jax.sharding import Mesh
from jax.sharding import PartitionSpec as P

DILATIONS = (6, 12, 18)
SETS = 2
CHIPS = 8
CELLS = 216
PADDED = 224
WIDTH = 72
HALO = 3
K = 512
COLS = 1792
BF16 = jnp.bfloat16
F32 = jnp.float32


def column_order():
    def tap(g, ky, kx):
        return 1 + 9 * g + 3 * (ky + 1) + (kx + 1)

    order = []
    for g in range(3):
        for ky in (-1, 0, 1):
            order += [tap(g, ky, -1), tap(g, ky, 1)]
    order += [tap(0, 0, 0), tap(1, 0, 0), tap(2, 0, 0), 0]
    for g in range(3):
        order += [tap(g, -1, 0), tap(g, 1, 0)]
    return order


ORDER = column_order()


def cell_column():
    row = lax.broadcasted_iota(jnp.int32, (CELLS, 128), 0)
    return jnp.where(row >= 144, row - 144, jnp.where(row >= 72, row - 72, row))


def low_lanes():
    return lax.broadcasted_iota(jnp.int32, (CELLS, 128), 1) < 64


def swap_halves(v):
    return pltpu.roll(v, 64, 1)


def forward_kernel(core, own, other, wt, out, a0, a1, a2, m0, m1, m2, b01, b2p):
    a, m = (a0, a1, a2), (m0, m1, m2)
    column = cell_column()
    low = low_lanes()
    me = core[0]
    zeros = jnp.zeros((HALO, CELLS, 128), F32)
    for which, x in enumerate((own, other)):
        slot = me if which == 0 else 1 - me
        for g in range(3):
            a[g][...] = jnp.zeros((CHIPS + 2 * HALO, CELLS, 128), F32)
            m[g][:HALO] = zeros
            m[g][HALO + CHIPS :] = zeros

        def step(i, _):
            rows = x[pl.ds(pl.multiple_of(i * 2 * CELLS, 2 * CELLS), 2 * CELLS), :]
            y = lax.dot_general(
                rows, wt[...], (((1,), (1,)), ((), ())), preferred_element_type=F32
            )
            for sub in range(2):
                j = 2 * i + sub
                part = y[sub * CELLS : (sub + 1) * CELLS]
                for g in range(3):
                    for n, ky in enumerate((-1, 0, 1)):
                        col = (3 * g + n) * 128
                        a[g][HALO + j - ky * (g + 1)] += part[:, col : col + 128]
                b01[j] = part[:, 9 * 128 : 10 * 128]
                b2p[j] = part[:, 10 * 128 : 11 * 128]
                for g in range(3):
                    m[g][HALO + j] = part[:, (11 + g) * 128 : (12 + g) * 128]
            return 0

        lax.fori_loop(0, CHIPS // 2, step, 0)

        def finish(j, _):
            totals = []
            for g, d in enumerate(DILATIONS):
                v = a[g][HALO + j]
                minus = jnp.where(column >= d, pltpu.roll(v, d, 0), 0.0)
                plus = jnp.where(column < WIDTH - d, pltpu.roll(v, CELLS - d, 0), 0.0)
                s = jnp.where(
                    low,
                    minus + m[g][HALO + j - (g + 1)],
                    plus + m[g][HALO + j + (g + 1)],
                )
                totals.append(s + swap_halves(s))
            c01 = swap_halves(b01[j])
            c2p = swap_halves(b2p[j])
            first = jnp.where(low, c2p, totals[0] + c01)
            second = jnp.where(low, totals[1] + c01, totals[2] + c2p)
            out[j, slot] = jnp.concatenate([first, second], 1).astype(BF16)
            return 0

        lax.fori_loop(0, CHIPS, finish, 0)


def forward(core, own, other, wt):
    vmem = pl.BlockSpec(memory_space=pltpu.VMEM)
    big = pltpu.VMEM((CHIPS + 2 * HALO, CELLS, 128), F32)
    small = pltpu.VMEM((CHIPS, CELLS, 128), F32)
    return pl.pallas_call(
        forward_kernel,
        out_shape=jax.ShapeDtypeStruct((CHIPS, SETS, CELLS, 256), BF16),
        in_specs=[pl.BlockSpec(memory_space=pltpu.SMEM), vmem, vmem, vmem],
        out_specs=vmem,
        scratch_shapes=[big] * 6 + [small] * 2,
        compiler_params=pltpu.CompilerParams(vmem_limit_bytes=56 << 20),
        cost_estimate=pl.CostEstimate(
            flops=2 * 3456 * K * COLS, bytes_accessed=8 << 20, transcendentals=0
        ),
    )(core, own, other, wt)


def sigmoid(v):
    return 1.0 / (1.0 + jnp.exp(-v))


def middle_kernel(got, proj, cot, projected, send, grad):
    parts = []
    for yh in range(2):
        for c in range(2):
            total = got[yh * 8 + c].astype(F32)
            for x in range(1, 4):
                total = total + got[yh * 8 + x * 2 + c].astype(F32)
            parts.append(total)
    pre = jnp.concatenate(parts, 1).astype(BF16).astype(F32)
    sig = sigmoid(pre)
    acts = (pre * sig).astype(BF16)
    slope = sig + pre * sig * (1.0 - sig)
    weight = proj[...]
    out_pre = jnp.dot(acts, weight, preferred_element_type=F32)
    osig = sigmoid(out_pre)
    projected[...] = (out_pre * osig).astype(BF16)
    dout = (cot[...].astype(F32) * (osig + out_pre * osig * (1.0 - osig))).astype(BF16)
    grad[...] = lax.dot_general(
        acts, dout, (((0,), (0,)), ((), ())), preferred_element_type=F32
    )
    dacts = lax.dot_general(
        dout, weight, (((1,), (1,)), ((), ())), preferred_element_type=F32
    )
    dpre = (dacts * slope).astype(BF16)
    for yh in range(2):
        for c in range(2):
            q = 2 * yh + c
            for x in range(4):
                send[yh * 8 + x * 2 + c] = dpre[:, q * 256 : (q + 1) * 256]


def middle(got, proj, cot):
    vmem = pl.BlockSpec(memory_space=pltpu.VMEM)
    return pl.pallas_call(
        middle_kernel,
        out_shape=(
            jax.ShapeDtypeStruct((CELLS, 256), BF16),
            jax.ShapeDtypeStruct((16, CELLS, 256), BF16),
            jax.ShapeDtypeStruct((1024, 256), F32),
        ),
        in_specs=[vmem] * 3,
        out_specs=(vmem,) * 3,
        compiler_params=pltpu.CompilerParams(vmem_limit_bytes=48 << 20),
    )(got, proj, cot)


def spread(got, slot, c, e, f01, f2p, dup):
    column = cell_column()
    low = low_lanes()
    halo = jnp.zeros((HALO, PADDED, 128), BF16)
    tail = jnp.zeros((PADDED - CELLS, 128), BF16)
    for g in range(3):
        for ref in (c[g], dup[g]):
            ref[:HALO] = halo
            ref[HALO + CHIPS :] = halo

    def put(ref, j, v):
        ref[j, :CELLS] = v.astype(BF16)
        ref[j, CELLS:] = tail

    def step(j, _):
        block = got[2 * j + slot]
        lo = block[:, :128].astype(F32)
        hi = block[:, 128:].astype(F32)
        rlo, rhi = swap_halves(lo), swap_halves(hi)
        twice = (jnp.where(low, rlo, lo), jnp.where(low, hi, rhi), jnp.where(low, rhi, hi))
        for g, d in enumerate(DILATIONS):
            v = twice[g]
            minus = jnp.where(column < WIDTH - d, pltpu.roll(v, CELLS - d, 0), 0.0)
            plus = jnp.where(column >= d, pltpu.roll(v, d, 0), 0.0)
            put(c[g], HALO + j, jnp.where(low, minus, plus))
            put(dup[g], HALO + j, v)
        put(f01, j, jnp.where(low, rlo, rhi))
        put(f2p, j, jnp.where(low, rhi, rlo))
        return 0

    lax.fori_loop(0, CHIPS, step, 0)
    lanes = lax.broadcasted_iota(jnp.int32, (PADDED, 128), 1) < 64

    def mix(j, _):
        for g in range(3):
            up = dup[g][HALO + j + g + 1].astype(F32)
            down = dup[g][HALO + j - g - 1].astype(F32)
            e[g][j] = jnp.where(lanes, up, down).astype(BF16)
        return 0

    lax.fori_loop(0, CHIPS, mix, 0)


def spread_scratch():
    halo = pltpu.VMEM((CHIPS + 2 * HALO, PADDED, 128), BF16)
    plain = pltpu.VMEM((CHIPS, PADDED, 128), BF16)
    return [halo] * 6 + [plain] * 5


def spread_columns(scratch, first, count):
    c, e, f01, f2p = scratch[0:3], scratch[6:9], scratch[9], scratch[10]

    def flat(v):
        return v.reshape(count * PADDED, 128)

    blocks = []
    for g in range(3):
        for ky in (-1, 0, 1):
            begin = HALO + first - ky * (g + 1)
            blocks.append(flat(c[g][pl.ds(begin, count)]))
    for ref in (f01, f2p, e[0], e[1], e[2]):
        blocks.append(flat(ref[pl.ds(first, count)]))
    return blocks


def kernel_grad_kernel(core, got, xt, out, total, *scratch):
    me = core[0]
    for which in range(2):
        slot = me if which == 0 else 1 - me
        spread(got, slot, scratch[0:3], scratch[6:9], scratch[9], scratch[10], scratch[3:6])
        left = xt[which]
        blocks = spread_columns(scratch, 0, CHIPS)
        for n in range(7):
            right = jnp.concatenate([blocks[2 * n], blocks[2 * n + 1]], 1)
            part = jnp.dot(left, right, preferred_element_type=F32)
            cols = slice(n * 256, (n + 1) * 256)
            if which == 0:
                total[:, cols] = part
            else:
                part = (part + total[:, cols]).astype(BF16)
                for q in range(4):
                    out[:, q, :, cols] = part[q * 128 : (q + 1) * 128].reshape(8, 16, 256)


def kernel_grad(core, got, xt):
    vmem = pl.BlockSpec(memory_space=pltpu.VMEM)
    return pl.pallas_call(
        kernel_grad_kernel,
        out_shape=jax.ShapeDtypeStruct((8, 4, 16, COLS), BF16),
        in_specs=[pl.BlockSpec(memory_space=pltpu.SMEM), vmem, vmem],
        out_specs=vmem,
        scratch_shapes=[pltpu.VMEM((K, COLS), F32)] + spread_scratch(),
        compiler_params=pltpu.CompilerParams(vmem_limit_bytes=56 << 20),
        cost_estimate=pl.CostEstimate(
            flops=2 * 3456 * K * COLS, bytes_accessed=8 << 20, transcendentals=0
        ),
    )(core, got, xt)


def feature_grad_kernel(core, got, wt, own, other, *scratch):
    me = core[0]
    for which, out in ((1, other), (0, own)):
        slot = me if which == 0 else 1 - me
        spread(got, slot, scratch[0:3], scratch[6:9], scratch[9], scratch[10], scratch[3:6])

        def step(i, _):
            left = jnp.concatenate(spread_columns(scratch, 2 * i, 2), 1)
            part = jnp.dot(left, wt[...], preferred_element_type=F32)
            for sub in range(2):
                out[2 * i + sub] = part[sub * PADDED : sub * PADDED + CELLS].astype(BF16)
            return 0

        lax.fori_loop(0, CHIPS // 2, step, 0)


def feature_grad(core, got, wt):
    vmem = pl.BlockSpec(memory_space=pltpu.VMEM)
    return pl.pallas_call(
        feature_grad_kernel,
        out_shape=(jax.ShapeDtypeStruct((CHIPS, CELLS, K), BF16),) * 2,
        in_specs=[pl.BlockSpec(memory_space=pltpu.SMEM), vmem, vmem],
        out_specs=(vmem,) * 2,
        scratch_shapes=spread_scratch(),
        compiler_params=pltpu.CompilerParams(vmem_limit_bytes=56 << 20),
        cost_estimate=pl.CostEstimate(
            flops=2 * 3456 * K * COLS, bytes_accessed=8 << 20, transcendentals=0
        ),
    )(core, got, wt)


def place_matrix():
    place = np.zeros((4, 128, 512), np.float32)
    for yh in range(2):
        for c in range(2):
            for tap in range(2):
                for x in range(4):
                    for i in range(16):
                        place[2 * yh + c, tap * 64 + x * 16 + i, tap * 256 + yh * 128 + x * 32 + c * 16 + i] = 0.125
    return place.reshape(512, 512)


def place_kernel(got, place, point, atrous):
    for v in range(14):
        lanes = slice(v * 128, (v + 1) * 128)
        left = jnp.concatenate([got[:, q, :, lanes].reshape(128, 128) for q in range(4)], 1)
        wide = jnp.dot(left, place[...], preferred_element_type=F32)
        for half in range(2):
            tap = ORDER[2 * v + half]
            part = wide[:, half * 256 : (half + 1) * 256]
            if tap == 0:
                point[...] = part
            else:
                atrous[tap - 1] = part


def place_grads(got):
    vmem = pl.BlockSpec(memory_space=pltpu.VMEM)
    return pl.pallas_call(
        place_kernel,
        out_shape=(
            jax.ShapeDtypeStruct((128, 256), F32),
            jax.ShapeDtypeStruct((27, 128, 256), F32),
        ),
        in_specs=[vmem] * 2,
        out_specs=(vmem,) * 2,
        compiler_params=pltpu.CompilerParams(vmem_limit_bytes=40 << 20),
    )(got, jnp.asarray(place_matrix(), BF16))


def shards(features, atrous_weight, point_weight, proj_weight, cotangent):
    core = lax.axis_index("c").astype(jnp.int32).reshape(1)

    atrous_t = jnp.transpose(atrous_weight, (0, 2, 1))
    point_t = jnp.transpose(point_weight, (1, 0))[None]
    every_t = [point_t] + [atrous_t[t : t + 1] for t in range(27)]
    stacked = jnp.concatenate([every_t[t] for t in ORDER], 0)
    w_send = jnp.transpose(stacked.reshape(28, 16, 2, 4, 2, 128), (3, 0, 1, 2, 4, 5))
    w_got = lax.all_to_all(w_send.reshape(4, 28, 16, K), "x", 0, 0, tiled=True)
    wt = jnp.transpose(w_got, (1, 0, 2, 3)).reshape(COLS, K)

    by_column = jnp.transpose(features.reshape(CELLS, 2, 4, 2, 128), (2, 0, 1, 3, 4)).reshape(4, CELLS, K)
    x_send = jnp.broadcast_to(by_column[None], (2, 4, CELLS, K)).reshape(CHIPS, CELLS, K)
    own = lax.all_to_all(x_send, ("yh", "x"), 0, 0, tiled=True)
    other = lax.ppermute(own, "c", [(0, 1), (1, 0)])

    partial = forward(core, own.reshape(CHIPS * CELLS, K), other.reshape(CHIPS * CELLS, K), wt)
    got = lax.all_to_all(partial.reshape(16, CELLS, 256), ("yh", "x", "c"), 0, 0, tiled=True)

    proj = proj_weight.reshape(4, 2, 4, 2, 16, 256).transpose(1, 3, 0, 2, 4, 5).reshape(1024, 256)
    projected, d_send, proj_part = middle(got, proj, cotangent.reshape(CELLS, 256))
    proj_sum = lax.psum(proj_part, ("z", "yl", "yh", "x", "c"))
    grad_proj = (
        proj_sum.reshape(2, 2, 4, 4, 16, 256).transpose(2, 0, 3, 1, 4, 5).reshape(1024, 256) * 0.125
    )
    dpre = lax.all_to_all(d_send, ("yh", "x", "c"), 0, 0, tiled=True)

    def turned(v):
        padded = jnp.pad(v, ((0, 0), (0, PADDED - CELLS), (0, 0)))
        return jnp.transpose(padded.reshape(CHIPS * PADDED, K))

    xt = jnp.stack([turned(own), turned(other)])
    g_part = kernel_grad(core, dpre, xt)
    g_got = lax.all_to_all(g_part.reshape(32, 16, COLS), ("z", "yl", "yh", "c"), 0, 0, tiled=True)
    g_sum = jnp.sum(g_got.reshape(8, 4, 16, COLS).astype(F32), 0).astype(BF16)
    g_all = lax.all_to_all(
        jnp.broadcast_to(g_sum[None], (8, 4, 16, COLS)), ("z", "yl"), 0, 0, tiled=True
    )
    grad_point, grad_atrous = place_grads(g_all)

    back_own, back_other = feature_grad(core, dpre, wt)
    back_got = lax.ppermute(back_other, "c", [(0, 1), (1, 0)])
    back = (back_own.astype(F32) + back_got.astype(F32)).astype(BF16)
    b_got = lax.all_to_all(back, ("yh", "x"), 0, 0, tiled=True).reshape(2, 4, CELLS, 2, 256)
    b_sum = (b_got[0].astype(F32) + b_got[1].astype(F32)).astype(BF16)
    input_grad = jnp.transpose(b_sum, (1, 2, 0, 3)).reshape(1, 3, WIDTH, 2048)

    return (
        projected.reshape(1, 3, WIDTH, 256),
        input_grad,
        grad_point,
        grad_atrous,
        grad_proj,
    )


def solution(mesh):
    fine = Mesh(mesh.devices.reshape(4, 2, 2, 4, 2), ("z", "yl", "yh", "x", "c"))
    rep, sp = ("z", "yl"), ("yh", "x", "c")
    in_specs = (
        P(rep, sp, None, None),
        P(None, None, sp),
        P(None, sp),
        P(),
        P(rep, sp, None, None),
    )
    out_specs = (
        P(rep, sp, None, None),
        P(rep, sp, None, None),
        P(sp, None),
        P(None, sp, None),
        P(),
    )
    return jax.shard_map(shards, mesh=fine, in_specs=in_specs, out_specs=out_specs, check_vma=False)
```

```python
import jax
import jax.numpy as jnp
from jax import lax
from jax.experimental import pallas as pl
from jax.experimental.pallas import tpu as pltpu
from jax.sharding import Mesh
from jax.sharding import PartitionSpec as P

DILATIONS = (6, 12, 18)
CHIPS = 8
CELLS = 216
PADDED = 224
WIDTH = 72
HALO = 3
K = 512
TAPS = 28
COLS = TAPS * 128
QUARTER = TAPS // 4
BF16 = jnp.bfloat16
F32 = jnp.float32
VMEM = pl.BlockSpec(memory_space=pltpu.VMEM)
SMEM = pl.BlockSpec(memory_space=pltpu.SMEM)


def tap_of(g, ky, kx):
    return 1 + 9 * g + 3 * (ky + 1) + (kx + 1)


def tap_pairs():
    def tap(g, ky, kx):
        return (tap_of(g, ky, kx), g, ky, kx)

    pairs = [((0, -1, 0, 0), tap(0, 0, 0)), (tap(1, 0, 0), tap(2, 0, 0))]
    for ky in (0, -1, 1):
        for g in range(3):
            pairs.append((tap(g, ky, -1), tap(g, ky, 1)))
    for ky in (-1, 1):
        pairs.append((tap(0, ky, 0), tap(1, ky, 0)))
    pairs.append((tap(2, -1, 0), tap(2, 1, 0)))
    return pairs


PAIRS = tap_pairs()


def params(mib):
    return pltpu.CompilerParams(vmem_limit_bytes=mib << 20)


def cost(flops, nbytes):
    return pl.CostEstimate(flops=flops, bytes_accessed=nbytes, transcendentals=0)


CONV_COST = cost(2 * 1728 * K * COLS, 8 << 20)


def cell_column(rows):
    row = lax.broadcasted_iota(jnp.int32, (rows, 128), 0)
    return jnp.where(row >= 144, row - 144, jnp.where(row >= 72, row - 72, row))


def split_features_kernel(x, out):
    for col in range(4):
        for yh in range(2):
            part = x[:, (yh * 4 + col) * 256 : (yh * 4 + col + 1) * 256]
            for dest in range(2):
                out[dest * 4 + col, :, yh * 256 : (yh + 1) * 256] = part


def split_features(x):
    return pl.pallas_call(
        split_features_kernel,
        out_shape=jax.ShapeDtypeStruct((CHIPS, CELLS, K), BF16),
        in_specs=[VMEM],
        out_specs=VMEM,
        compiler_params=params(16),
        cost_estimate=cost(0, 3 << 20),
    )(x)


def split_weights_kernel(place, point, atrous, out0, out1, out2, out3, taps, sem):
    z, x = place[0], place[1]
    begin = jnp.where(z == 0, 0, QUARTER * z - 1)
    copy = pltpu.make_async_copy(atrous.at[pl.ds(begin, QUARTER)], taps.at[pl.ds(1, QUARTER)], sem)
    copy.start()
    taps[0] = point[...]
    copy.wait()
    first = jnp.where(z == 0, 0, 1)
    for d, out in enumerate((out0, out1, out2, out3)):
        col = lax.rem(x + d, 4)
        for yh in range(2):
            lanes = pl.ds(pl.multiple_of((yh * 4 + col) * 256, 256), 256)
            for t in range(QUARTER):
                out[t, :, yh * 256 : (yh + 1) * 256] = taps[first + t, :, lanes]


def split_weights(place, point, atrous):
    return pl.pallas_call(
        split_weights_kernel,
        out_shape=(jax.ShapeDtypeStruct((QUARTER, 16, K), BF16),) * 4,
        in_specs=[SMEM, VMEM, pl.BlockSpec(memory_space=pl.ANY)],
        out_specs=(VMEM,) * 4,
        scratch_shapes=[pltpu.VMEM((QUARTER + 1, 16, 2048), BF16), pltpu.SemaphoreType.DMA],
        compiler_params=params(16),
        cost_estimate=cost(0, 1 << 20),
    )(place, point, atrous)


def join_weights_kernel(place, *refs):
    out = refs[8]
    z, me = place[0], place[2]
    for which in range(2):
        c = me if which == 0 else 1 - me
        for d in range(4):
            quarter = lax.rem(z + 4 - d, 4)
            block = refs[which * 4 + d]
            for x in range(4):
                for t in range(QUARTER):
                    out[quarter * QUARTER + t, x, c] = block[x, t]


def join_weights(place, blocks):
    return pl.pallas_call(
        join_weights_kernel,
        out_shape=jax.ShapeDtypeStruct((TAPS, 4, 2, 16, K), BF16),
        in_specs=[SMEM] + [VMEM] * 8,
        out_specs=VMEM,
        compiler_params=params(24),
        cost_estimate=cost(0, 8 << 20),
    )(place, *blocks)


def stack_columns_kernel(place, b0, b1, b2, b3, out):
    for d, block in enumerate((b0, b1, b2, b3)):
        out[lax.rem(place[1] + 4 - d, 4)] = block[...]


def stack_columns(place, blocks):
    return pl.pallas_call(
        stack_columns_kernel,
        out_shape=jax.ShapeDtypeStruct((4, QUARTER, 16, K), BF16),
        in_specs=[SMEM] + [VMEM] * 4,
        out_specs=VMEM,
        compiler_params=params(16),
        cost_estimate=cost(0, 1 << 20),
    )(place, *blocks)


def forward_kernel(x, wt, out, xs, acc):
    for j in range(CHIPS):
        xs[j, :CELLS] = x[j]
        xs[j, CELLS:] = jnp.zeros((PADDED - CELLS, K), BF16)

    def span(g, ky):
        return max(0, ky * (g + 1)), CHIPS + min(0, ky * (g + 1))

    for pair in PAIRS:
        begin = min(span(g, ky)[0] for _, g, ky, _ in pair)
        end = max(span(g, ky)[1] for _, g, ky, _ in pair)
        rows = xs[begin:end].reshape((end - begin) * PADDED, K)
        right = jnp.concatenate([wt[t] for t, _, _, _ in pair], 0)
        y = lax.dot_general(rows, right, (((1,), (1,)), ((), ())), preferred_element_type=F32)
        y = y.reshape(end - begin, PADDED, 256)
        for half, (_, g, ky, kx) in enumerate(pair):
            which = 3 if g < 0 else (g if kx == 0 else 4 + 2 * g + (kx + 1) // 2)
            lo, hi = span(g, ky)
            part = y[lo - begin : hi - begin, :, half * 128 : (half + 1) * 128]
            to = slice(lo - ky * (g + 1), hi - ky * (g + 1))
            if ky == 0:
                acc[which, to] = part
            else:
                acc[which, to] += part

    column = cell_column(PADDED)

    def finish(j, _):
        parts = [acc[3, j]]
        for g, d in enumerate(DILATIONS):
            minus = pltpu.roll(acc[4 + 2 * g, j], d, 0)
            plus = pltpu.roll(acc[5 + 2 * g, j], PADDED - d, 0)
            parts.append(
                acc[g, j]
                + jnp.where(column >= d, minus, 0.0)
                + jnp.where(column < WIDTH - d, plus, 0.0)
            )
        out[j] = jnp.concatenate(parts, 1).astype(BF16)[:CELLS]
        return 0

    lax.fori_loop(0, CHIPS, finish, 0)


def forward(x, wt):
    return pl.pallas_call(
        forward_kernel,
        out_shape=jax.ShapeDtypeStruct((CHIPS, CELLS, 512), BF16),
        in_specs=[VMEM] * 2,
        out_specs=VMEM,
        scratch_shapes=[
            pltpu.VMEM((CHIPS, PADDED, K), BF16),
            pltpu.VMEM((10, CHIPS, PADDED, 128), F32),
        ],
        compiler_params=params(56),
        cost_estimate=CONV_COST,
    )(x, wt)


def sigmoid(v):
    return 1.0 / (1.0 + jnp.exp(-v))


def middle_kernel(got, proj, cot, projected, send, grad):
    parts = []
    for yh in range(2):
        total = got[yh * 4].astype(F32)
        for x in range(1, 4):
            total = total + got[yh * 4 + x].astype(F32)
        parts.append(total)
    pre = jnp.concatenate(parts, 1).astype(BF16).astype(F32)
    sig = sigmoid(pre)
    acts = (pre * sig).astype(BF16)
    slope = sig + pre * sig * (1.0 - sig)
    weight = proj[...]
    out_pre = jnp.dot(acts, weight, preferred_element_type=F32)
    osig = sigmoid(out_pre)
    projected[...] = (out_pre * osig).astype(BF16)
    dout = (cot[...].astype(F32) * (osig + out_pre * osig * (1.0 - osig))).astype(BF16)
    dacts = lax.dot_general(
        dout, weight, (((1,), (1,)), ((), ())), preferred_element_type=F32
    )
    dpre = (dacts * slope).astype(BF16)
    for yh in range(2):
        for x in range(4):
            send[yh * 4 + x] = dpre[:, yh * 512 : (yh + 1) * 512]
    grad[...] = lax.dot_general(
        acts, dout, (((0,), (0,)), ((), ())), preferred_element_type=F32
    )


def middle(got, proj, cot):
    return pl.pallas_call(
        middle_kernel,
        out_shape=(
            jax.ShapeDtypeStruct((CELLS, 256), BF16),
            jax.ShapeDtypeStruct((CHIPS, CELLS, 512), BF16),
            jax.ShapeDtypeStruct((1024, 256), F32),
        ),
        in_specs=[VMEM] * 3,
        out_specs=(VMEM,) * 3,
        compiler_params=params(48),
    )(got, proj, cot)


SPREAD = [pltpu.VMEM((9, CHIPS + 2 * HALO, PADDED, 128), BF16), pltpu.VMEM((CHIPS, PADDED, 128), BF16)]


def spread(got, moved, point):
    column = cell_column(CELLS)
    for n in range(9):
        moved[n, :HALO] = jnp.zeros((HALO, PADDED, 128), BF16)
        moved[n, HALO + CHIPS :] = jnp.zeros((HALO, PADDED, 128), BF16)
    tail = jnp.zeros((PADDED - CELLS, 128), BF16)

    def step(j, _):
        point[j, :CELLS] = got[j, :, :128]
        point[j, CELLS:] = tail
        for g, d in enumerate(DILATIONS):
            v = got[j, :, (g + 1) * 128 : (g + 2) * 128]
            wide = v.astype(F32)
            minus = jnp.where(column < WIDTH - d, pltpu.roll(wide, CELLS - d, 0), 0.0)
            plus = jnp.where(column >= d, pltpu.roll(wide, d, 0), 0.0)
            for kx, part in enumerate((minus.astype(BF16), v, plus.astype(BF16))):
                moved[3 * g + kx, HALO + j, :CELLS] = part
                moved[3 * g + kx, HALO + j, CELLS:] = tail
        return 0

    lax.fori_loop(0, CHIPS, step, 0)


def spread_columns(moved, point, tap, first, count):
    _, g, ky, kx = tap
    if g < 0:
        v = point[pl.ds(first, count)]
    else:
        v = moved[3 * g + kx + 1, pl.ds(HALO + first - ky * (g + 1), count)]
    return v.reshape(count * PADDED, 128)


def kernel_grad_kernel(place, got, xt, keep, send, moved, point):
    spread(got, moved, point)
    c = place[2]
    for pair in PAIRS:
        right = jnp.concatenate([spread_columns(moved, point, tap, 0, CHIPS) for tap in pair], 1)
        part = jnp.dot(xt[...], right, preferred_element_type=F32).astype(BF16)
        for half, tap in enumerate(pair):
            cols = slice(tap[0] * 128, (tap[0] + 1) * 128)
            for yh in range(2):
                for core in range(2):
                    row = (yh * 2 + core) * 128
                    block = part[row : row + 128, half * 128 : (half + 1) * 128].reshape(8, 16, 128)

                    @pl.when(c == core)
                    def _():
                        keep[:, yh, :, cols] = block

                    @pl.when(c != core)
                    def _():
                        send[:, yh, :, cols] = block


def kernel_grad(place, got, xt):
    return pl.pallas_call(
        kernel_grad_kernel,
        out_shape=(jax.ShapeDtypeStruct((8, 2, 16, COLS), BF16),) * 2,
        in_specs=[SMEM, VMEM, VMEM],
        out_specs=(VMEM,) * 2,
        scratch_shapes=SPREAD,
        compiler_params=params(56),
        cost_estimate=CONV_COST,
    )(place, got, xt)


def feature_grad_kernel(got, wt, out, moved, point):
    spread(got, moved, point)

    def step(i, _):
        cols, rows = [], []
        for pair in PAIRS:
            for tap in pair:
                cols.append(spread_columns(moved, point, tap, 2 * i, 2))
                rows.append(wt[tap[0]])
        part = jnp.dot(
            jnp.concatenate(cols, 1), jnp.concatenate(rows, 0), preferred_element_type=F32
        )
        for sub in range(2):
            out[2 * i + sub] = part[sub * PADDED : sub * PADDED + CELLS].astype(BF16)
        return 0

    lax.fori_loop(0, CHIPS // 2, step, 0)


def feature_grad(got, wt):
    return pl.pallas_call(
        feature_grad_kernel,
        out_shape=jax.ShapeDtypeStruct((CHIPS, CELLS, K), BF16),
        in_specs=[VMEM, VMEM],
        out_specs=VMEM,
        scratch_shapes=SPREAD,
        compiler_params=params(56),
        cost_estimate=CONV_COST,
    )(got, wt)


def place_grads_kernel(place, *refs):
    blocks, point, atrous = refs[:8], refs[8], refs[9]
    z, yl = place[0], place[3]
    for d in range(4):
        for l in range(2):
            rep = 2 * lax.rem(z + 4 - d, 4) + lax.rem(yl + 2 - l, 2)
            rows = pl.ds(pl.multiple_of(rep * 16, 16), 16)
            block = blocks[2 * d + l]
            for yh in range(2):
                cols = slice(yh * 128, (yh + 1) * 128)
                for t in range(TAPS):
                    part = block[yh, :, t * 128 : (t + 1) * 128].astype(F32) * 0.125
                    if t == 0:
                        point[rows, cols] = part
                    else:
                        atrous[t - 1, rows, cols] = part


def place_grads(place, blocks):
    return pl.pallas_call(
        place_grads_kernel,
        out_shape=(
            jax.ShapeDtypeStruct((128, 256), F32),
            jax.ShapeDtypeStruct((27, 128, 256), F32),
        ),
        in_specs=[SMEM] + [VMEM] * 8,
        out_specs=(VMEM,) * 2,
        compiler_params=params(40),
    )(place, *blocks)


def join_features_kernel(got, out):
    for x in range(4):
        total = (got[x].astype(F32) + got[4 + x].astype(F32)).astype(BF16)
        for yh in range(2):
            out[:, (yh * 4 + x) * 256 : (yh * 4 + x + 1) * 256] = total[:, yh * 256 : (yh + 1) * 256]


def join_features(got):
    return pl.pallas_call(
        join_features_kernel,
        out_shape=jax.ShapeDtypeStruct((CELLS, 2048), BF16),
        in_specs=[VMEM],
        out_specs=VMEM,
        compiler_params=params(16),
    )(got)


def turn(n, d):
    return [(i, (i + d) % n) for i in range(n)]


def swap(v, axis):
    return lax.ppermute(v, axis, turn(2, 1))


def sum_everywhere(v):
    c, x, yh = (lax.axis_index(a) for a in ("c", "x", "yh"))
    beside = [(i, i ^ 1) for i in range(4)]
    across = [(i, 3 - i) for i in range(4)]
    halvings = (
        ("c", turn(2, 1), c),
        ("x", beside, (x ^ (x >> 1)) & 1),
        ("x", across, x >> 1),
        ("yh", turn(2, 1), yh),
    )
    for axis, pairs, bit in halvings:
        half = v.shape[0] // 2
        mine = lax.dynamic_slice_in_dim(v, bit * half, half, 0)
        theirs = lax.dynamic_slice_in_dim(v, (1 - bit) * half, half, 0)
        v = mine + lax.ppermute(theirs.astype(BF16), axis, pairs).astype(F32)
    for axis, pairs in (("yl", turn(2, 1)), ("z", beside), ("z", across)):
        v = v + lax.ppermute(v, axis, pairs)
    v = v.astype(BF16)
    for axis, pairs, bit in reversed(halvings):
        got = lax.ppermute(v, axis, pairs)
        v = jnp.where(bit == 0, jnp.concatenate([v, got], 0), jnp.concatenate([got, v], 0))
    return v.astype(F32)


def shards(features, atrous_weight, point_weight, proj_weight, cotangent):
    place = jnp.stack([lax.axis_index(a) for a in ("z", "x", "c", "yl")]).astype(jnp.int32)

    atrous_t = jnp.transpose(atrous_weight, (0, 2, 1))
    parts = split_weights(place, jnp.transpose(point_weight, (1, 0)), atrous_t)
    from_x = [parts[0]] + [lax.ppermute(parts[d], "x", turn(4, d)) for d in (1, 2, 3)]
    quarter = stack_columns(place, from_x)
    quarters = [quarter] + [lax.ppermute(quarter, "z", turn(4, d)) for d in (1, 2, 3)]
    blocks = quarters + [swap(v, "c") for v in quarters]
    wt = join_weights(place, blocks).reshape(TAPS, 128, K)

    x_send = split_features(features.reshape(CELLS, 2048))
    x = lax.all_to_all(x_send, ("yh", "x"), 0, 0, tiled=True)

    partial = forward(x, wt)
    got = lax.all_to_all(partial, ("yh", "x"), 0, 0, tiled=True)
    proj = proj_weight.reshape(4, 2, 128, 256).transpose(1, 0, 2, 3).reshape(1024, 256)
    projected, d_send, proj_part = middle(got, proj, cotangent.reshape(CELLS, 256))
    grad_proj = sum_everywhere(proj_part)
    grad_proj = grad_proj.reshape(2, 4, 128, 256).transpose(1, 0, 2, 3).reshape(1024, 256) * 0.125
    dpre = lax.all_to_all(d_send, ("yh", "x"), 0, 0, tiled=True)

    xt = jnp.transpose(
        jnp.pad(x, ((0, 0), (0, PADDED - CELLS), (0, 0))).reshape(CHIPS * PADDED, K)
    )
    keep, send = kernel_grad(place, dpre, xt)
    g_part = (keep.astype(F32) + swap(send, "c").astype(F32)).astype(BF16)
    g_got = lax.all_to_all(g_part.reshape(16, 16, COLS), ("z", "yl", "yh"), 0, 0, tiled=True)
    g_sum = jnp.sum(g_got.reshape(8, 2, 16, COLS).astype(F32), 0).astype(BF16)
    g_all = [g_sum]
    for d in range(4):
        for l in range(2):
            if d or l:
                pairs = [
                    (z * 2 + y, (z + d) % 4 * 2 + (y + l) % 2) for z in range(4) for y in range(2)
                ]
                g_all.append(lax.ppermute(g_sum, ("z", "yl"), pairs))
    grad_point, grad_atrous = place_grads(place, g_all)

    back = feature_grad(dpre, wt)
    back, _ = lax.optimization_barrier((back, g_sum))
    input_grad = join_features(lax.all_to_all(back, ("yh", "x"), 0, 0, tiled=True))

    return (
        projected.reshape(1, 3, WIDTH, 256),
        input_grad.reshape(1, 3, WIDTH, 2048),
        grad_point,
        grad_atrous,
        grad_proj,
    )


def solution(mesh):
    fine = Mesh(mesh.devices.reshape(4, 2, 2, 4, 2), ("z", "yl", "yh", "x", "c"))
    rep, sp = ("z", "yl"), ("yh", "x", "c")
    in_specs = (
        P(rep, sp, None, None),
        P(None, None, sp),
        P(None, sp),
        P(),
        P(rep, sp, None, None),
    )
    out_specs = (
        P(rep, sp, None, None),
        P(rep, sp, None, None),
        P(sp, None),
        P(None, sp, None),
        P(),
    )
    return jax.shard_map(shards, mesh=fine, in_specs=in_specs, out_specs=out_specs, check_vma=False)
```

```python
import jax
import jax.numpy as jnp
from jax import lax
from jax.experimental import pallas as pl
from jax.experimental.pallas import tpu as pltpu
from jax.sharding import Mesh
from jax.sharding import PartitionSpec as P

DILATIONS = (6, 12, 18)
CHIPS = 8
CELLS = 216
PADDED = 224
WIDTH = 72
HALO = 3
RIDER = 32
K = 512
TAPS = 28
COLS = TAPS * 128
QUARTER = TAPS // 4
BF16 = jnp.bfloat16
F32 = jnp.float32
VMEM = pl.BlockSpec(memory_space=pltpu.VMEM)
SMEM = pl.BlockSpec(memory_space=pltpu.SMEM)


def tap_of(g, ky, kx):
    return 1 + 9 * g + 3 * (ky + 1) + (kx + 1)


def tap_pairs():
    def tap(g, ky, kx):
        return (tap_of(g, ky, kx), g, ky, kx)

    pairs = [((0, -1, 0, 0), tap(0, 0, 0)), (tap(1, 0, 0), tap(2, 0, 0))]
    for ky in (0, -1, 1):
        for g in range(3):
            pairs.append((tap(g, ky, -1), tap(g, ky, 1)))
    for ky in (-1, 1):
        pairs.append((tap(0, ky, 0), tap(1, ky, 0)))
    pairs.append((tap(2, -1, 0), tap(2, 1, 0)))
    return pairs


PAIRS = tap_pairs()


def params(mib):
    return pltpu.CompilerParams(vmem_limit_bytes=mib << 20)


def cost(flops, nbytes):
    return pl.CostEstimate(flops=flops, bytes_accessed=nbytes, transcendentals=0)


CONV_COST = cost(2 * 1728 * K * COLS, 8 << 20)


def cell_column(rows):
    row = lax.broadcasted_iota(jnp.int32, (rows, 128), 0)
    return jnp.where(row >= 144, row - 144, jnp.where(row >= 72, row - 72, row))


def split_features_kernel(x, out):
    for col in range(4):
        for yh in range(2):
            part = x[:, (yh * 4 + col) * 256 : (yh * 4 + col + 1) * 256]
            for dest in range(2):
                out[dest * 4 + col, :, yh * 256 : (yh + 1) * 256] = part


def split_features(x):
    return pl.pallas_call(
        split_features_kernel,
        out_shape=jax.ShapeDtypeStruct((CHIPS, CELLS, K), BF16),
        in_specs=[VMEM],
        out_specs=VMEM,
        compiler_params=params(16),
        cost_estimate=cost(0, 3 << 20),
    )(x)


def split_weights_kernel(place, point, atrous, out0, out1, out2, out3, taps, sem):
    z, x = place[0], place[1]
    begin = jnp.where(z == 0, 0, QUARTER * z - 1)
    copy = pltpu.make_async_copy(atrous.at[pl.ds(begin, QUARTER)], taps.at[pl.ds(1, QUARTER)], sem)
    copy.start()
    taps[0] = point[...]
    copy.wait()
    first = jnp.where(z == 0, 0, 1)
    for d, out in enumerate((out0, out1, out2, out3)):
        col = lax.rem(x + d, 4)
        for yh in range(2):
            lanes = pl.ds(pl.multiple_of((yh * 4 + col) * 256, 256), 256)
            for t in range(QUARTER):
                out[t, :, yh * 256 : (yh + 1) * 256] = taps[first + t, :, lanes]


def split_weights(place, point, atrous):
    return pl.pallas_call(
        split_weights_kernel,
        out_shape=(jax.ShapeDtypeStruct((QUARTER, 16, K), BF16),) * 4,
        in_specs=[SMEM, VMEM, pl.BlockSpec(memory_space=pl.ANY)],
        out_specs=(VMEM,) * 4,
        scratch_shapes=[pltpu.VMEM((QUARTER + 1, 16, 2048), BF16), pltpu.SemaphoreType.DMA],
        compiler_params=params(16),
        cost_estimate=cost(0, 1 << 20),
    )(place, point, atrous)


def join_weights_kernel(place, *refs):
    out = refs[8]
    z, me = place[0], place[2]
    for which in range(2):
        c = me if which == 0 else 1 - me
        for d in range(4):
            quarter = lax.rem(z + 4 - d, 4)
            block = refs[which * 4 + d]
            for x in range(4):
                for t in range(QUARTER):
                    out[quarter * QUARTER + t, x, c] = block[x, t]


def join_weights(place, blocks):
    return pl.pallas_call(
        join_weights_kernel,
        out_shape=jax.ShapeDtypeStruct((TAPS, 4, 2, 16, K), BF16),
        in_specs=[SMEM] + [VMEM] * 8,
        out_specs=VMEM,
        compiler_params=params(24),
        cost_estimate=cost(0, 8 << 20),
    )(place, *blocks)


def stack_columns_kernel(place, b0, b1, b2, b3, out):
    for d, block in enumerate((b0, b1, b2, b3)):
        out[lax.rem(place[1] + 4 - d, 4)] = block[...]


def stack_columns(place, blocks):
    return pl.pallas_call(
        stack_columns_kernel,
        out_shape=jax.ShapeDtypeStruct((4, QUARTER, 16, K), BF16),
        in_specs=[SMEM] + [VMEM] * 4,
        out_specs=VMEM,
        compiler_params=params(16),
        cost_estimate=cost(0, 1 << 20),
    )(place, *blocks)


def forward_kernel(x, wt, out, xs, acc):
    for j in range(CHIPS):
        xs[j, :CELLS] = x[j]
        xs[j, CELLS:] = jnp.zeros((PADDED - CELLS, K), BF16)

    def span(g, ky):
        return max(0, ky * (g + 1)), CHIPS + min(0, ky * (g + 1))

    for pair in PAIRS:
        begin = min(span(g, ky)[0] for _, g, ky, _ in pair)
        end = max(span(g, ky)[1] for _, g, ky, _ in pair)
        rows = xs[begin:end].reshape((end - begin) * PADDED, K)
        right = jnp.concatenate([wt[t] for t, _, _, _ in pair], 0)
        y = lax.dot_general(rows, right, (((1,), (1,)), ((), ())), preferred_element_type=F32)
        y = y.reshape(end - begin, PADDED, 256)
        for half, (_, g, ky, kx) in enumerate(pair):
            which = 3 if g < 0 else (g if kx == 0 else 4 + 2 * g + (kx + 1) // 2)
            lo, hi = span(g, ky)
            part = y[lo - begin : hi - begin, :, half * 128 : (half + 1) * 128]
            to = slice(lo - ky * (g + 1), hi - ky * (g + 1))
            if ky == 0:
                acc[which, to] = part
            else:
                acc[which, to] += part

    column = cell_column(PADDED)

    def finish(j, _):
        parts = [acc[3, j]]
        for g, d in enumerate(DILATIONS):
            minus = pltpu.roll(acc[4 + 2 * g, j], d, 0)
            plus = pltpu.roll(acc[5 + 2 * g, j], PADDED - d, 0)
            parts.append(
                acc[g, j]
                + jnp.where(column >= d, minus, 0.0)
                + jnp.where(column < WIDTH - d, plus, 0.0)
            )
        out[j] = jnp.concatenate(parts, 1).astype(BF16)[:CELLS]
        return 0

    lax.fori_loop(0, CHIPS, finish, 0)


def forward(x, wt):
    return pl.pallas_call(
        forward_kernel,
        out_shape=jax.ShapeDtypeStruct((CHIPS, CELLS, 512), BF16),
        in_specs=[VMEM] * 2,
        out_specs=VMEM,
        scratch_shapes=[
            pltpu.VMEM((CHIPS, PADDED, K), BF16),
            pltpu.VMEM((10, CHIPS, PADDED, 128), F32),
        ],
        compiler_params=params(56),
        cost_estimate=CONV_COST,
    )(x, wt)


def sigmoid(v):
    return 1.0 / (1.0 + jnp.exp(-v))


def middle_kernel(got, proj, cot, projected, send, grad):
    parts = []
    for yh in range(2):
        total = got[yh * 4].astype(F32)
        for x in range(1, 4):
            total = total + got[yh * 4 + x].astype(F32)
        parts.append(total)
    pre = jnp.concatenate(parts, 1).astype(BF16).astype(F32)
    sig = sigmoid(pre)
    acts = (pre * sig).astype(BF16)
    slope = sig + pre * sig * (1.0 - sig)
    weight = proj[...]
    out_pre = jnp.dot(acts, weight, preferred_element_type=F32)
    osig = sigmoid(out_pre)
    projected[...] = (out_pre * osig).astype(BF16)
    dout = (cot[...].astype(F32) * (osig + out_pre * osig * (1.0 - osig))).astype(BF16)
    dacts = lax.dot_general(
        dout, weight, (((1,), (1,)), ((), ())), preferred_element_type=F32
    )
    dpre = (dacts * slope).astype(BF16)
    for yh in range(2):
        for x in range(4):
            send[yh * 4 + x] = dpre[:, yh * 512 : (yh + 1) * 512]
    grad[...] = lax.dot_general(
        acts, dout, (((0,), (0,)), ((), ())), preferred_element_type=F32
    )


def middle(got, proj, cot):
    return pl.pallas_call(
        middle_kernel,
        out_shape=(
            jax.ShapeDtypeStruct((CELLS, 256), BF16),
            jax.ShapeDtypeStruct((CHIPS, CELLS, 512), BF16),
            jax.ShapeDtypeStruct((1024, 256), F32),
        ),
        in_specs=[VMEM] * 3,
        out_specs=(VMEM,) * 3,
        compiler_params=params(48),
    )(got, proj, cot)


SPREAD = [pltpu.VMEM((9, CHIPS + 2 * HALO, PADDED, 128), BF16), pltpu.VMEM((CHIPS, PADDED, 128), BF16)]


def spread(got, moved, point):
    column = cell_column(CELLS)
    for n in range(9):
        moved[n, :HALO] = jnp.zeros((HALO, PADDED, 128), BF16)
        moved[n, HALO + CHIPS :] = jnp.zeros((HALO, PADDED, 128), BF16)
    tail = jnp.zeros((PADDED - CELLS, 128), BF16)

    def step(j, _):
        point[j, :CELLS] = got[j, :, :128]
        point[j, CELLS:] = tail
        for g, d in enumerate(DILATIONS):
            v = got[j, :, (g + 1) * 128 : (g + 2) * 128]
            wide = v.astype(F32)
            minus = jnp.where(column < WIDTH - d, pltpu.roll(wide, CELLS - d, 0), 0.0)
            plus = jnp.where(column >= d, pltpu.roll(wide, d, 0), 0.0)
            for kx, part in enumerate((minus.astype(BF16), v, plus.astype(BF16))):
                moved[3 * g + kx, HALO + j, :CELLS] = part
                moved[3 * g + kx, HALO + j, CELLS:] = tail
        return 0

    lax.fori_loop(0, CHIPS, step, 0)


def spread_columns(moved, point, tap, first, count):
    _, g, ky, kx = tap
    if g < 0:
        v = point[pl.ds(first, count)]
    else:
        v = moved[3 * g + kx + 1, pl.ds(HALO + first - ky * (g + 1), count)]
    return v.reshape(count * PADDED, 128)


def turn_features_kernel(place, x, out, xs):
    for j in range(CHIPS):
        xs[j, :CELLS] = x[j]
        xs[j, CELLS:] = jnp.zeros((PADDED - CELLS, K), BF16)
    flat = xs[...].reshape(CHIPS * PADDED, K)
    for yh in range(2):
        for core in range(2):
            lanes = slice((yh * 2 + core) * 128, (yh * 2 + core + 1) * 128)
            away = jnp.where(place[2] == core, 0, 1)
            for n in range(7):
                block = flat[n * 256 : (n + 1) * 256, lanes]
                out[2 * away + yh, :, n * 256 : (n + 1) * 256] = block.T


def turn_features(place, x):
    return pl.pallas_call(
        turn_features_kernel,
        out_shape=jax.ShapeDtypeStruct((4, 128, CHIPS * PADDED), BF16),
        in_specs=[SMEM, VMEM],
        out_specs=VMEM,
        scratch_shapes=[pltpu.VMEM((CHIPS, PADDED, K), BF16)],
        compiler_params=params(32),
        cost_estimate=cost(0, 8 << 20),
    )(place, x)


def kernel_grad_kernel(got, xt, keep, send, moved, point):
    spread(got, moved, point)
    left = xt[...].reshape(K, CHIPS * PADDED)
    for pair in PAIRS:
        right = jnp.concatenate([spread_columns(moved, point, tap, 0, CHIPS) for tap in pair], 1)
        part = jnp.dot(left, right, preferred_element_type=F32).astype(BF16)
        for half, tap in enumerate(pair):
            cols = slice(tap[0] * 128, (tap[0] + 1) * 128)
            block = part[:, half * 128 : (half + 1) * 128].reshape(2, 2, 8, 16, 128)
            for yh in range(2):
                keep[:, yh, :, cols] = block[0, yh]
                send[:, yh, :, cols] = block[1, yh]


def kernel_grad(got, xt):
    return pl.pallas_call(
        kernel_grad_kernel,
        out_shape=(jax.ShapeDtypeStruct((8, 2, 16, COLS), BF16),) * 2,
        in_specs=[VMEM, VMEM],
        out_specs=(VMEM,) * 2,
        scratch_shapes=SPREAD,
        compiler_params=params(56),
        cost_estimate=CONV_COST,
    )(got, xt)


def sum_samples_kernel(got, first, second):
    for yh, out in enumerate((first, second)):
        total = got[yh].astype(F32)
        for rep in range(1, 8):
            total = total + got[2 * rep + yh].astype(F32)
        out[...] = total.astype(BF16)


def sum_samples(got):
    return pl.pallas_call(
        sum_samples_kernel,
        out_shape=(jax.ShapeDtypeStruct((16, COLS), BF16),) * 2,
        in_specs=[VMEM],
        out_specs=(VMEM,) * 2,
        compiler_params=params(24),
    )(got)


def feature_grad_kernel(got, wt, proj, out, moved, point):
    spread(got, moved, point)
    rider = jnp.concatenate([proj[:RIDER], proj[RIDER:]], 1).astype(BF16)

    def step(i, _):
        cols, rows = [], []
        for pair in PAIRS:
            for tap in pair:
                cols.append(spread_columns(moved, point, tap, 2 * i, 2))
                rows.append(wt[tap[0]])
        part = jnp.dot(
            jnp.concatenate(cols, 1), jnp.concatenate(rows, 0), preferred_element_type=F32
        )
        part = part.astype(BF16)
        for sub in range(2):
            out[2 * i + sub, :PADDED] = part[sub * PADDED : (sub + 1) * PADDED]
            out[2 * i + sub, PADDED:] = rider
        return 0

    lax.fori_loop(0, CHIPS // 2, step, 0)


def feature_grad(got, wt, proj):
    return pl.pallas_call(
        feature_grad_kernel,
        out_shape=jax.ShapeDtypeStruct((CHIPS, PADDED + RIDER, K), BF16),
        in_specs=[VMEM] * 3,
        out_specs=VMEM,
        scratch_shapes=SPREAD,
        compiler_params=params(56),
        cost_estimate=CONV_COST,
    )(got, wt, proj)


def place_grads_kernel(place, *refs):
    point, atrous = refs[6], refs[7]
    z, yl = place[0], place[3]
    for d in range(4):
        for l in range(2):
            rep = 2 * lax.rem(z + 4 - d, 4) + lax.rem(yl + l, 2)
            rows = pl.ds(pl.multiple_of(rep * 16, 16), 16)
            for yh, block in enumerate((refs[d][l], refs[4 + l][d])):
                cols = slice(yh * 128, (yh + 1) * 128)
                for t in range(TAPS):
                    part = block[:, t * 128 : (t + 1) * 128].astype(F32) * 0.125
                    if t == 0:
                        point[rows, cols] = part
                    else:
                        atrous[t - 1, rows, cols] = part


def place_grads(place, blocks):
    return pl.pallas_call(
        place_grads_kernel,
        out_shape=(
            jax.ShapeDtypeStruct((128, 256), F32),
            jax.ShapeDtypeStruct((27, 128, 256), F32),
        ),
        in_specs=[SMEM] + [VMEM] * 6,
        out_specs=(VMEM,) * 2,
        compiler_params=params(40),
    )(place, *blocks)


def gray(x):
    return (x ^ (x >> 1)) & 1


def join_features_kernel(got, out, proj):
    for x in range(4):
        total = (got[x, :CELLS].astype(F32) + got[4 + x, :CELLS].astype(F32)).astype(BF16)
        for yh in range(2):
            out[:, (yh * 4 + x) * 256 : (yh * 4 + x + 1) * 256] = total[:, yh * 256 : (yh + 1) * 256]
            rider = got[yh * 4 + x, PADDED:]
            row = gray(x) * 256 + (x >> 1) * 128 + yh * 64
            proj[row : row + RIDER] = rider[:, :256]
            proj[row + RIDER : row + 2 * RIDER] = rider[:, 256:]


def join_features(got):
    return pl.pallas_call(
        join_features_kernel,
        out_shape=(
            jax.ShapeDtypeStruct((CELLS, 2048), BF16),
            jax.ShapeDtypeStruct((512, 256), BF16),
        ),
        in_specs=[VMEM],
        out_specs=(VMEM,) * 2,
        compiler_params=params(16),
    )(got)


def turn(n, d):
    return [(i, (i + d) % n) for i in range(n)]


def swap(v, axis):
    return lax.ppermute(v, axis, turn(2, 1))


BESIDE = [(i, i ^ 1) for i in range(4)]
ACROSS = [(i, 3 - i) for i in range(4)]


def halved(v, axis, pairs, bit):
    half = v.shape[0] // 2
    mine = lax.dynamic_slice_in_dim(v, bit * half, half, 0)
    theirs = lax.dynamic_slice_in_dim(v, (1 - bit) * half, half, 0)
    return mine + lax.ppermute(theirs.astype(BF16), axis, pairs).astype(F32)


def shards(features, atrous_weight, point_weight, proj_weight, cotangent):
    place = jnp.stack([lax.axis_index(a) for a in ("z", "x", "c", "yl")]).astype(jnp.int32)

    atrous_t = jnp.transpose(atrous_weight, (0, 2, 1))
    parts = split_weights(place, jnp.transpose(point_weight, (1, 0)), atrous_t)
    from_x = [parts[0]] + [lax.ppermute(parts[d], "x", turn(4, d)) for d in (1, 2, 3)]
    quarter = stack_columns(place, from_x)
    quarters = [quarter] + [lax.ppermute(quarter, "z", turn(4, d)) for d in (1, 2, 3)]
    blocks = quarters + [swap(v, "c") for v in quarters]
    wt = join_weights(place, blocks).reshape(TAPS, 128, K)

    x_send = split_features(features.reshape(CELLS, 2048))
    x_send, quarter = lax.optimization_barrier((x_send, quarter))
    x = lax.all_to_all(x_send, ("yh", "x"), 0, 0, tiled=True)

    partial = forward(x, wt)
    got = lax.all_to_all(partial, ("yh", "x"), 0, 0, tiled=True)
    proj = proj_weight.reshape(4, 2, 128, 256).transpose(1, 0, 2, 3).reshape(1024, 256)
    projected, d_send, proj_part = middle(got, proj, cotangent.reshape(CELLS, 256))
    dpre = lax.all_to_all(d_send, ("yh", "x"), 0, 0, tiled=True)
    xt = turn_features(place, x)

    core, column, side = (lax.axis_index(a) for a in ("c", "x", "yh"))
    share = halved(proj_part, "c", turn(2, 1), core)
    share = halved(share, "x", BESIDE, gray(column))
    share = halved(share, "x", ACROSS, column >> 1)
    dpre, share = lax.optimization_barrier((dpre, share))

    keep, send = kernel_grad(dpre, xt)
    g_part = (keep.astype(F32) + swap(send, "c").astype(F32)).astype(BF16)
    g_got = lax.all_to_all(g_part.reshape(16, 16, COLS), ("z", "yl", "yh"), 0, 0, tiled=True)

    share = halved(share, "yh", turn(2, 1), side)
    share = share + swap(share, "yl")
    share = share + lax.ppermute(share, "z", BESIDE)
    share = share + lax.ppermute(share, "z", ACROSS)
    back = feature_grad(dpre, wt, share)

    first, second = sum_samples(g_got)
    back, first, second = lax.optimization_barrier((back, first, second))
    pair = jnp.stack([first, swap(first, "yl")])
    four = jnp.stack([second] + [lax.ppermute(second, "z", turn(4, d)) for d in (1, 2, 3)])
    pairs = [pair] + [lax.ppermute(pair, "z", turn(4, d)) for d in (1, 2, 3)]
    grad_point, grad_atrous = place_grads(place, pairs + [four, swap(four, "yl")])

    b_got = lax.all_to_all(back, ("yh", "x"), 0, 0, tiled=True)
    input_grad, half = join_features(b_got)
    other = swap(half, "c")
    grad_proj = jnp.where(core == 0, jnp.stack([half, other]), jnp.stack([other, half]))
    grad_proj = grad_proj.astype(F32).reshape(2, 4, 128, 256).transpose(1, 0, 2, 3)
    grad_proj = grad_proj.reshape(1024, 256) * 0.125

    return (
        projected.reshape(1, 3, WIDTH, 256),
        input_grad.reshape(1, 3, WIDTH, 2048),
        grad_point,
        grad_atrous,
        grad_proj,
    )


def solution(mesh):
    fine = Mesh(mesh.devices.reshape(4, 2, 2, 4, 2), ("z", "yl", "yh", "x", "c"))
    rep, sp = ("z", "yl"), ("yh", "x", "c")
    in_specs = (
        P(rep, sp, None, None),
        P(None, None, sp),
        P(None, sp),
        P(),
        P(rep, sp, None, None),
    )
    out_specs = (
        P(rep, sp, None, None),
        P(rep, sp, None, None),
        P(sp, None),
        P(None, sp, None),
        P(),
    )
    return jax.shard_map(shards, mesh=fine, in_specs=in_specs, out_specs=out_specs, check_vma=False)
```

```python
import jax
import jax.numpy as jnp
from jax import lax
from jax.experimental import pallas as pl
from jax.experimental.pallas import tpu as pltpu
from jax.sharding import Mesh
from jax.sharding import PartitionSpec as P

DILATIONS = (6, 12, 18)
CHIPS = 8
CELLS = 216
PADDED = 224
WIDTH = 72
HALO = 3
K = 512
TAPS = 28
COLS = TAPS * 128
QUARTER = TAPS // 4
BF16 = jnp.bfloat16
F32 = jnp.float32
VMEM = pl.BlockSpec(memory_space=pltpu.VMEM)
SMEM = pl.BlockSpec(memory_space=pltpu.SMEM)


def tap_of(g, ky, kx):
    return 1 + 9 * g + 3 * (ky + 1) + (kx + 1)


def tap_pairs():
    def tap(g, ky, kx):
        return (tap_of(g, ky, kx), g, ky, kx)

    pairs = [((0, -1, 0, 0), tap(0, 0, 0)), (tap(1, 0, 0), tap(2, 0, 0))]
    for ky in (0, -1, 1):
        for g in range(3):
            pairs.append((tap(g, ky, -1), tap(g, ky, 1)))
    for ky in (-1, 1):
        pairs.append((tap(0, ky, 0), tap(1, ky, 0)))
    pairs.append((tap(2, -1, 0), tap(2, 1, 0)))
    return pairs


PAIRS = tap_pairs()


def params(mib):
    return pltpu.CompilerParams(vmem_limit_bytes=mib << 20)


def cost(flops, nbytes):
    return pl.CostEstimate(flops=flops, bytes_accessed=nbytes, transcendentals=0)


CONV_COST = cost(2 * 1728 * K * COLS, 8 << 20)


def cell_column(rows):
    row = lax.broadcasted_iota(jnp.int32, (rows, 128), 0)
    return jnp.where(row >= 144, row - 144, jnp.where(row >= 72, row - 72, row))


def split_features_kernel(x, out):
    for col in range(4):
        for yh in range(2):
            part = x[:, (yh * 4 + col) * 256 : (yh * 4 + col + 1) * 256]
            for dest in range(2):
                out[dest * 4 + col, :, yh * 256 : (yh + 1) * 256] = part


def split_features(x):
    return pl.pallas_call(
        split_features_kernel,
        out_shape=jax.ShapeDtypeStruct((CHIPS, CELLS, K), BF16),
        in_specs=[VMEM],
        out_specs=VMEM,
        compiler_params=params(16),
        cost_estimate=cost(0, 3 << 20),
    )(x)


def split_weights_kernel(place, point, atrous, out0, out1, out2, out3, taps, sem):
    z, x = place[0], place[1]
    begin = jnp.where(z == 0, 0, QUARTER * z - 1)
    copy = pltpu.make_async_copy(atrous.at[pl.ds(begin, QUARTER)], taps.at[pl.ds(1, QUARTER)], sem)
    copy.start()
    taps[0] = point[...]
    copy.wait()
    first = jnp.where(z == 0, 0, 1)
    for d, out in enumerate((out0, out1, out2, out3)):
        col = lax.rem(x + d, 4)
        for yh in range(2):
            lanes = pl.ds(pl.multiple_of((yh * 4 + col) * 256, 256), 256)
            for t in range(QUARTER):
                out[t, :, yh * 256 : (yh + 1) * 256] = taps[first + t, :, lanes]


def split_weights(place, point, atrous):
    return pl.pallas_call(
        split_weights_kernel,
        out_shape=(jax.ShapeDtypeStruct((QUARTER, 16, K), BF16),) * 4,
        in_specs=[SMEM, VMEM, pl.BlockSpec(memory_space=pl.ANY)],
        out_specs=(VMEM,) * 4,
        scratch_shapes=[pltpu.VMEM((QUARTER + 1, 16, 2048), BF16), pltpu.SemaphoreType.DMA],
        compiler_params=params(16),
        cost_estimate=cost(0, 1 << 20),
    )(place, point, atrous)


def join_weights_kernel(place, *refs):
    out = refs[8]
    z, me = place[0], place[2]
    for which in range(2):
        c = me if which == 0 else 1 - me
        for d in range(4):
            quarter = lax.rem(z + 4 - d, 4)
            block = refs[which * 4 + d]
            for x in range(4):
                for t in range(QUARTER):
                    out[quarter * QUARTER + t, x, c] = block[x, t]


def join_weights(place, blocks):
    return pl.pallas_call(
        join_weights_kernel,
        out_shape=jax.ShapeDtypeStruct((TAPS, 4, 2, 16, K), BF16),
        in_specs=[SMEM] + [VMEM] * 8,
        out_specs=VMEM,
        compiler_params=params(24),
        cost_estimate=cost(0, 8 << 20),
    )(place, *blocks)


def stack_columns_kernel(place, b0, b1, b2, b3, out):
    for d, block in enumerate((b0, b1, b2, b3)):
        out[lax.rem(place[1] + 4 - d, 4)] = block[...]


def stack_columns(place, blocks):
    return pl.pallas_call(
        stack_columns_kernel,
        out_shape=jax.ShapeDtypeStruct((4, QUARTER, 16, K), BF16),
        in_specs=[SMEM] + [VMEM] * 4,
        out_specs=VMEM,
        compiler_params=params(16),
        cost_estimate=cost(0, 1 << 20),
    )(place, *blocks)


def forward_kernel(x, wt, out, xs, acc):
    for j in range(CHIPS):
        xs[j, :CELLS] = x[j]
        xs[j, CELLS:] = jnp.zeros((PADDED - CELLS, K), BF16)

    def span(g, ky):
        return max(0, ky * (g + 1)), CHIPS + min(0, ky * (g + 1))

    for pair in PAIRS:
        begin = min(span(g, ky)[0] for _, g, ky, _ in pair)
        end = max(span(g, ky)[1] for _, g, ky, _ in pair)
        rows = xs[begin:end].reshape((end - begin) * PADDED, K)
        right = jnp.concatenate([wt[t] for t, _, _, _ in pair], 0)
        y = lax.dot_general(rows, right, (((1,), (1,)), ((), ())), preferred_element_type=F32)
        y = y.reshape(end - begin, PADDED, 256)
        for half, (_, g, ky, kx) in enumerate(pair):
            which = 3 if g < 0 else (g if kx == 0 else 4 + 2 * g + (kx + 1) // 2)
            lo, hi = span(g, ky)
            part = y[lo - begin : hi - begin, :, half * 128 : (half + 1) * 128]
            to = slice(lo - ky * (g + 1), hi - ky * (g + 1))
            if ky == 0:
                acc[which, to] = part
            else:
                acc[which, to] += part

    column = cell_column(PADDED)

    def finish(j, _):
        parts = [acc[3, j]]
        for g, d in enumerate(DILATIONS):
            minus = pltpu.roll(acc[4 + 2 * g, j], d, 0)
            plus = pltpu.roll(acc[5 + 2 * g, j], PADDED - d, 0)
            parts.append(
                acc[g, j]
                + jnp.where(column >= d, minus, 0.0)
                + jnp.where(column < WIDTH - d, plus, 0.0)
            )
        out[j] = jnp.concatenate(parts, 1).astype(BF16)[:CELLS]
        return 0

    lax.fori_loop(0, CHIPS, finish, 0)


def forward(x, wt):
    return pl.pallas_call(
        forward_kernel,
        out_shape=jax.ShapeDtypeStruct((CHIPS, CELLS, 512), BF16),
        in_specs=[VMEM] * 2,
        out_specs=VMEM,
        scratch_shapes=[
            pltpu.VMEM((CHIPS, PADDED, K), BF16),
            pltpu.VMEM((10, CHIPS, PADDED, 128), F32),
        ],
        compiler_params=params(56),
        cost_estimate=CONV_COST,
    )(x, wt)


def sigmoid(v):
    return 1.0 / (1.0 + jnp.exp(-v))


def middle_kernel(got, proj, cot, projected, send, grad):
    parts = []
    for yh in range(2):
        total = got[yh * 4].astype(F32)
        for x in range(1, 4):
            total = total + got[yh * 4 + x].astype(F32)
        parts.append(total)
    pre = jnp.concatenate(parts, 1).astype(BF16).astype(F32)
    sig = sigmoid(pre)
    acts = (pre * sig).astype(BF16)
    slope = sig + pre * sig * (1.0 - sig)
    weight = proj[...]
    out_pre = jnp.dot(acts, weight, preferred_element_type=F32)
    osig = sigmoid(out_pre)
    projected[...] = (out_pre * osig).astype(BF16)
    dout = (cot[...].astype(F32) * (osig + out_pre * osig * (1.0 - osig))).astype(BF16)
    dacts = lax.dot_general(
        dout, weight, (((1,), (1,)), ((), ())), preferred_element_type=F32
    )
    dpre = (dacts * slope).astype(BF16)
    for yh in range(2):
        for x in range(4):
            send[yh * 4 + x] = dpre[:, yh * 512 : (yh + 1) * 512]
    grad[...] = lax.dot_general(
        acts, dout, (((0,), (0,)), ((), ())), preferred_element_type=F32
    )


def middle(got, proj, cot):
    return pl.pallas_call(
        middle_kernel,
        out_shape=(
            jax.ShapeDtypeStruct((CELLS, 256), BF16),
            jax.ShapeDtypeStruct((CHIPS, CELLS, 512), BF16),
            jax.ShapeDtypeStruct((1024, 256), F32),
        ),
        in_specs=[VMEM] * 3,
        out_specs=(VMEM,) * 3,
        compiler_params=params(48),
    )(got, proj, cot)


SPREAD = [pltpu.VMEM((9, CHIPS + 2 * HALO, PADDED, 128), BF16), pltpu.VMEM((CHIPS, PADDED, 128), BF16)]


def spread(got, moved, point):
    column = cell_column(CELLS)
    for n in range(9):
        moved[n, :HALO] = jnp.zeros((HALO, PADDED, 128), BF16)
        moved[n, HALO + CHIPS :] = jnp.zeros((HALO, PADDED, 128), BF16)
    tail = jnp.zeros((PADDED - CELLS, 128), BF16)

    def step(j, _):
        point[j, :CELLS] = got[j, :, :128]
        point[j, CELLS:] = tail
        for g, d in enumerate(DILATIONS):
            v = got[j, :, (g + 1) * 128 : (g + 2) * 128]
            wide = v.astype(F32)
            minus = jnp.where(column < WIDTH - d, pltpu.roll(wide, CELLS - d, 0), 0.0)
            plus = jnp.where(column >= d, pltpu.roll(wide, d, 0), 0.0)
            for kx, part in enumerate((minus.astype(BF16), v, plus.astype(BF16))):
                moved[3 * g + kx, HALO + j, :CELLS] = part
                moved[3 * g + kx, HALO + j, CELLS:] = tail
        return 0

    lax.fori_loop(0, CHIPS, step, 0)


def spread_columns(moved, point, tap, first, count):
    _, g, ky, kx = tap
    if g < 0:
        v = point[pl.ds(first, count)]
    else:
        v = moved[3 * g + kx + 1, pl.ds(HALO + first - ky * (g + 1), count)]
    return v.reshape(count * PADDED, 128)


def turn_features_kernel(place, x, out, xs):
    for j in range(CHIPS):
        xs[j, :CELLS] = x[j]
        xs[j, CELLS:] = jnp.zeros((PADDED - CELLS, K), BF16)
    flat = xs[...].reshape(CHIPS * PADDED, K)
    for yh in range(2):
        for core in range(2):
            lanes = slice((yh * 2 + core) * 128, (yh * 2 + core + 1) * 128)
            away = jnp.where(place[2] == core, 0, 1)
            for n in range(7):
                block = flat[n * 256 : (n + 1) * 256, lanes]
                out[2 * away + yh, :, n * 256 : (n + 1) * 256] = block.T


def turn_features(place, x):
    return pl.pallas_call(
        turn_features_kernel,
        out_shape=jax.ShapeDtypeStruct((4, 128, CHIPS * PADDED), BF16),
        in_specs=[SMEM, VMEM],
        out_specs=VMEM,
        scratch_shapes=[pltpu.VMEM((CHIPS, PADDED, K), BF16)],
        compiler_params=params(32),
        cost_estimate=cost(0, 8 << 20),
    )(place, x)


def kernel_grad_kernel(got, xt, keep, send, moved, point):
    spread(got, moved, point)
    left = xt[...].reshape(K, CHIPS * PADDED)
    for pair in PAIRS:
        right = jnp.concatenate([spread_columns(moved, point, tap, 0, CHIPS) for tap in pair], 1)
        part = jnp.dot(left, right, preferred_element_type=F32).astype(BF16)
        for half, tap in enumerate(pair):
            cols = slice(tap[0] * 128, (tap[0] + 1) * 128)
            block = part[:, half * 128 : (half + 1) * 128].reshape(2, 2, 8, 16, 128)
            for yh in range(2):
                keep[:, yh, :, cols] = block[0, yh]
                send[:, yh, :, cols] = block[1, yh]


def kernel_grad(got, xt):
    return pl.pallas_call(
        kernel_grad_kernel,
        out_shape=(jax.ShapeDtypeStruct((8, 2, 16, COLS), BF16),) * 2,
        in_specs=[VMEM, VMEM],
        out_specs=(VMEM,) * 2,
        scratch_shapes=SPREAD,
        compiler_params=params(56),
        cost_estimate=CONV_COST,
    )(got, xt)


def sum_samples_kernel(got, out):
    for yh in range(2):
        total = got[yh].astype(F32)
        for rep in range(1, 8):
            total = total + got[2 * rep + yh].astype(F32)
        out[yh] = total.astype(BF16)


def sum_samples(got):
    return pl.pallas_call(
        sum_samples_kernel,
        out_shape=jax.ShapeDtypeStruct((2, 16, COLS), BF16),
        in_specs=[VMEM],
        out_specs=VMEM,
        compiler_params=params(24),
    )(got)


def feature_grad_kernel(got, wt, out, moved, point):
    spread(got, moved, point)
    taps = [tap for pair in PAIRS for tap in pair]

    def step(i, _):
        left = jnp.concatenate([spread_columns(moved, point, tap, 2 * i, 2) for tap in taps], 1)
        right = jnp.concatenate([wt[tap[0]] for tap in taps], 0)
        part = jnp.dot(left, right, preferred_element_type=F32).astype(BF16)
        for sub in range(2):
            out[2 * i + sub] = part[sub * PADDED : sub * PADDED + CELLS]
        return 0

    lax.fori_loop(0, CHIPS // 2, step, 0)


def feature_grad(got, wt):
    return pl.pallas_call(
        feature_grad_kernel,
        out_shape=jax.ShapeDtypeStruct((CHIPS, CELLS, K), BF16),
        in_specs=[VMEM] * 2,
        out_specs=VMEM,
        scratch_shapes=SPREAD,
        compiler_params=params(56),
        cost_estimate=CONV_COST,
    )(got, wt)


def pack_sums_kernel(mine, other, proj, out):
    for n, block in enumerate((mine, other)):
        for yh in range(2):
            out[n, yh, :, :COLS] = block[yh]
            for half in range(2):
                row = half * 64 + n * 32 + yh * 16
                lane = COLS + half * 256
                out[n, yh, :, lane : lane + 256] = proj[row : row + 16, :].astype(BF16)


def pack_sums(mine, other, proj):
    return pl.pallas_call(
        pack_sums_kernel,
        out_shape=jax.ShapeDtypeStruct((2, 2, 16, COLS + 512), BF16),
        in_specs=[VMEM] * 3,
        out_specs=VMEM,
        compiler_params=params(16),
    )(mine, other, proj)


def place_grads_kernel(place, *refs):
    point, atrous = refs[4], refs[5]
    z, yl = place[0], place[3]
    for d in range(4):
        for l in range(2):
            rep = 2 * lax.rem(z + 4 - d, 4) + lax.rem(yl + l, 2)
            rows = pl.ds(pl.multiple_of(rep * 16, 16), 16)
            for yh in range(2):
                cols = slice(yh * 128, (yh + 1) * 128)
                for t in range(TAPS):
                    part = refs[d][l, yh, :, t * 128 : (t + 1) * 128].astype(F32) * 0.125
                    if t == 0:
                        point[rows, cols] = part
                    else:
                        atrous[t - 1, rows, cols] = part


def place_grads(place, blocks):
    return pl.pallas_call(
        place_grads_kernel,
        out_shape=(
            jax.ShapeDtypeStruct((128, 256), F32),
            jax.ShapeDtypeStruct((27, 128, 256), F32),
        ),
        in_specs=[SMEM] + [VMEM] * 4,
        out_specs=(VMEM,) * 2,
        compiler_params=params(40),
    )(place, *blocks)


def proj_half_kernel(place, b0, b1, b2, b3, out):
    for d, block in enumerate((b0, b1, b2, b3)):
        z = lax.rem(place[0] + 4 - d, 4)
        row = gray(z) * 256 + (z >> 1) * 128
        for n in range(2):
            for yh in range(2):
                for half in range(2):
                    at = pl.multiple_of(row + half * 64 + n * 32 + yh * 16, 16)
                    lane = COLS + half * 256
                    out[pl.ds(at, 16), :] = block[n, yh, :, lane : lane + 256]


def proj_half(place, blocks):
    return pl.pallas_call(
        proj_half_kernel,
        out_shape=jax.ShapeDtypeStruct((512, 256), BF16),
        in_specs=[SMEM] + [VMEM] * 4,
        out_specs=VMEM,
        compiler_params=params(24),
    )(place, *blocks)


def join_proj_kernel(place, mine, other, out):
    c = place[2]
    for half, block in enumerate((mine, other)):
        yh = c if half == 0 else 1 - c
        for branch in range(4):
            part = block[branch * 128 : (branch + 1) * 128, :].astype(F32) * 0.125
            rows = pl.multiple_of(branch * 256 + yh * 128, 128)
            out[pl.ds(rows, 128), :] = part


def join_proj(place, mine, other):
    return pl.pallas_call(
        join_proj_kernel,
        out_shape=jax.ShapeDtypeStruct((1024, 256), F32),
        in_specs=[SMEM, VMEM, VMEM],
        out_specs=VMEM,
        compiler_params=params(16),
    )(place, mine, other)


def join_features_kernel(got, out):
    for x in range(4):
        total = (got[x].astype(F32) + got[4 + x].astype(F32)).astype(BF16)
        for yh in range(2):
            out[:, (yh * 4 + x) * 256 : (yh * 4 + x + 1) * 256] = total[:, yh * 256 : (yh + 1) * 256]


def join_features(got):
    return pl.pallas_call(
        join_features_kernel,
        out_shape=jax.ShapeDtypeStruct((CELLS, 2048), BF16),
        in_specs=[VMEM],
        out_specs=VMEM,
        compiler_params=params(16),
    )(got)


def turn(n, d):
    return [(i, (i + d) % n) for i in range(n)]


def swap(v, axis):
    return lax.ppermute(v, axis, turn(2, 1))


BESIDE = [(i, i ^ 1) for i in range(4)]
ACROSS = [(i, 3 - i) for i in range(4)]


def gray(i):
    return (i ^ (i >> 1)) & 1


def halved(v, axis, pairs, bit):
    half = v.shape[0] // 2
    mine = lax.dynamic_slice_in_dim(v, bit * half, half, 0)
    theirs = lax.dynamic_slice_in_dim(v, (1 - bit) * half, half, 0)
    return mine + lax.ppermute(theirs.astype(BF16), axis, pairs).astype(F32)


def added(v, axis, pairs):
    return v + lax.ppermute(v.astype(BF16), axis, pairs).astype(F32)


def added_over_y(v):
    total, sent = v, v.astype(BF16)
    for l, h in ((0, 1), (1, 0), (1, 1)):
        pairs = [(2 * i + j, 2 * ((i + l) % 2) + (j + h) % 2) for i in range(2) for j in range(2)]
        total = total + lax.ppermute(sent, ("yl", "yh"), pairs).astype(F32)
    return total


def shards(features, atrous_weight, point_weight, proj_weight, cotangent):
    place = jnp.stack([lax.axis_index(a) for a in ("z", "x", "c", "yl", "yh")]).astype(jnp.int32)

    atrous_t = jnp.transpose(atrous_weight, (0, 2, 1))
    parts = split_weights(place, jnp.transpose(point_weight, (1, 0)), atrous_t)
    from_x = [parts[0]] + [lax.ppermute(parts[d], "x", turn(4, d)) for d in (1, 2, 3)]
    quarter = stack_columns(place, from_x)
    quarters = [quarter] + [lax.ppermute(quarter, "z", turn(4, d)) for d in (1, 2, 3)]
    blocks = quarters + [swap(v, "c") for v in quarters]
    wt = join_weights(place, blocks).reshape(TAPS, 128, K)

    x_send = split_features(features.reshape(CELLS, 2048))
    x_send, quarter = lax.optimization_barrier((x_send, quarter))
    x = lax.all_to_all(x_send, ("yh", "x"), 0, 0, tiled=True)

    partial = forward(x, wt)
    got = lax.all_to_all(partial, ("yh", "x"), 0, 0, tiled=True)
    proj = proj_weight.reshape(4, 2, 128, 256).transpose(1, 0, 2, 3).reshape(1024, 256)
    projected, d_send, proj_part = middle(got, proj, cotangent.reshape(CELLS, 256))
    dpre = lax.all_to_all(d_send, ("yh", "x"), 0, 0, tiled=True)
    xt = turn_features(place, x)

    core, layer = lax.axis_index("c"), lax.axis_index("z")
    share = halved(proj_part, "c", turn(2, 1), core)
    share = halved(share, "z", BESIDE, gray(layer))
    share = halved(share, "z", ACROSS, layer >> 1)
    share = added_over_y(share)
    dpre, share = lax.optimization_barrier((dpre, share))

    keep, send = kernel_grad(dpre, xt)
    g_part = (keep.astype(F32) + swap(send, "c").astype(F32)).astype(BF16)
    g_got = lax.all_to_all(g_part.reshape(16, 16, COLS), ("z", "yl", "yh"), 0, 0, tiled=True)

    dpre, _ = lax.optimization_barrier((dpre, g_part))
    back = feature_grad(dpre, wt)
    share, _ = lax.optimization_barrier((share, back))
    share = added(share, "x", BESIDE)
    share = added(share, "x", ACROSS)

    g_got, back, share = lax.optimization_barrier((g_got, back, share))
    g_sum = sum_samples(g_got)
    swapped = swap(g_sum, "yl")
    back, swapped = lax.optimization_barrier((back, swapped))
    pair = pack_sums(g_sum, swapped, share)
    pairs = [pair] + [lax.ppermute(pair, "z", turn(4, d)) for d in (1, 2, 3)]
    input_grad = join_features(lax.all_to_all(back, ("yh", "x"), 0, 0, tiled=True))
    half = proj_half(place, pairs)
    grad_point, grad_atrous = place_grads(place, pairs)
    grad_proj = join_proj(place, half, swap(half, "c"))

    return (
        projected.reshape(1, 3, WIDTH, 256),
        input_grad.reshape(1, 3, WIDTH, 2048),
        grad_point,
        grad_atrous,
        grad_proj,
    )


def solution(mesh):
    fine = Mesh(mesh.devices.reshape(4, 2, 2, 4, 2), ("z", "yl", "yh", "x", "c"))
    rep, sp = ("z", "yl"), ("yh", "x", "c")
    in_specs = (
        P(rep, sp, None, None),
        P(None, None, sp),
        P(None, sp),
        P(),
        P(rep, sp, None, None),
    )
    out_specs = (
        P(rep, sp, None, None),
        P(rep, sp, None, None),
        P(sp, None),
        P(None, sp, None),
        P(),
    )
    return jax.shard_map(shards, mesh=fine, in_specs=in_specs, out_specs=out_specs, check_vma=False)
```

```python
import jax
import jax.numpy as jnp
from jax import lax
from jax.experimental import pallas as pl
from jax.experimental.pallas import tpu as pltpu
from jax.sharding import Mesh
from jax.sharding import PartitionSpec as P

DILATIONS = (6, 12, 18)
CHIPS = 8
CELLS = 216
PADDED = 224
WIDTH = 72
HALO = 3
K = 512
TAPS = 28
COLS = TAPS * 128
QUARTER = TAPS // 4
BF16 = jnp.bfloat16
F32 = jnp.float32
VMEM = pl.BlockSpec(memory_space=pltpu.VMEM)
SMEM = pl.BlockSpec(memory_space=pltpu.SMEM)
ANY = pl.BlockSpec(memory_space=pl.ANY)


def tap_of(g, ky, kx):
    return 1 + 9 * g + 3 * (ky + 1) + (kx + 1)


def tap_pairs():
    def tap(g, ky, kx):
        return (tap_of(g, ky, kx), g, ky, kx)

    pairs = [((0, -1, 0, 0), tap(0, 0, 0)), (tap(1, 0, 0), tap(2, 0, 0))]
    for ky in (0, -1, 1):
        for g in range(3):
            pairs.append((tap(g, ky, -1), tap(g, ky, 1)))
    for ky in (-1, 1):
        pairs.append((tap(0, ky, 0), tap(1, ky, 0)))
    pairs.append((tap(2, -1, 0), tap(2, 1, 0)))
    return pairs


PAIRS = tap_pairs()


def params(mib):
    return pltpu.CompilerParams(vmem_limit_bytes=mib << 20)


def cost(flops, nbytes):
    return pl.CostEstimate(flops=flops, bytes_accessed=nbytes, transcendentals=0)


CONV_COST = cost(2 * 1728 * K * COLS, 8 << 20)


def cell_column(rows):
    row = lax.broadcasted_iota(jnp.int32, (rows, 128), 0)
    return jnp.where(row >= 144, row - 144, jnp.where(row >= 72, row - 72, row))


def split_features_kernel(x, out):
    for col in range(4):
        for yh in range(2):
            part = x[:, (yh * 4 + col) * 256 : (yh * 4 + col + 1) * 256]
            for dest in range(2):
                out[dest * 4 + col, :CELLS, yh * 256 : (yh + 1) * 256] = part
    for chip in range(CHIPS):
        out[chip, CELLS:] = jnp.zeros((PADDED - CELLS, K), BF16)


def split_features(x):
    return pl.pallas_call(
        split_features_kernel,
        out_shape=jax.ShapeDtypeStruct((CHIPS, PADDED, K), BF16),
        in_specs=[VMEM],
        out_specs=VMEM,
        compiler_params=params(16),
        cost_estimate=cost(0, 3 << 20),
    )(x)


def split_weights_kernel(place, point, atrous, out0, out1, out2, out3, taps, sem):
    z, x = place[0], place[1]
    begin = jnp.where(z == 0, 0, QUARTER * z - 1)
    copy = pltpu.make_async_copy(atrous.at[pl.ds(begin, QUARTER)], taps.at[pl.ds(1, QUARTER)], sem)
    copy.start()
    taps[0] = point[...]
    copy.wait()
    first = jnp.where(z == 0, 0, 1)
    for d, out in enumerate((out0, out1, out2, out3)):
        col = lax.rem(x + d, 4)
        for yh in range(2):
            lanes = pl.ds(pl.multiple_of((yh * 4 + col) * 256, 256), 256)
            for t in range(QUARTER):
                out[t, :, yh * 256 : (yh + 1) * 256] = taps[first + t, :, lanes]


def split_weights(place, point, atrous):
    return pl.pallas_call(
        split_weights_kernel,
        out_shape=(jax.ShapeDtypeStruct((QUARTER, 16, K), BF16),) * 4,
        in_specs=[SMEM, VMEM, ANY],
        out_specs=(VMEM,) * 4,
        scratch_shapes=[pltpu.VMEM((QUARTER + 1, 16, 2048), BF16), pltpu.SemaphoreType.DMA],
        compiler_params=params(16),
        cost_estimate=cost(0, 1 << 20),
    )(place, point, atrous)


WEIGHTS = (2, 4, 4, QUARTER, 16, K)


def weights_of(wt, taps):
    rows = []
    for t in taps:
        rows += [wt[c, t // QUARTER, x, t % QUARTER] for x in range(4) for c in range(2)]
    return jnp.concatenate(rows, 0)


def stack_columns_kernel(place, b0, b1, b2, b3, out):
    for d, block in enumerate((b0, b1, b2, b3)):
        out[lax.rem(place[1] + 4 - d, 4)] = block[...]


def stack_columns(place, blocks):
    return pl.pallas_call(
        stack_columns_kernel,
        out_shape=jax.ShapeDtypeStruct((4, QUARTER, 16, K), BF16),
        in_specs=[SMEM] + [VMEM] * 4,
        out_specs=VMEM,
        compiler_params=params(16),
        cost_estimate=cost(0, 1 << 20),
    )(place, *blocks)


def forward_kernel(place, x, *refs):
    blocks, (out, kept, done, acc, out_sem, wt, w_sem) = refs[:8], refs[8:]
    for n, block in enumerate(blocks):
        c = place[2] if n < 4 else 1 - place[2]
        wt[c, lax.rem(place[0] + 4 - n % 4, 4)] = block[...]
    keep = pltpu.make_async_copy(wt, kept, w_sem)
    keep.start()

    def span(g, ky):
        return max(0, ky * (g + 1)), CHIPS + min(0, ky * (g + 1))

    for pair in PAIRS:
        begin = min(span(g, ky)[0] for _, g, ky, _ in pair)
        end = max(span(g, ky)[1] for _, g, ky, _ in pair)
        rows = x[begin:end].reshape((end - begin) * PADDED, K)
        right = weights_of(wt, [tap[0] for tap in pair])
        y = lax.dot_general(rows, right, (((1,), (1,)), ((), ())), preferred_element_type=F32)
        y = y.reshape(end - begin, PADDED, 256)
        for half, (_, g, ky, kx) in enumerate(pair):
            which = 3 if g < 0 else (g if kx == 0 else 4 + 2 * g + (kx + 1) // 2)
            lo, hi = span(g, ky)
            part = y[lo - begin : hi - begin, :, half * 128 : (half + 1) * 128]
            to = slice(lo - ky * (g + 1), hi - ky * (g + 1))
            if ky == 0:
                acc[which, to] = part
            else:
                acc[which, to] += part

    column = cell_column(PADDED)

    def finish(j, _):
        parts = [acc[3, j]]
        for g, d in enumerate(DILATIONS):
            minus = pltpu.roll(acc[4 + 2 * g, j], d, 0)
            plus = pltpu.roll(acc[5 + 2 * g, j], PADDED - d, 0)
            parts.append(
                acc[g, j]
                + jnp.where(column >= d, minus, 0.0)
                + jnp.where(column < WIDTH - d, plus, 0.0)
            )
        done[j] = jnp.concatenate(parts, 1).astype(BF16)[:CELLS]
        pltpu.make_async_copy(done.at[j], out.at[j], out_sem.at[j]).start()
        return 0

    lax.fori_loop(0, CHIPS, finish, 0)
    for j in range(CHIPS):
        pltpu.make_async_copy(done.at[j], out.at[j], out_sem.at[j]).wait()
    keep.wait()


def forward(place, x, blocks):
    return pl.pallas_call(
        forward_kernel,
        out_shape=(
            jax.ShapeDtypeStruct((CHIPS, CELLS, 512), BF16),
            jax.ShapeDtypeStruct(WEIGHTS, BF16),
        ),
        in_specs=[SMEM] + [VMEM] * 9,
        out_specs=(ANY,) * 2,
        scratch_shapes=[
            pltpu.VMEM((CHIPS, CELLS, 512), BF16),
            pltpu.VMEM((10, CHIPS, PADDED, 128), F32),
            pltpu.SemaphoreType.DMA((CHIPS,)),
            pltpu.VMEM(WEIGHTS, BF16),
            pltpu.SemaphoreType.DMA,
        ],
        compiler_params=params(56),
        cost_estimate=CONV_COST,
    )(place, x, *blocks)


def sigmoid(v):
    return 1.0 / (1.0 + jnp.exp(-v))


def middle_kernel(got, proj, cot, projected, send, grad):
    parts = []
    for yh in range(2):
        total = got[yh * 4].astype(F32)
        for x in range(1, 4):
            total = total + got[yh * 4 + x].astype(F32)
        parts.append(total)
    pre = jnp.concatenate(parts, 1).astype(BF16).astype(F32)
    sig = sigmoid(pre)
    acts = (pre * sig).astype(BF16)
    slope = sig + pre * sig * (1.0 - sig)
    weight = proj[...]
    out_pre = jnp.dot(acts, weight, preferred_element_type=F32)
    osig = sigmoid(out_pre)
    projected[...] = (out_pre * osig).astype(BF16)
    dout = (cot[...].astype(F32) * (osig + out_pre * osig * (1.0 - osig))).astype(BF16)
    dacts = lax.dot_general(
        dout, weight, (((1,), (1,)), ((), ())), preferred_element_type=F32
    )
    dpre = (dacts * slope).astype(BF16)
    for yh in range(2):
        for x in range(4):
            send[yh * 4 + x] = dpre[:, yh * 512 : (yh + 1) * 512]
    grad[...] = lax.dot_general(
        acts, dout, (((0,), (0,)), ((), ())), preferred_element_type=F32
    )


def middle(got, proj, cot):
    return pl.pallas_call(
        middle_kernel,
        out_shape=(
            jax.ShapeDtypeStruct((CELLS, 256), BF16),
            jax.ShapeDtypeStruct((CHIPS, CELLS, 512), BF16),
            jax.ShapeDtypeStruct((1024, 256), F32),
        ),
        in_specs=[VMEM] * 3,
        out_specs=(VMEM,) * 3,
        compiler_params=params(48),
    )(got, proj, cot)


SPREAD = [pltpu.VMEM((9, CHIPS + 2 * HALO, PADDED, 128), BF16), pltpu.VMEM((CHIPS, PADDED, 128), BF16)]


def spread(got, moved, point):
    column = cell_column(CELLS)
    for n in range(9):
        moved[n, :HALO] = jnp.zeros((HALO, PADDED, 128), BF16)
        moved[n, HALO + CHIPS :] = jnp.zeros((HALO, PADDED, 128), BF16)
    tail = jnp.zeros((PADDED - CELLS, 128), BF16)

    def step(j, _):
        point[j, :CELLS] = got[j, :, :128]
        point[j, CELLS:] = tail
        for g, d in enumerate(DILATIONS):
            v = got[j, :, (g + 1) * 128 : (g + 2) * 128]
            wide = v.astype(F32)
            minus = jnp.where(column < WIDTH - d, pltpu.roll(wide, CELLS - d, 0), 0.0)
            plus = jnp.where(column >= d, pltpu.roll(wide, d, 0), 0.0)
            for kx, part in enumerate((minus.astype(BF16), v, plus.astype(BF16))):
                moved[3 * g + kx, HALO + j, :CELLS] = part
                moved[3 * g + kx, HALO + j, CELLS:] = tail
        return 0

    lax.fori_loop(0, CHIPS, step, 0)


def spread_columns(moved, point, tap, first, count):
    _, g, ky, kx = tap
    if g < 0:
        v = point[pl.ds(first, count)]
    else:
        v = moved[3 * g + kx + 1, pl.ds(HALO + first - ky * (g + 1), count)]
    return v.reshape(count * PADDED, 128)


def turn_features_kernel(place, x, out):
    flat = x[...].reshape(CHIPS * PADDED, K)
    for yh in range(2):
        for core in range(2):
            lanes = slice((yh * 2 + core) * 128, (yh * 2 + core + 1) * 128)
            away = jnp.where(place[2] == core, 0, 1)
            for n in range(7):
                block = flat[n * 256 : (n + 1) * 256, lanes]
                out[2 * away + yh, :, n * 256 : (n + 1) * 256] = block.T


def turn_features(place, x):
    return pl.pallas_call(
        turn_features_kernel,
        out_shape=jax.ShapeDtypeStruct((4, 128, CHIPS * PADDED), BF16),
        in_specs=[SMEM, VMEM],
        out_specs=VMEM,
        compiler_params=params(32),
        cost_estimate=cost(0, 8 << 20),
    )(place, x)


def kernel_grad_kernel(got, xt, keep, send, kept, sent, xs, x_sem, out_sem, moved, point):
    load = pltpu.make_async_copy(xt, xs, x_sem)
    load.start()
    spread(got, moved, point)
    load.wait()
    left = xs[...].reshape(K, CHIPS * PADDED)
    stores = []
    for pair in PAIRS:
        right = jnp.concatenate([spread_columns(moved, point, tap, 0, CHIPS) for tap in pair], 1)
        part = jnp.dot(left, right, preferred_element_type=F32).astype(BF16)
        for half, tap in enumerate(pair):
            cols = pl.ds(tap[0] * 128, 128)
            block = part[:, half * 128 : (half + 1) * 128].reshape(2, 2, 8, 16, 128)
            for n, (local, out) in enumerate(((kept, keep), (sent, send))):
                for yh in range(2):
                    local[:, yh, :, cols] = block[n, yh]
                view = (slice(None), slice(None), slice(None), cols)
                stores.append(
                    pltpu.make_async_copy(local.at[view], out.at[view], out_sem.at[n, tap[0]])
                )
                stores[-1].start()
    for copy in stores:
        copy.wait()


def kernel_grad(got, xt):
    local = pltpu.VMEM((8, 2, 16, COLS), BF16)
    return pl.pallas_call(
        kernel_grad_kernel,
        out_shape=(jax.ShapeDtypeStruct((8, 2, 16, COLS), BF16),) * 2,
        in_specs=[VMEM, ANY],
        out_specs=(ANY,) * 2,
        scratch_shapes=[
            local,
            local,
            pltpu.VMEM((4, 128, CHIPS * PADDED), BF16),
            pltpu.SemaphoreType.DMA,
            pltpu.SemaphoreType.DMA((2, TAPS)),
        ]
        + SPREAD,
        compiler_params=params(56),
        cost_estimate=CONV_COST,
    )(got, xt)


def add_cores_kernel(mine, other, out):
    out[...] = (mine[...].astype(F32) + other[...].astype(F32)).astype(BF16)


def add_cores(mine, other):
    spec = pl.BlockSpec((2, 2, 16, COLS), lambda i: (i, 0, 0, 0))
    return pl.pallas_call(
        add_cores_kernel,
        grid=(4,),
        out_shape=jax.ShapeDtypeStruct((8, 2, 16, COLS), BF16),
        in_specs=[spec] * 2,
        out_specs=spec,
        compiler_params=params(16),
    )(mine, other)


def sum_samples_kernel(got, out):
    for yh in range(2):
        total = got[yh].astype(F32)
        for rep in range(1, 8):
            total = total + got[2 * rep + yh].astype(F32)
        out[yh] = total.astype(BF16)


def sum_samples(got):
    return pl.pallas_call(
        sum_samples_kernel,
        out_shape=jax.ShapeDtypeStruct((2, 16, COLS), BF16),
        in_specs=[VMEM],
        out_specs=VMEM,
        compiler_params=params(24),
    )(got)


def feature_grad_kernel(got, kept, out, moved, point, wt, w_sem):
    load = pltpu.make_async_copy(kept, wt, w_sem)
    load.start()
    spread(got, moved, point)
    load.wait()
    taps = [tap for pair in PAIRS for tap in pair]

    def step(i, _):
        left = jnp.concatenate([spread_columns(moved, point, tap, 2 * i, 2) for tap in taps], 1)
        right = weights_of(wt, [tap[0] for tap in taps])
        part = jnp.dot(left, right, preferred_element_type=F32).astype(BF16)
        for sub in range(2):
            out[2 * i + sub] = part[sub * PADDED : sub * PADDED + CELLS]
        return 0

    lax.fori_loop(0, CHIPS // 2, step, 0)


def feature_grad(got, kept):
    return pl.pallas_call(
        feature_grad_kernel,
        out_shape=jax.ShapeDtypeStruct((CHIPS, CELLS, K), BF16),
        in_specs=[VMEM, ANY],
        out_specs=VMEM,
        scratch_shapes=SPREAD + [pltpu.VMEM(WEIGHTS, BF16), pltpu.SemaphoreType.DMA],
        compiler_params=params(56),
        cost_estimate=CONV_COST,
    )(got, kept)


def pack_sums_kernel(mine, other, proj, out):
    for n, block in enumerate((mine, other)):
        for yh in range(2):
            out[n, yh, :, :COLS] = block[yh]
            for half in range(2):
                row = half * 64 + n * 32 + yh * 16
                lane = COLS + half * 256
                out[n, yh, :, lane : lane + 256] = proj[row : row + 16, :].astype(BF16)


def pack_sums(mine, other, proj):
    return pl.pallas_call(
        pack_sums_kernel,
        out_shape=jax.ShapeDtypeStruct((2, 2, 16, COLS + 512), BF16),
        in_specs=[VMEM] * 3,
        out_specs=VMEM,
        compiler_params=params(16),
    )(mine, other, proj)


def place_grads_kernel(place, *refs):
    point, atrous = refs[4], refs[5]
    z, yl = place[0], place[3]
    for d in range(4):
        for l in range(2):
            rep = 2 * lax.rem(z + 4 - d, 4) + lax.rem(yl + l, 2)
            rows = pl.ds(pl.multiple_of(rep * 16, 16), 16)
            for yh in range(2):
                cols = slice(yh * 128, (yh + 1) * 128)
                for t in range(TAPS):
                    part = refs[d][l, yh, :, t * 128 : (t + 1) * 128].astype(F32) * 0.125
                    if t == 0:
                        point[rows, cols] = part
                    else:
                        atrous[t - 1, rows, cols] = part


def place_grads(place, blocks):
    return pl.pallas_call(
        place_grads_kernel,
        out_shape=(
            jax.ShapeDtypeStruct((128, 256), F32),
            jax.ShapeDtypeStruct((27, 128, 256), F32),
        ),
        in_specs=[SMEM] + [VMEM] * 4,
        out_specs=(VMEM,) * 2,
        compiler_params=params(40),
    )(place, *blocks)


def proj_half_kernel(place, b0, b1, b2, b3, out):
    for d, block in enumerate((b0, b1, b2, b3)):
        z = lax.rem(place[0] + 4 - d, 4)
        row = gray(z) * 256 + (z >> 1) * 128
        for n in range(2):
            for yh in range(2):
                for half in range(2):
                    at = pl.multiple_of(row + half * 64 + n * 32 + yh * 16, 16)
                    lane = COLS + half * 256
                    out[pl.ds(at, 16), :] = block[n, yh, :, lane : lane + 256]


def proj_half(place, blocks):
    return pl.pallas_call(
        proj_half_kernel,
        out_shape=jax.ShapeDtypeStruct((512, 256), BF16),
        in_specs=[SMEM] + [VMEM] * 4,
        out_specs=VMEM,
        compiler_params=params(24),
    )(place, *blocks)


def join_proj_kernel(place, mine, other, out):
    c = place[2]
    for half, block in enumerate((mine, other)):
        yh = c if half == 0 else 1 - c
        for branch in range(4):
            part = block[branch * 128 : (branch + 1) * 128, :].astype(F32) * 0.125
            rows = pl.multiple_of(branch * 256 + yh * 128, 128)
            out[pl.ds(rows, 128), :] = part


def join_proj(place, mine, other):
    return pl.pallas_call(
        join_proj_kernel,
        out_shape=jax.ShapeDtypeStruct((1024, 256), F32),
        in_specs=[SMEM, VMEM, VMEM],
        out_specs=VMEM,
        compiler_params=params(16),
    )(place, mine, other)


def join_features_kernel(got, out):
    for x in range(4):
        total = (got[x].astype(F32) + got[4 + x].astype(F32)).astype(BF16)
        for yh in range(2):
            out[:, (yh * 4 + x) * 256 : (yh * 4 + x + 1) * 256] = total[:, yh * 256 : (yh + 1) * 256]


def join_features(got):
    return pl.pallas_call(
        join_features_kernel,
        out_shape=jax.ShapeDtypeStruct((CELLS, 2048), BF16),
        in_specs=[VMEM],
        out_specs=VMEM,
        compiler_params=params(16),
    )(got)


def turn(n, d):
    return [(i, (i + d) % n) for i in range(n)]


def swap(v, axis):
    return lax.ppermute(v, axis, turn(2, 1))


BESIDE = [(i, i ^ 1) for i in range(4)]
ACROSS = [(i, 3 - i) for i in range(4)]


def gray(i):
    return (i ^ (i >> 1)) & 1


def halved(v, axis, pairs, bit):
    half = v.shape[0] // 2
    mine = lax.dynamic_slice_in_dim(v, bit * half, half, 0)
    theirs = lax.dynamic_slice_in_dim(v, (1 - bit) * half, half, 0)
    return mine + lax.ppermute(theirs.astype(BF16), axis, pairs).astype(F32)


def added(v, axis, pairs):
    return v + lax.ppermute(v.astype(BF16), axis, pairs).astype(F32)


def added_over_y(v):
    total, sent = v, v.astype(BF16)
    for l, h in ((0, 1), (1, 0), (1, 1)):
        pairs = [(2 * i + j, 2 * ((i + l) % 2) + (j + h) % 2) for i in range(2) for j in range(2)]
        total = total + lax.ppermute(sent, ("yl", "yh"), pairs).astype(F32)
    return total


def shards(features, atrous_weight, point_weight, proj_weight, cotangent):
    place = jnp.stack([lax.axis_index(a) for a in ("z", "x", "c", "yl", "yh")]).astype(jnp.int32)

    atrous_t = jnp.transpose(atrous_weight, (0, 2, 1))
    parts = split_weights(place, jnp.transpose(point_weight, (1, 0)), atrous_t)
    from_x = [parts[0]] + [lax.ppermute(parts[d], "x", turn(4, d)) for d in (1, 2, 3)]
    quarter = stack_columns(place, from_x)
    quarters = [quarter] + [lax.ppermute(quarter, "z", turn(4, d)) for d in (1, 2, 3)]
    blocks = quarters + [swap(v, "c") for v in quarters]

    x_send = split_features(features.reshape(CELLS, 2048))
    x_send, quarter = lax.optimization_barrier((x_send, quarter))
    x = lax.all_to_all(x_send, ("yh", "x"), 0, 0, tiled=True)

    partial, wt = forward(place, x, blocks)
    got = lax.all_to_all(partial, ("yh", "x"), 0, 0, tiled=True)
    proj = proj_weight.reshape(4, 2, 128, 256).transpose(1, 0, 2, 3).reshape(1024, 256)
    projected, d_send, proj_part = middle(got, proj, cotangent.reshape(CELLS, 256))
    dpre = lax.all_to_all(d_send, ("yh", "x"), 0, 0, tiled=True)
    xt = turn_features(place, x)

    core, layer = lax.axis_index("c"), lax.axis_index("z")
    share = halved(proj_part, "c", turn(2, 1), core)
    share = halved(share, "z", BESIDE, gray(layer))
    share = halved(share, "z", ACROSS, layer >> 1)
    share = added_over_y(share)
    dpre, share = lax.optimization_barrier((dpre, share))

    keep, send = kernel_grad(dpre, xt)
    g_part = add_cores(keep, swap(send, "c"))
    g_got = lax.all_to_all(g_part.reshape(16, 16, COLS), ("z", "yl", "yh"), 0, 0, tiled=True)

    dpre, _ = lax.optimization_barrier((dpre, g_part))
    back = feature_grad(dpre, wt)
    share, _ = lax.optimization_barrier((share, back))
    share = added(share, "x", BESIDE)
    share = added(share, "x", ACROSS)

    g_got, back, share = lax.optimization_barrier((g_got, back, share))
    g_sum = sum_samples(g_got)
    swapped = swap(g_sum, "yl")
    back, swapped = lax.optimization_barrier((back, swapped))
    pair = pack_sums(g_sum, swapped, share)
    pairs = [pair] + [lax.ppermute(pair, "z", turn(4, d)) for d in (1, 2, 3)]
    input_grad = join_features(lax.all_to_all(back, ("yh", "x"), 0, 0, tiled=True))
    half = proj_half(place, pairs)
    grad_point, grad_atrous = place_grads(place, pairs)
    grad_proj = join_proj(place, half, swap(half, "c"))

    return (
        projected.reshape(1, 3, WIDTH, 256),
        input_grad.reshape(1, 3, WIDTH, 2048),
        grad_point,
        grad_atrous,
        grad_proj,
    )


def solution(mesh):
    fine = Mesh(mesh.devices.reshape(4, 2, 2, 4, 2), ("z", "yl", "yh", "x", "c"))
    rep, sp = ("z", "yl"), ("yh", "x", "c")
    in_specs = (
        P(rep, sp, None, None),
        P(None, None, sp),
        P(None, sp),
        P(),
        P(rep, sp, None, None),
    )
    out_specs = (
        P(rep, sp, None, None),
        P(rep, sp, None, None),
        P(sp, None),
        P(None, sp, None),
        P(),
    )
    return jax.shard_map(shards, mesh=fine, in_specs=in_specs, out_specs=out_specs, check_vma=False)
```

```python
import jax
import jax.numpy as jnp
from jax import lax
from jax.experimental import pallas as pl
from jax.experimental.pallas import tpu as pltpu
from jax.sharding import Mesh
from jax.sharding import PartitionSpec as P

DILATIONS = (6, 12, 18)
CHIPS = 8
CELLS = 216
PADDED = 224
WIDTH = 72
HALO = 3
K = 512
TAPS = 28
COLS = TAPS * 128
QUARTER = TAPS // 4
BF16 = jnp.bfloat16
F32 = jnp.float32
VMEM = pl.BlockSpec(memory_space=pltpu.VMEM)
SMEM = pl.BlockSpec(memory_space=pltpu.SMEM)
ANY = pl.BlockSpec(memory_space=pl.ANY)


def tap_of(g, ky, kx):
    return 1 + 9 * g + 3 * (ky + 1) + (kx + 1)


def tap_pairs():
    def tap(g, ky, kx):
        return (tap_of(g, ky, kx), g, ky, kx)

    sides = [[(tap(g, ky, -1), tap(g, ky, 1)) for ky in (0, -1, 1)] for g in range(3)]
    pairs = [((0, -1, 0, 0), tap(0, 0, 0))] + sides[0] + sides[1]
    pairs += [(tap(1, 0, 0), tap(2, 0, 0))]
    pairs += [(tap(0, ky, 0), tap(1, ky, 0)) for ky in (-1, 1)]
    pairs += sides[2] + [(tap(2, -1, 0), tap(2, 1, 0))]
    return pairs


PAIRS = tap_pairs()


def params(mib):
    return pltpu.CompilerParams(vmem_limit_bytes=mib << 20)


def cost(flops, nbytes):
    return pl.CostEstimate(flops=flops, bytes_accessed=nbytes, transcendentals=0)


CONV_COST = cost(2 * 1728 * K * COLS, 8 << 20)


def cell_column(rows):
    row = lax.broadcasted_iota(jnp.int32, (rows, 128), 0)
    return jnp.where(row >= 144, row - 144, jnp.where(row >= 72, row - 72, row))


def split_features_kernel(x, out):
    for col in range(4):
        for yh in range(2):
            part = x[:, (yh * 4 + col) * 256 : (yh * 4 + col + 1) * 256]
            for dest in range(2):
                out[dest * 4 + col, :CELLS, yh * 256 : (yh + 1) * 256] = part
    for chip in range(CHIPS):
        out[chip, CELLS:] = jnp.zeros((PADDED - CELLS, K), BF16)


def split_features(x):
    return pl.pallas_call(
        split_features_kernel,
        out_shape=jax.ShapeDtypeStruct((CHIPS, PADDED, K), BF16),
        in_specs=[VMEM],
        out_specs=VMEM,
        compiler_params=params(16),
        cost_estimate=cost(0, 3 << 20),
    )(x)


def split_weights_kernel(place, point, atrous, out0, out1, out2, out3, taps, sem):
    z, x = place[0], place[1]
    begin = jnp.where(z == 0, 0, QUARTER * z - 1)
    copy = pltpu.make_async_copy(atrous.at[pl.ds(begin, QUARTER)], taps.at[pl.ds(1, QUARTER)], sem)
    copy.start()
    taps[0] = point[...]
    copy.wait()
    first = jnp.where(z == 0, 0, 1)
    for d, out in enumerate((out0, out1, out2, out3)):
        col = lax.rem(x + d, 4)
        for yh in range(2):
            lanes = pl.ds(pl.multiple_of((yh * 4 + col) * 256, 256), 256)
            for t in range(QUARTER):
                out[t, :, yh * 256 : (yh + 1) * 256] = taps[first + t, :, lanes]


def split_weights(place, point, atrous):
    return pl.pallas_call(
        split_weights_kernel,
        out_shape=(jax.ShapeDtypeStruct((QUARTER, 16, K), BF16),) * 4,
        in_specs=[SMEM, VMEM, ANY],
        out_specs=(VMEM,) * 4,
        scratch_shapes=[pltpu.VMEM((QUARTER + 1, 16, 2048), BF16), pltpu.SemaphoreType.DMA],
        compiler_params=params(16),
        cost_estimate=cost(0, 1 << 20),
    )(place, point, atrous)


WEIGHTS = (2, 4, 4, QUARTER, 16, K)


def weights_of(wt, taps):
    rows = []
    for t in taps:
        rows += [wt[c, t // QUARTER, x, t % QUARTER] for x in range(4) for c in range(2)]
    return jnp.concatenate(rows, 0)


def stack_columns_kernel(place, b0, b1, b2, b3, out):
    for d, block in enumerate((b0, b1, b2, b3)):
        out[lax.rem(place[1] + 4 - d, 4)] = block[...]


def stack_columns(place, blocks):
    return pl.pallas_call(
        stack_columns_kernel,
        out_shape=jax.ShapeDtypeStruct((4, QUARTER, 16, K), BF16),
        in_specs=[SMEM] + [VMEM] * 4,
        out_specs=VMEM,
        compiler_params=params(16),
        cost_estimate=cost(0, 1 << 20),
    )(place, *blocks)


def forward_kernel(place, x, *refs):
    blocks, (out, kept, xt, done, acc, out_sem, wt, w_sem, turned, x_sem) = refs[:8], refs[8:]
    for n, block in enumerate(blocks):
        c = place[2] if n < 4 else 1 - place[2]
        wt[c, lax.rem(place[0] + 4 - n % 4, 4)] = block[...]
    keep = pltpu.make_async_copy(wt, kept, w_sem)
    keep.start()
    flat = x[...].reshape(CHIPS * PADDED, K)
    for n in range(7):
        for yh in range(2):
            for core in range(2):
                lane = (yh * 2 + core) * 128
                away = jnp.where(place[2] == core, 0, 1)
                block = flat[n * 256 : (n + 1) * 256, lane : lane + 128]
                turned[2 * away + yh, :, n * 256 : (n + 1) * 256] = block.T
    turn_out = pltpu.make_async_copy(turned, xt, x_sem)
    turn_out.start()

    def span(g, ky):
        return max(0, ky * (g + 1)), CHIPS + min(0, ky * (g + 1))

    for pair in PAIRS:
        begin = min(span(g, ky)[0] for _, g, ky, _ in pair)
        end = max(span(g, ky)[1] for _, g, ky, _ in pair)
        rows = x[begin:end].reshape((end - begin) * PADDED, K)
        right = weights_of(wt, [tap[0] for tap in pair])
        y = lax.dot_general(rows, right, (((1,), (1,)), ((), ())), preferred_element_type=F32)
        y = y.reshape(end - begin, PADDED, 256)
        for half, (_, g, ky, kx) in enumerate(pair):
            which = 3 if g < 0 else (g if kx == 0 else 4 + 2 * g + (kx + 1) // 2)
            lo, hi = span(g, ky)
            part = y[lo - begin : hi - begin, :, half * 128 : (half + 1) * 128]
            to = slice(lo - ky * (g + 1), hi - ky * (g + 1))
            if ky == 0:
                acc[which, to] = part
            else:
                acc[which, to] += part

    column = cell_column(PADDED)

    def finish(j, _):
        parts = [acc[3, j]]
        for g, d in enumerate(DILATIONS):
            minus = pltpu.roll(acc[4 + 2 * g, j], d, 0)
            plus = pltpu.roll(acc[5 + 2 * g, j], PADDED - d, 0)
            parts.append(
                acc[g, j]
                + jnp.where(column >= d, minus, 0.0)
                + jnp.where(column < WIDTH - d, plus, 0.0)
            )
        done[j] = jnp.concatenate(parts, 1).astype(BF16)[:CELLS]
        pltpu.make_async_copy(done.at[j], out.at[j], out_sem.at[j]).start()
        return 0

    lax.fori_loop(0, CHIPS, finish, 0)
    for j in range(CHIPS):
        pltpu.make_async_copy(done.at[j], out.at[j], out_sem.at[j]).wait()
    keep.wait()
    turn_out.wait()


def forward(place, x, blocks):
    return pl.pallas_call(
        forward_kernel,
        out_shape=(
            jax.ShapeDtypeStruct((CHIPS, CELLS, 512), BF16),
            jax.ShapeDtypeStruct(WEIGHTS, BF16),
            jax.ShapeDtypeStruct((4, 128, CHIPS * PADDED), BF16),
        ),
        in_specs=[SMEM] + [VMEM] * 9,
        out_specs=(ANY,) * 3,
        scratch_shapes=[
            pltpu.VMEM((CHIPS, CELLS, 512), BF16),
            pltpu.VMEM((10, CHIPS, PADDED, 128), F32),
            pltpu.SemaphoreType.DMA((CHIPS,)),
            pltpu.VMEM(WEIGHTS, BF16),
            pltpu.SemaphoreType.DMA,
            pltpu.VMEM((4, 128, CHIPS * PADDED), BF16),
            pltpu.SemaphoreType.DMA,
        ],
        compiler_params=params(51),
        cost_estimate=CONV_COST,
    )(place, x, *blocks)


def sigmoid(v):
    return 1.0 / (1.0 + jnp.exp(-v))


def middle_kernel(got, proj, cot, projected, send, grad):
    parts = []
    for yh in range(2):
        total = got[yh * 4].astype(F32)
        for x in range(1, 4):
            total = total + got[yh * 4 + x].astype(F32)
        parts.append(total)
    pre = jnp.concatenate(parts, 1).astype(BF16).astype(F32)
    sig = sigmoid(pre)
    acts = (pre * sig).astype(BF16)
    slope = sig + pre * sig * (1.0 - sig)
    weight = proj[...]
    out_pre = jnp.dot(acts, weight, preferred_element_type=F32)
    osig = sigmoid(out_pre)
    projected[...] = (out_pre * osig).astype(BF16)
    dout = (cot[...].astype(F32) * (osig + out_pre * osig * (1.0 - osig))).astype(BF16)
    dacts = lax.dot_general(
        dout, weight, (((1,), (1,)), ((), ())), preferred_element_type=F32
    )
    dpre = (dacts * slope).astype(BF16)
    for yh in range(2):
        for x in range(4):
            send[yh * 4 + x] = dpre[:, yh * 512 : (yh + 1) * 512]
    grad[...] = lax.dot_general(
        acts, dout, (((0,), (0,)), ((), ())), preferred_element_type=F32
    )


def middle(got, proj, cot):
    return pl.pallas_call(
        middle_kernel,
        out_shape=(
            jax.ShapeDtypeStruct((CELLS, 256), BF16),
            jax.ShapeDtypeStruct((CHIPS, CELLS, 512), BF16),
            jax.ShapeDtypeStruct((1024, 256), F32),
        ),
        in_specs=[VMEM] * 3,
        out_specs=(VMEM,) * 3,
        compiler_params=params(48),
    )(got, proj, cot)


SPREAD = [pltpu.VMEM((9, CHIPS + 2 * HALO, PADDED, 128), BF16), pltpu.VMEM((CHIPS, PADDED, 128), BF16)]


def spread_point(got, point, j):
    point[j, :CELLS] = got[j, :, :128]
    point[j, CELLS:] = jnp.zeros((PADDED - CELLS, 128), BF16)


def spread_branch(got, moved, column, g, j):
    d = DILATIONS[g]
    v = got[j, :, (g + 1) * 128 : (g + 2) * 128]
    wide = v.astype(F32)
    minus = jnp.where(column < WIDTH - d, pltpu.roll(wide, CELLS - d, 0), 0.0)
    plus = jnp.where(column >= d, pltpu.roll(wide, d, 0), 0.0)
    for kx, part in enumerate((minus.astype(BF16), v, plus.astype(BF16))):
        moved[3 * g + kx, HALO + j, :CELLS] = part
        moved[3 * g + kx, HALO + j, CELLS:] = jnp.zeros((PADDED - CELLS, 128), BF16)


def spread_edges(moved, g):
    for n in range(3 * g, 3 * g + 3):
        moved[n, :HALO] = jnp.zeros((HALO, PADDED, 128), BF16)
        moved[n, HALO + CHIPS :] = jnp.zeros((HALO, PADDED, 128), BF16)


def spread(got, moved, point):
    column = cell_column(CELLS)
    for g in range(3):
        spread_edges(moved, g)

    def step(j, _):
        spread_point(got, point, j)
        for g in range(3):
            spread_branch(got, moved, column, g, j)
        return 0

    lax.fori_loop(0, CHIPS, step, 0)


def spread_columns(moved, point, tap, first, count):
    _, g, ky, kx = tap
    if g < 0:
        v = point[pl.ds(first, count)]
    else:
        v = moved[3 * g + kx + 1, pl.ds(HALO + first - ky * (g + 1), count)]
    return v.reshape(count * PADDED, 128)


def kernel_grad_kernel(got, xt, keep, send, again, sent, xs, x_sem, g_sem, out_sem, moved, point):
    load = pltpu.make_async_copy(xt, xs, x_sem)
    load.start()
    copy_got = pltpu.make_async_copy(got, again, g_sem)
    copy_got.start()
    column = cell_column(CELLS)
    stores = []
    ready = -1
    for index, pair in enumerate(PAIRS):
        for g in range(ready + 1, max(tap[1] for tap in pair) + 1):
            spread_edges(moved, g)
            for j in range(CHIPS):
                if g == 0:
                    spread_point(got, point, j)
                spread_branch(got, moved, column, g, j)
            ready = g
        if index == 0:
            load.wait()
        left = xs[...].reshape(K, CHIPS * PADDED)
        right = jnp.concatenate([spread_columns(moved, point, tap, 0, CHIPS) for tap in pair], 1)
        part = jnp.dot(left, right, preferred_element_type=F32).astype(BF16)
        for half, tap in enumerate(pair):
            cols = pl.ds(tap[0] * 128, 128)
            block = part[:, half * 128 : (half + 1) * 128].reshape(2, 2, 8, 16, 128)
            for yh in range(2):
                keep[:, yh, :, cols] = block[0, yh]
                sent[:, yh, :, cols] = block[1, yh]
            view = (slice(None), slice(None), slice(None), cols)
            stores.append(pltpu.make_async_copy(sent.at[view], send.at[view], out_sem.at[tap[0]]))
            stores[-1].start()
    for copy in stores:
        copy.wait()
    copy_got.wait()


def kernel_grad(got, xt):
    return pl.pallas_call(
        kernel_grad_kernel,
        out_shape=(jax.ShapeDtypeStruct((8, 2, 16, COLS), BF16),) * 2
        + (jax.ShapeDtypeStruct((CHIPS, CELLS, 512), BF16),),
        in_specs=[VMEM, ANY],
        out_specs=(VMEM, ANY, ANY),
        scratch_shapes=[
            pltpu.VMEM((8, 2, 16, COLS), BF16),
            pltpu.VMEM((4, 128, CHIPS * PADDED), BF16),
            pltpu.SemaphoreType.DMA,
            pltpu.SemaphoreType.DMA,
            pltpu.SemaphoreType.DMA((TAPS,)),
        ]
        + SPREAD,
        compiler_params=params(48),
        cost_estimate=CONV_COST,
    )(got, xt)


def add_cores_kernel(mine, other, out):
    out[...] = (mine[...].astype(F32) + other[...].astype(F32)).astype(BF16)


def add_cores(mine, other):
    spec = pl.BlockSpec((2, 2, 16, COLS), lambda i: (i, 0, 0, 0))
    return pl.pallas_call(
        add_cores_kernel,
        grid=(4,),
        out_shape=jax.ShapeDtypeStruct((8, 2, 16, COLS), BF16),
        in_specs=[spec] * 2,
        out_specs=spec,
        compiler_params=params(16),
    )(mine, other)


def sum_samples_kernel(got, out):
    for yh in range(2):
        total = got[yh].astype(F32)
        for rep in range(1, 8):
            total = total + got[2 * rep + yh].astype(F32)
        out[yh] = total.astype(BF16)


def sum_samples(got):
    return pl.pallas_call(
        sum_samples_kernel,
        out_shape=jax.ShapeDtypeStruct((2, 16, COLS), BF16),
        in_specs=[VMEM],
        out_specs=VMEM,
        compiler_params=params(24),
    )(got)


def feature_grad_kernel(got, kept, out, moved, point, wt, w_sem):
    load = pltpu.make_async_copy(kept, wt, w_sem)
    load.start()
    spread(got, moved, point)
    load.wait()
    taps = [tap for pair in PAIRS for tap in pair]

    def step(i, _):
        left = jnp.concatenate([spread_columns(moved, point, tap, 2 * i, 2) for tap in taps], 1)
        right = weights_of(wt, [tap[0] for tap in taps])
        part = jnp.dot(left, right, preferred_element_type=F32).astype(BF16)
        for sub in range(2):
            out[2 * i + sub] = part[sub * PADDED : sub * PADDED + CELLS]
        return 0

    lax.fori_loop(0, CHIPS // 2, step, 0)


def feature_grad(got, kept):
    return pl.pallas_call(
        feature_grad_kernel,
        out_shape=jax.ShapeDtypeStruct((CHIPS, CELLS, K), BF16),
        in_specs=[VMEM, ANY],
        out_specs=VMEM,
        scratch_shapes=SPREAD + [pltpu.VMEM(WEIGHTS, BF16), pltpu.SemaphoreType.DMA],
        compiler_params=params(56),
        cost_estimate=CONV_COST,
    )(got, kept)


def pack_sums_kernel(mine, other, proj, out):
    for n, block in enumerate((mine, other)):
        for yh in range(2):
            out[n, yh, :, :COLS] = block[yh]
            for half in range(2):
                row = half * 64 + n * 32 + yh * 16
                lane = COLS + half * 256
                out[n, yh, :, lane : lane + 256] = proj[row : row + 16, :].astype(BF16)


def pack_sums(mine, other, proj):
    return pl.pallas_call(
        pack_sums_kernel,
        out_shape=jax.ShapeDtypeStruct((2, 2, 16, COLS + 512), BF16),
        in_specs=[VMEM] * 3,
        out_specs=VMEM,
        compiler_params=params(16),
    )(mine, other, proj)


def place_grads_kernel(place, *refs):
    point, atrous = refs[4], refs[5]
    z, yl = place[0], place[3]
    for d in range(4):
        for l in range(2):
            rep = 2 * lax.rem(z + 4 - d, 4) + lax.rem(yl + l, 2)
            rows = pl.ds(pl.multiple_of(rep * 16, 16), 16)
            for yh in range(2):
                cols = slice(yh * 128, (yh + 1) * 128)
                for t in range(TAPS):
                    part = refs[d][l, yh, :, t * 128 : (t + 1) * 128].astype(F32) * 0.125
                    if t == 0:
                        point[rows, cols] = part
                    else:
                        atrous[t - 1, rows, cols] = part


def place_grads(place, blocks):
    return pl.pallas_call(
        place_grads_kernel,
        out_shape=(
            jax.ShapeDtypeStruct((128, 256), F32),
            jax.ShapeDtypeStruct((27, 128, 256), F32),
        ),
        in_specs=[SMEM] + [VMEM] * 4,
        out_specs=(VMEM,) * 2,
        compiler_params=params(40),
    )(place, *blocks)


def proj_half_kernel(place, b0, b1, b2, b3, out):
    for d, block in enumerate((b0, b1, b2, b3)):
        z = lax.rem(place[0] + 4 - d, 4)
        row = gray(z) * 256 + (z >> 1) * 128
        for n in range(2):
            for yh in range(2):
                for half in range(2):
                    at = pl.multiple_of(row + half * 64 + n * 32 + yh * 16, 16)
                    lane = COLS + half * 256
                    out[pl.ds(at, 16), :] = block[n, yh, :, lane : lane + 256]


def proj_half(place, blocks):
    return pl.pallas_call(
        proj_half_kernel,
        out_shape=jax.ShapeDtypeStruct((512, 256), BF16),
        in_specs=[SMEM] + [VMEM] * 4,
        out_specs=VMEM,
        compiler_params=params(24),
    )(place, *blocks)


def join_proj_kernel(place, mine, other, out):
    c = place[2]
    for half, block in enumerate((mine, other)):
        yh = c if half == 0 else 1 - c
        for branch in range(4):
            part = block[branch * 128 : (branch + 1) * 128, :].astype(F32) * 0.125
            rows = pl.multiple_of(branch * 256 + yh * 128, 128)
            out[pl.ds(rows, 128), :] = part


def join_proj(place, mine, other):
    return pl.pallas_call(
        join_proj_kernel,
        out_shape=jax.ShapeDtypeStruct((1024, 256), F32),
        in_specs=[SMEM, VMEM, VMEM],
        out_specs=VMEM,
        compiler_params=params(16),
    )(place, mine, other)


def join_features_kernel(got, out):
    for x in range(4):
        total = (got[x].astype(F32) + got[4 + x].astype(F32)).astype(BF16)
        for yh in range(2):
            out[:, (yh * 4 + x) * 256 : (yh * 4 + x + 1) * 256] = total[:, yh * 256 : (yh + 1) * 256]


def join_features(got):
    return pl.pallas_call(
        join_features_kernel,
        out_shape=jax.ShapeDtypeStruct((CELLS, 2048), BF16),
        in_specs=[VMEM],
        out_specs=VMEM,
        compiler_params=params(16),
    )(got)


def turn(n, d):
    return [(i, (i + d) % n) for i in range(n)]


def swap(v, axis):
    return lax.ppermute(v, axis, turn(2, 1))


BESIDE = [(i, i ^ 1) for i in range(4)]
ACROSS = [(i, 3 - i) for i in range(4)]


def gray(i):
    return (i ^ (i >> 1)) & 1


def halved(v, axis, pairs, bit):
    half = v.shape[0] // 2
    mine = lax.dynamic_slice_in_dim(v, bit * half, half, 0)
    theirs = lax.dynamic_slice_in_dim(v, (1 - bit) * half, half, 0)
    return mine + lax.ppermute(theirs.astype(BF16), axis, pairs).astype(F32)


def added(v, axis, pairs):
    return v + lax.ppermute(v.astype(BF16), axis, pairs).astype(F32)


def added_over_y(v):
    total, sent = v, v.astype(BF16)
    for l, h in ((0, 1), (1, 0), (1, 1)):
        pairs = [(2 * i + j, 2 * ((i + l) % 2) + (j + h) % 2) for i in range(2) for j in range(2)]
        total = total + lax.ppermute(sent, ("yl", "yh"), pairs).astype(F32)
    return total


def shards(features, atrous_weight, point_weight, proj_weight, cotangent):
    place = jnp.stack([lax.axis_index(a) for a in ("z", "x", "c", "yl", "yh")]).astype(jnp.int32)

    atrous_t = jnp.transpose(atrous_weight, (0, 2, 1))
    parts = split_weights(place, jnp.transpose(point_weight, (1, 0)), atrous_t)
    from_x = [parts[0]] + [lax.ppermute(parts[d], "x", turn(4, d)) for d in (1, 2, 3)]
    quarter = stack_columns(place, from_x)
    quarters = [quarter] + [lax.ppermute(quarter, "z", turn(4, d)) for d in (1, 2, 3)]
    blocks = quarters + [swap(v, "c") for v in quarters]

    x_send = split_features(features.reshape(CELLS, 2048))
    x_send, quarter = lax.optimization_barrier((x_send, quarter))
    x = lax.all_to_all(x_send, ("yh", "x"), 0, 0, tiled=True)

    partial, wt, xt = forward(place, x, blocks)
    got = lax.all_to_all(partial, ("yh", "x"), 0, 0, tiled=True)
    proj = proj_weight.reshape(4, 2, 128, 256).transpose(1, 0, 2, 3).reshape(1024, 256)
    projected, d_send, proj_part = middle(got, proj, cotangent.reshape(CELLS, 256))
    dpre = lax.all_to_all(d_send, ("yh", "x"), 0, 0, tiled=True)

    core, layer = lax.axis_index("c"), lax.axis_index("z")
    share = halved(proj_part, "c", turn(2, 1), core)
    share = halved(share, "z", BESIDE, gray(layer))
    share = halved(share, "z", ACROSS, layer >> 1)
    share = added_over_y(share)
    dpre, share = lax.optimization_barrier((dpre, share))

    keep, send, dpre = kernel_grad(dpre, xt)
    g_part = add_cores(keep, swap(send, "c"))
    g_got = lax.all_to_all(g_part.reshape(16, 16, COLS), ("z", "yl", "yh"), 0, 0, tiled=True)

    dpre, _ = lax.optimization_barrier((dpre, g_part))
    back = feature_grad(dpre, wt)
    share, _ = lax.optimization_barrier((share, back))
    share = added(share, "x", BESIDE)
    share = added(share, "x", ACROSS)

    g_got, back, share = lax.optimization_barrier((g_got, back, share))
    g_sum = sum_samples(g_got)
    swapped = swap(g_sum, "yl")
    back, swapped = lax.optimization_barrier((back, swapped))
    pair = pack_sums(g_sum, swapped, share)
    pairs = [pair] + [lax.ppermute(pair, "z", turn(4, d)) for d in (1, 2, 3)]
    input_grad = join_features(lax.all_to_all(back, ("yh", "x"), 0, 0, tiled=True))
    half = proj_half(place, pairs)
    grad_point, grad_atrous = place_grads(place, pairs)
    grad_proj = join_proj(place, half, swap(half, "c"))

    return (
        projected.reshape(1, 3, WIDTH, 256),
        input_grad.reshape(1, 3, WIDTH, 2048),
        grad_point,
        grad_atrous,
        grad_proj,
    )


def solution(mesh):
    fine = Mesh(mesh.devices.reshape(4, 2, 2, 4, 2), ("z", "yl", "yh", "x", "c"))
    rep, sp = ("z", "yl"), ("yh", "x", "c")
    in_specs = (
        P(rep, sp, None, None),
        P(None, None, sp),
        P(None, sp),
        P(),
        P(rep, sp, None, None),
    )
    out_specs = (
        P(rep, sp, None, None),
        P(rep, sp, None, None),
        P(sp, None),
        P(None, sp, None),
        P(),
    )
    return jax.shard_map(shards, mesh=fine, in_specs=in_specs, out_specs=out_specs, check_vma=False)
```

```python
import jax
import jax.numpy as jnp
from jax import lax
from jax.experimental import pallas as pl
from jax.experimental.pallas import tpu as pltpu
from jax.sharding import Mesh
from jax.sharding import PartitionSpec as P

DILATIONS = (6, 12, 18)
CHIPS = 8
CELLS = 216
PADDED = 224
WIDTH = 72
HALO = 3
K = 512
TAPS = 28
COLS = TAPS * 128
QUARTER = TAPS // 4
BF16 = jnp.bfloat16
F32 = jnp.float32
VMEM = pl.BlockSpec(memory_space=pltpu.VMEM)
SMEM = pl.BlockSpec(memory_space=pltpu.SMEM)
ANY = pl.BlockSpec(memory_space=pl.ANY)


def tap_of(g, ky, kx):
    return 1 + 9 * g + 3 * (ky + 1) + (kx + 1)


def tap_pairs():
    def tap(g, ky, kx):
        return (tap_of(g, ky, kx), g, ky, kx)

    sides = [[(tap(g, ky, -1), tap(g, ky, 1)) for ky in (0, -1, 1)] for g in range(3)]
    pairs = [((0, -1, 0, 0), tap(0, 0, 0))] + sides[0] + sides[1]
    pairs += [(tap(1, 0, 0), tap(2, 0, 0))]
    pairs += [(tap(0, ky, 0), tap(1, ky, 0)) for ky in (-1, 1)]
    pairs += sides[2] + [(tap(2, -1, 0), tap(2, 1, 0))]
    return pairs


PAIRS = tap_pairs()


def params(mib):
    return pltpu.CompilerParams(vmem_limit_bytes=mib << 20)


def cost(flops, nbytes):
    return pl.CostEstimate(flops=flops, bytes_accessed=nbytes, transcendentals=0)


CONV_COST = cost(2 * 1728 * K * COLS, 8 << 20)


def cell_column(rows):
    row = lax.broadcasted_iota(jnp.int32, (rows, 128), 0)
    return jnp.where(row >= 144, row - 144, jnp.where(row >= 72, row - 72, row))


def split_features_kernel(x, out):
    for col in range(4):
        for yh in range(2):
            part = x[:, (yh * 4 + col) * 256 : (yh * 4 + col + 1) * 256]
            for dest in range(2):
                out[dest * 4 + col, :CELLS, yh * 256 : (yh + 1) * 256] = part
    for chip in range(CHIPS):
        out[chip, CELLS:] = jnp.zeros((PADDED - CELLS, K), BF16)


def split_features(x):
    return pl.pallas_call(
        split_features_kernel,
        out_shape=jax.ShapeDtypeStruct((CHIPS, PADDED, K), BF16),
        in_specs=[VMEM],
        out_specs=VMEM,
        compiler_params=params(16),
        cost_estimate=cost(0, 3 << 20),
    )(x)


def split_weights_kernel(place, point, atrous, out0, out1, out2, out3, taps, sem):
    z, x = place[0], place[1]
    begin = jnp.where(z == 0, 0, QUARTER * z - 1)
    copy = pltpu.make_async_copy(atrous.at[pl.ds(begin, QUARTER)], taps.at[pl.ds(1, QUARTER)], sem)
    copy.start()
    taps[0] = point[...]
    copy.wait()
    first = jnp.where(z == 0, 0, 1)
    for d, out in enumerate((out0, out1, out2, out3)):
        col = lax.rem(x + d, 4)
        for yh in range(2):
            lanes = pl.ds(pl.multiple_of((yh * 4 + col) * 256, 256), 256)
            for t in range(QUARTER):
                out[t, :, yh * 256 : (yh + 1) * 256] = taps[first + t, :, lanes]


def split_weights(place, point, atrous):
    return pl.pallas_call(
        split_weights_kernel,
        out_shape=(jax.ShapeDtypeStruct((QUARTER, 16, K), BF16),) * 4,
        in_specs=[SMEM, VMEM, ANY],
        out_specs=(VMEM,) * 4,
        scratch_shapes=[pltpu.VMEM((QUARTER + 1, 16, 2048), BF16), pltpu.SemaphoreType.DMA],
        compiler_params=params(16),
        cost_estimate=cost(0, 1 << 20),
    )(place, point, atrous)


WEIGHTS = (2, 4, 4, QUARTER, 16, K)


def weights_of(wt, taps):
    rows = []
    for t in taps:
        rows += [wt[c, t // QUARTER, x, t % QUARTER] for x in range(4) for c in range(2)]
    return jnp.concatenate(rows, 0)


def stack_columns_kernel(place, b0, b1, b2, b3, out):
    for d, block in enumerate((b0, b1, b2, b3)):
        out[lax.rem(place[1] + 4 - d, 4)] = block[...]


def stack_columns(place, blocks):
    return pl.pallas_call(
        stack_columns_kernel,
        out_shape=jax.ShapeDtypeStruct((4, QUARTER, 16, K), BF16),
        in_specs=[SMEM] + [VMEM] * 4,
        out_specs=VMEM,
        compiler_params=params(16),
        cost_estimate=cost(0, 1 << 20),
    )(place, *blocks)


def forward_kernel(place, x, *refs):
    blocks, (out, kept, xt, done, acc, out_sem, wt, w_sem, turned, x_sem) = refs[:8], refs[8:]
    for n, block in enumerate(blocks):
        c = place[2] if n < 4 else 1 - place[2]
        wt[c, lax.rem(place[0] + 4 - n % 4, 4)] = block[...]
    keep = pltpu.make_async_copy(wt, kept, w_sem)
    keep.start()
    flat = x[...].reshape(CHIPS * PADDED, K)
    for n in range(7):
        for yh in range(2):
            for core in range(2):
                lane = (yh * 2 + core) * 128
                away = jnp.where(place[2] == core, 0, 1)
                block = flat[n * 256 : (n + 1) * 256, lane : lane + 128]
                turned[2 * away + yh, :, n * 256 : (n + 1) * 256] = block.T
    turn_out = pltpu.make_async_copy(turned, xt, x_sem)
    turn_out.start()

    def span(g, ky):
        return max(0, ky * (g + 1)), CHIPS + min(0, ky * (g + 1))

    for pair in PAIRS:
        begin = min(span(g, ky)[0] for _, g, ky, _ in pair)
        end = max(span(g, ky)[1] for _, g, ky, _ in pair)
        rows = x[begin:end].reshape((end - begin) * PADDED, K)
        right = weights_of(wt, [tap[0] for tap in pair])
        y = lax.dot_general(rows, right, (((1,), (1,)), ((), ())), preferred_element_type=F32)
        y = y.reshape(end - begin, PADDED, 256)
        for half, (_, g, ky, kx) in enumerate(pair):
            which = 3 if g < 0 else (g if kx == 0 else 4 + 2 * g + (kx + 1) // 2)
            lo, hi = span(g, ky)
            part = y[lo - begin : hi - begin, :, half * 128 : (half + 1) * 128]
            to = slice(lo - ky * (g + 1), hi - ky * (g + 1))
            if ky == 0:
                acc[which, to] = part
            else:
                acc[which, to] += part

    column = cell_column(PADDED)

    def finish(j, _):
        parts = [acc[3, j]]
        for g, d in enumerate(DILATIONS):
            minus = pltpu.roll(acc[4 + 2 * g, j], d, 0)
            plus = pltpu.roll(acc[5 + 2 * g, j], PADDED - d, 0)
            parts.append(
                acc[g, j]
                + jnp.where(column >= d, minus, 0.0)
                + jnp.where(column < WIDTH - d, plus, 0.0)
            )
        done[j] = jnp.concatenate(parts, 1).astype(BF16)[:CELLS]
        pltpu.make_async_copy(done.at[j], out.at[j], out_sem.at[j]).start()
        return 0

    lax.fori_loop(0, CHIPS, finish, 0)
    for j in range(CHIPS):
        pltpu.make_async_copy(done.at[j], out.at[j], out_sem.at[j]).wait()
    keep.wait()
    turn_out.wait()


def forward(place, x, blocks):
    return pl.pallas_call(
        forward_kernel,
        out_shape=(
            jax.ShapeDtypeStruct((CHIPS, CELLS, 512), BF16),
            jax.ShapeDtypeStruct(WEIGHTS, BF16),
            jax.ShapeDtypeStruct((4, 128, CHIPS * PADDED), BF16),
        ),
        in_specs=[SMEM] + [VMEM] * 9,
        out_specs=(ANY,) * 3,
        scratch_shapes=[
            pltpu.VMEM((CHIPS, CELLS, 512), BF16),
            pltpu.VMEM((10, CHIPS, PADDED, 128), F32),
            pltpu.SemaphoreType.DMA((CHIPS,)),
            pltpu.VMEM(WEIGHTS, BF16),
            pltpu.SemaphoreType.DMA,
            pltpu.VMEM((4, 128, CHIPS * PADDED), BF16),
            pltpu.SemaphoreType.DMA,
        ],
        compiler_params=params(51),
        cost_estimate=CONV_COST,
    )(place, x, *blocks)


def sigmoid(v):
    return 1.0 / (1.0 + jnp.exp(-v))


def middle_kernel(got, proj, cot, projected, send, grad):
    parts = []
    for yh in range(2):
        total = got[yh * 4].astype(F32)
        for x in range(1, 4):
            total = total + got[yh * 4 + x].astype(F32)
        parts.append(total)
    pre = jnp.concatenate(parts, 1).astype(BF16).astype(F32)
    sig = sigmoid(pre)
    acts = (pre * sig).astype(BF16)
    slope = sig + pre * sig * (1.0 - sig)
    weight = proj[...]
    out_pre = jnp.dot(acts, weight, preferred_element_type=F32)
    osig = sigmoid(out_pre)
    projected[...] = (out_pre * osig).astype(BF16)
    dout = (cot[...].astype(F32) * (osig + out_pre * osig * (1.0 - osig))).astype(BF16)
    dacts = lax.dot_general(
        dout, weight, (((1,), (1,)), ((), ())), preferred_element_type=F32
    )
    dpre = (dacts * slope).astype(BF16)
    for yh in range(2):
        for x in range(4):
            send[yh * 4 + x] = dpre[:, yh * 512 : (yh + 1) * 512]
    grad[...] = lax.dot_general(
        acts, dout, (((0,), (0,)), ((), ())), preferred_element_type=F32
    )


def middle(got, proj, cot):
    return pl.pallas_call(
        middle_kernel,
        out_shape=(
            jax.ShapeDtypeStruct((CELLS, 256), BF16),
            jax.ShapeDtypeStruct((CHIPS, CELLS, 512), BF16),
            jax.ShapeDtypeStruct((1024, 256), F32),
        ),
        in_specs=[VMEM] * 3,
        out_specs=(VMEM,) * 3,
        compiler_params=params(48),
    )(got, proj, cot)


SPREAD = [pltpu.VMEM((9, CHIPS + 2 * HALO, PADDED, 128), BF16), pltpu.VMEM((CHIPS, PADDED, 128), BF16)]


def spread_point(got, point, j):
    point[j, :CELLS] = got[j, :, :128]
    point[j, CELLS:] = jnp.zeros((PADDED - CELLS, 128), BF16)


def spread_branch(got, moved, column, g, j):
    d = DILATIONS[g]
    v = got[j, :, (g + 1) * 128 : (g + 2) * 128]
    wide = v.astype(F32)
    minus = jnp.where(column < WIDTH - d, pltpu.roll(wide, CELLS - d, 0), 0.0)
    plus = jnp.where(column >= d, pltpu.roll(wide, d, 0), 0.0)
    for kx, part in enumerate((minus.astype(BF16), v, plus.astype(BF16))):
        moved[3 * g + kx, HALO + j, :CELLS] = part
        moved[3 * g + kx, HALO + j, CELLS:] = jnp.zeros((PADDED - CELLS, 128), BF16)


def spread_edges(moved, g):
    for n in range(3 * g, 3 * g + 3):
        moved[n, :HALO] = jnp.zeros((HALO, PADDED, 128), BF16)
        moved[n, HALO + CHIPS :] = jnp.zeros((HALO, PADDED, 128), BF16)


def spread(got, moved, point):
    column = cell_column(CELLS)
    for g in range(3):
        spread_edges(moved, g)

    def step(j, _):
        spread_point(got, point, j)
        for g in range(3):
            spread_branch(got, moved, column, g, j)
        return 0

    lax.fori_loop(0, CHIPS, step, 0)


def spread_columns(moved, point, tap, first, count):
    _, g, ky, kx = tap
    if g < 0:
        v = point[pl.ds(first, count)]
    else:
        v = moved[3 * g + kx + 1, pl.ds(HALO + first - ky * (g + 1), count)]
    return v.reshape(count * PADDED, 128)


def kernel_grad_kernel(got, xt, keep, send, again, sent, xs, x_sem, g_sem, out_sem, moved, point):
    load = pltpu.make_async_copy(xt, xs, x_sem)
    load.start()
    copy_got = pltpu.make_async_copy(got, again, g_sem)
    copy_got.start()
    column = cell_column(CELLS)
    stores = []
    ready = -1
    for index, pair in enumerate(PAIRS):
        for g in range(ready + 1, max(tap[1] for tap in pair) + 1):
            spread_edges(moved, g)
            for j in range(CHIPS):
                if g == 0:
                    spread_point(got, point, j)
                spread_branch(got, moved, column, g, j)
            ready = g
        if index == 0:
            load.wait()
        left = xs[...].reshape(K, CHIPS * PADDED)
        right = jnp.concatenate([spread_columns(moved, point, tap, 0, CHIPS) for tap in pair], 1)
        part = jnp.dot(left, right, preferred_element_type=F32).astype(BF16)
        for half, tap in enumerate(pair):
            cols = pl.ds(tap[0] * 128, 128)
            block = part[:, half * 128 : (half + 1) * 128].reshape(2, 2, 8, 16, 128)
            for yh in range(2):
                keep[:, yh, :, cols] = block[0, yh]
                sent[:, yh, :, cols] = block[1, yh]
            view = (slice(None), slice(None), slice(None), cols)
            stores.append(pltpu.make_async_copy(sent.at[view], send.at[view], out_sem.at[tap[0]]))
            stores[-1].start()
    for copy in stores:
        copy.wait()
    copy_got.wait()


def kernel_grad(got, xt):
    return pl.pallas_call(
        kernel_grad_kernel,
        out_shape=(jax.ShapeDtypeStruct((8, 2, 16, COLS), BF16),) * 2
        + (jax.ShapeDtypeStruct((CHIPS, CELLS, 512), BF16),),
        in_specs=[VMEM, ANY],
        out_specs=(VMEM, ANY, ANY),
        scratch_shapes=[
            pltpu.VMEM((8, 2, 16, COLS), BF16),
            pltpu.VMEM((4, 128, CHIPS * PADDED), BF16),
            pltpu.SemaphoreType.DMA,
            pltpu.SemaphoreType.DMA,
            pltpu.SemaphoreType.DMA((TAPS,)),
        ]
        + SPREAD,
        compiler_params=params(48),
        cost_estimate=CONV_COST,
    )(got, xt)


def add_cores_kernel(mine, other, out):
    out[...] = (mine[...].astype(F32) + other[...].astype(F32)).astype(BF16)


def add_cores(mine, other):
    spec = pl.BlockSpec((2, 2, 16, COLS), lambda i: (i, 0, 0, 0))
    return pl.pallas_call(
        add_cores_kernel,
        grid=(4,),
        out_shape=jax.ShapeDtypeStruct((8, 2, 16, COLS), BF16),
        in_specs=[spec] * 2,
        out_specs=spec,
        compiler_params=params(16),
    )(mine, other)


def sum_samples_kernel(got, out):
    for yh in range(2):
        total = got[yh].astype(F32)
        for rep in range(1, 8):
            total = total + got[2 * rep + yh].astype(F32)
        out[yh] = total.astype(BF16)


def sum_samples(got):
    return pl.pallas_call(
        sum_samples_kernel,
        out_shape=jax.ShapeDtypeStruct((2, 16, COLS), BF16),
        in_specs=[VMEM],
        out_specs=VMEM,
        compiler_params=params(24),
    )(got)


def feature_grad_kernel(got, kept, out, moved, point, wt, w_sem):
    load = pltpu.make_async_copy(kept, wt, w_sem)
    load.start()
    spread(got, moved, point)
    load.wait()
    taps = [tap for pair in PAIRS for tap in pair]

    def step(i, _):
        left = jnp.concatenate([spread_columns(moved, point, tap, 2 * i, 2) for tap in taps], 1)
        right = weights_of(wt, [tap[0] for tap in taps])
        part = jnp.dot(left, right, preferred_element_type=F32).astype(BF16)
        for sub in range(2):
            out[2 * i + sub] = part[sub * PADDED : sub * PADDED + CELLS]
        return 0

    lax.fori_loop(0, CHIPS // 2, step, 0)


def feature_grad(got, kept):
    return pl.pallas_call(
        feature_grad_kernel,
        out_shape=jax.ShapeDtypeStruct((CHIPS, CELLS, K), BF16),
        in_specs=[VMEM, ANY],
        out_specs=VMEM,
        scratch_shapes=SPREAD + [pltpu.VMEM(WEIGHTS, BF16), pltpu.SemaphoreType.DMA],
        compiler_params=params(56),
        cost_estimate=CONV_COST,
    )(got, kept)


def pack_sums_kernel(mine, other, proj, out):
    for n, block in enumerate((mine, other)):
        for yh in range(2):
            out[n, yh, :, :COLS] = block[yh]
            for half in range(2):
                row = half * 64 + n * 32 + yh * 16
                lane = COLS + half * 256
                out[n, yh, :, lane : lane + 256] = proj[row : row + 16, :].astype(BF16)


def pack_sums(mine, other, proj):
    return pl.pallas_call(
        pack_sums_kernel,
        out_shape=jax.ShapeDtypeStruct((2, 2, 16, COLS + 512), BF16),
        in_specs=[VMEM] * 3,
        out_specs=VMEM,
        compiler_params=params(16),
    )(mine, other, proj)


def side_of(refs, d, l):
    return refs[2 + l] if d == 2 else refs[(0, 1, 2, 4)[d]].at[l]


def place_grads_kernel(place, *refs):
    point, atrous = refs[5], refs[6]
    z, yl = place[0], place[3]
    for d in range(4):
        for l in range(2):
            rep = 2 * lax.rem(z + 4 - d, 4) + lax.rem(yl + l, 2)
            rows = pl.ds(pl.multiple_of(rep * 16, 16), 16)
            for yh in range(2):
                cols = slice(yh * 128, (yh + 1) * 128)
                for t in range(TAPS):
                    part = side_of(refs, d, l)[yh, :, t * 128 : (t + 1) * 128].astype(F32) * 0.125
                    if t == 0:
                        point[rows, cols] = part
                    else:
                        atrous[t - 1, rows, cols] = part


def place_grads(place, blocks):
    return pl.pallas_call(
        place_grads_kernel,
        out_shape=(
            jax.ShapeDtypeStruct((128, 256), F32),
            jax.ShapeDtypeStruct((27, 128, 256), F32),
        ),
        in_specs=[SMEM] + [VMEM] * 5,
        out_specs=(VMEM,) * 2,
        compiler_params=params(40),
    )(place, *blocks)


def proj_half_kernel(place, *refs):
    out = refs[5]
    for d in range(4):
        z = lax.rem(place[0] + 4 - d, 4)
        row = gray(z) * 256 + (z >> 1) * 128
        for n in range(2):
            for yh in range(2):
                for half in range(2):
                    at = pl.multiple_of(row + half * 64 + n * 32 + yh * 16, 16)
                    lane = COLS + half * 256
                    out[pl.ds(at, 16), :] = side_of(refs, d, n)[yh, :, lane : lane + 256]


def proj_half(place, blocks):
    return pl.pallas_call(
        proj_half_kernel,
        out_shape=jax.ShapeDtypeStruct((512, 256), BF16),
        in_specs=[SMEM] + [VMEM] * 5,
        out_specs=VMEM,
        compiler_params=params(24),
    )(place, *blocks)


def join_proj_kernel(place, mine, other, out):
    c = place[2]
    for half, block in enumerate((mine, other)):
        yh = c if half == 0 else 1 - c
        for branch in range(4):
            part = block[branch * 128 : (branch + 1) * 128, :].astype(F32) * 0.125
            rows = pl.multiple_of(branch * 256 + yh * 128, 128)
            out[pl.ds(rows, 128), :] = part


def join_proj(place, mine, other):
    return pl.pallas_call(
        join_proj_kernel,
        out_shape=jax.ShapeDtypeStruct((1024, 256), F32),
        in_specs=[SMEM, VMEM, VMEM],
        out_specs=VMEM,
        compiler_params=params(16),
    )(place, mine, other)


def join_features_kernel(got, out):
    for x in range(4):
        total = (got[x].astype(F32) + got[4 + x].astype(F32)).astype(BF16)
        for yh in range(2):
            out[:, (yh * 4 + x) * 256 : (yh * 4 + x + 1) * 256] = total[:, yh * 256 : (yh + 1) * 256]


def join_features(got):
    return pl.pallas_call(
        join_features_kernel,
        out_shape=jax.ShapeDtypeStruct((CELLS, 2048), BF16),
        in_specs=[VMEM],
        out_specs=VMEM,
        compiler_params=params(16),
    )(got)


def turn(n, d):
    return [(i, (i + d) % n) for i in range(n)]


def swap(v, axis):
    return lax.ppermute(v, axis, turn(2, 1))


BESIDE = [(i, i ^ 1) for i in range(4)]
ACROSS = [(i, 3 - i) for i in range(4)]


def gray(i):
    return (i ^ (i >> 1)) & 1


def halved(v, axis, pairs, bit):
    half = v.shape[0] // 2
    mine = lax.dynamic_slice_in_dim(v, bit * half, half, 0)
    theirs = lax.dynamic_slice_in_dim(v, (1 - bit) * half, half, 0)
    return mine + lax.ppermute(theirs.astype(BF16), axis, pairs).astype(F32)


def added(v, axis, pairs):
    return v + lax.ppermute(v.astype(BF16), axis, pairs).astype(F32)


def added_over_y(v):
    total, sent = v, v.astype(BF16)
    for l, h in ((0, 1), (1, 0), (1, 1)):
        pairs = [(2 * i + j, 2 * ((i + l) % 2) + (j + h) % 2) for i in range(2) for j in range(2)]
        total = total + lax.ppermute(sent, ("yl", "yh"), pairs).astype(F32)
    return total


def shards(features, atrous_weight, point_weight, proj_weight, cotangent):
    place = jnp.stack([lax.axis_index(a) for a in ("z", "x", "c", "yl", "yh")]).astype(jnp.int32)

    atrous_t = jnp.transpose(atrous_weight, (0, 2, 1))
    parts = split_weights(place, jnp.transpose(point_weight, (1, 0)), atrous_t)
    from_x = [parts[0]] + [lax.ppermute(parts[d], "x", turn(4, d)) for d in (1, 2, 3)]
    quarter = stack_columns(place, from_x)
    quarters = [quarter] + [lax.ppermute(quarter, "z", turn(4, d)) for d in (1, 2, 3)]
    blocks = quarters + [swap(v, "c") for v in quarters]

    x_send = split_features(features.reshape(CELLS, 2048))
    x_send, quarter = lax.optimization_barrier((x_send, quarter))
    x = lax.all_to_all(x_send, ("yh", "x"), 0, 0, tiled=True)

    partial, wt, xt = forward(place, x, blocks)
    got = lax.all_to_all(partial, ("yh", "x"), 0, 0, tiled=True)
    proj = proj_weight.reshape(4, 2, 128, 256).transpose(1, 0, 2, 3).reshape(1024, 256)
    projected, d_send, proj_part = middle(got, proj, cotangent.reshape(CELLS, 256))
    dpre = lax.all_to_all(d_send, ("yh", "x"), 0, 0, tiled=True)

    core, layer = lax.axis_index("c"), lax.axis_index("z")
    share = halved(proj_part, "c", turn(2, 1), core)
    share = halved(share, "z", BESIDE, gray(layer))
    share = halved(share, "z", ACROSS, layer >> 1)
    share = added_over_y(share)
    dpre, share = lax.optimization_barrier((dpre, share))

    keep, send, dpre = kernel_grad(dpre, xt)
    g_part = add_cores(keep, swap(send, "c"))
    g_got = lax.all_to_all(g_part.reshape(16, 16, COLS), ("z", "yl", "yh"), 0, 0, tiled=True)

    dpre, _ = lax.optimization_barrier((dpre, g_part))
    back = feature_grad(dpre, wt)
    share, _ = lax.optimization_barrier((share, back))
    share = added(share, "x", BESIDE)
    share = added(share, "x", ACROSS)

    g_got, back, share = lax.optimization_barrier((g_got, back, share))
    g_sum = sum_samples(g_got)
    swapped = swap(g_sum, "yl")
    back, swapped = lax.optimization_barrier((back, swapped))
    pair = pack_sums(g_sum, swapped, share)
    below, above = lax.ppermute(pair, "z", turn(4, 1)), lax.ppermute(pair, "z", turn(4, 3))
    opposite = [lax.ppermute(above[0], "z", turn(4, 3)), lax.ppermute(below[1], "z", turn(4, 1))]
    pairs = [pair, below, *opposite, above]
    input_grad = join_features(lax.all_to_all(back, ("yh", "x"), 0, 0, tiled=True))
    half = proj_half(place, pairs)
    grad_point, grad_atrous = place_grads(place, pairs)
    grad_proj = join_proj(place, half, swap(half, "c"))

    return (
        projected.reshape(1, 3, WIDTH, 256),
        input_grad.reshape(1, 3, WIDTH, 2048),
        grad_point,
        grad_atrous,
        grad_proj,
    )


def solution(mesh):
    fine = Mesh(mesh.devices.reshape(4, 2, 2, 4, 2), ("z", "yl", "yh", "x", "c"))
    rep, sp = ("z", "yl"), ("yh", "x", "c")
    in_specs = (
        P(rep, sp, None, None),
        P(None, None, sp),
        P(None, sp),
        P(),
        P(rep, sp, None, None),
    )
    out_specs = (
        P(rep, sp, None, None),
        P(rep, sp, None, None),
        P(sp, None),
        P(None, sp, None),
        P(),
    )
    return jax.shard_map(shards, mesh=fine, in_specs=in_specs, out_specs=out_specs, check_vma=False)
```

```python
import jax
import jax.numpy as jnp
from jax import lax
from jax.experimental import pallas as pl
from jax.experimental.pallas import tpu as pltpu
from jax.sharding import Mesh
from jax.sharding import PartitionSpec as P

DILATIONS = (6, 12, 18)
CHIPS = 8
CELLS = 216
PADDED = 224
WIDTH = 72
HALO = 3
K = 512
TAPS = 28
COLS = TAPS * 128
QUARTER = TAPS // 4
BF16 = jnp.bfloat16
F32 = jnp.float32
VMEM = pl.BlockSpec(memory_space=pltpu.VMEM)
SMEM = pl.BlockSpec(memory_space=pltpu.SMEM)
ANY = pl.BlockSpec(memory_space=pl.ANY)


def tap_of(g, ky, kx):
    return 1 + 9 * g + 3 * (ky + 1) + (kx + 1)


def tap_pairs():
    def tap(g, ky, kx):
        return (tap_of(g, ky, kx), g, ky, kx)

    sides = [[(tap(g, ky, -1), tap(g, ky, 1)) for ky in (0, -1, 1)] for g in range(3)]
    pairs = [((0, -1, 0, 0), tap(0, 0, 0))] + sides[0] + sides[1]
    pairs += [(tap(1, 0, 0), tap(2, 0, 0))]
    pairs += [(tap(0, ky, 0), tap(1, ky, 0)) for ky in (-1, 1)]
    pairs += sides[2] + [(tap(2, -1, 0), tap(2, 1, 0))]
    return pairs


PAIRS = tap_pairs()


def params(mib):
    return pltpu.CompilerParams(vmem_limit_bytes=mib << 20)


def cost(flops, nbytes):
    return pl.CostEstimate(flops=flops, bytes_accessed=nbytes, transcendentals=0)


CONV_COST = cost(2 * 1728 * K * COLS, 8 << 20)


def cell_column(rows):
    row = lax.broadcasted_iota(jnp.int32, (rows, 128), 0)
    return jnp.where(row >= 144, row - 144, jnp.where(row >= 72, row - 72, row))


def split_features_kernel(x, out):
    for col in range(4):
        for yh in range(2):
            part = x[:, (yh * 4 + col) * 256 : (yh * 4 + col + 1) * 256]
            for dest in range(2):
                out[dest * 4 + col, :CELLS, yh * 256 : (yh + 1) * 256] = part
    for chip in range(CHIPS):
        out[chip, CELLS:] = jnp.zeros((PADDED - CELLS, K), BF16)


def split_features(x):
    return pl.pallas_call(
        split_features_kernel,
        out_shape=jax.ShapeDtypeStruct((CHIPS, PADDED, K), BF16),
        in_specs=[VMEM],
        out_specs=VMEM,
        compiler_params=params(16),
        cost_estimate=cost(0, 3 << 20),
    )(x)


def split_weights_kernel(place, taps, out0, out1, out2, out3):
    for d, out in enumerate((out0, out1, out2, out3)):
        col = lax.rem(place[1] + d, 4)
        for yh in range(2):
            lanes = pl.ds(pl.multiple_of((yh * 4 + col) * 256, 256), 256)
            for t in range(QUARTER):
                out[t, :, yh * 256 : (yh + 1) * 256] = taps[t, :, lanes]


def split_weights(place, taps):
    return pl.pallas_call(
        split_weights_kernel,
        out_shape=(jax.ShapeDtypeStruct((QUARTER, 16, K), BF16),) * 4,
        in_specs=[SMEM, VMEM],
        out_specs=(VMEM,) * 4,
        compiler_params=params(16),
        cost_estimate=cost(0, 1 << 20),
    )(place, taps)


WEIGHTS = (2, 4, 4, QUARTER, 16, K)


def weights_of(wt, taps):
    rows = []
    for t in taps:
        rows += [wt[c, t // QUARTER, x, t % QUARTER] for x in range(4) for c in range(2)]
    return jnp.concatenate(rows, 0)


def stack_columns_kernel(place, b0, b1, b2, b3, out):
    for d, block in enumerate((b0, b1, b2, b3)):
        out[lax.rem(place[1] + 4 - d, 4)] = block[...]


def stack_columns(place, blocks):
    return pl.pallas_call(
        stack_columns_kernel,
        out_shape=jax.ShapeDtypeStruct((4, QUARTER, 16, K), BF16),
        in_specs=[SMEM] + [VMEM] * 4,
        out_specs=VMEM,
        compiler_params=params(16),
        cost_estimate=cost(0, 1 << 20),
    )(place, *blocks)


def forward_kernel(place, x, *refs):
    blocks, (out, kept, xt, done, acc, out_sem, wt, w_sem, turned, x_sem) = refs[:10], refs[10:]
    for n, block in enumerate(blocks):
        c = place[2] if n < 5 else 1 - place[2]
        d, begin = ((0, 0), (1, 0), (2, 0), (2, 2), (3, 0))[n % 5]
        wt[c, lax.rem(place[0] + 4 - d, 4), begin : begin + block.shape[0]] = block[...]
    keep = pltpu.make_async_copy(wt, kept, w_sem)
    keep.start()
    flat = x[...].reshape(CHIPS * PADDED, K)
    for n in range(7):
        for yh in range(2):
            for core in range(2):
                lane = (yh * 2 + core) * 128
                away = jnp.where(place[2] == core, 0, 1)
                block = flat[n * 256 : (n + 1) * 256, lane : lane + 128]
                turned[2 * away + yh, :, n * 256 : (n + 1) * 256] = block.T
    turn_out = pltpu.make_async_copy(turned, xt, x_sem)
    turn_out.start()

    def span(g, ky):
        return max(0, ky * (g + 1)), CHIPS + min(0, ky * (g + 1))

    for pair in PAIRS:
        begin = min(span(g, ky)[0] for _, g, ky, _ in pair)
        end = max(span(g, ky)[1] for _, g, ky, _ in pair)
        rows = x[begin:end].reshape((end - begin) * PADDED, K)
        right = weights_of(wt, [tap[0] for tap in pair])
        y = lax.dot_general(rows, right, (((1,), (1,)), ((), ())), preferred_element_type=F32)
        y = y.reshape(end - begin, PADDED, 256)
        for half, (_, g, ky, kx) in enumerate(pair):
            which = 3 if g < 0 else (g if kx == 0 else 4 + 2 * g + (kx + 1) // 2)
            lo, hi = span(g, ky)
            part = y[lo - begin : hi - begin, :, half * 128 : (half + 1) * 128]
            to = slice(lo - ky * (g + 1), hi - ky * (g + 1))
            if ky == 0:
                acc[which, to] = part
            else:
                acc[which, to] += part

    column = cell_column(PADDED)

    def finish(j, _):
        parts = [acc[3, j]]
        for g, d in enumerate(DILATIONS):
            minus = pltpu.roll(acc[4 + 2 * g, j], d, 0)
            plus = pltpu.roll(acc[5 + 2 * g, j], PADDED - d, 0)
            parts.append(
                acc[g, j]
                + jnp.where(column >= d, minus, 0.0)
                + jnp.where(column < WIDTH - d, plus, 0.0)
            )
        done[j] = jnp.concatenate(parts, 1).astype(BF16)[:CELLS]
        pltpu.make_async_copy(done.at[j], out.at[j], out_sem.at[j]).start()
        return 0

    lax.fori_loop(0, CHIPS, finish, 0)
    for j in range(CHIPS):
        pltpu.make_async_copy(done.at[j], out.at[j], out_sem.at[j]).wait()
    keep.wait()
    turn_out.wait()


def forward(place, x, blocks):
    return pl.pallas_call(
        forward_kernel,
        out_shape=(
            jax.ShapeDtypeStruct((CHIPS, CELLS, 512), BF16),
            jax.ShapeDtypeStruct(WEIGHTS, BF16),
            jax.ShapeDtypeStruct((4, 128, CHIPS * PADDED), BF16),
        ),
        in_specs=[SMEM] + [VMEM] * 11,
        out_specs=(ANY,) * 3,
        scratch_shapes=[
            pltpu.VMEM((CHIPS, CELLS, 512), BF16),
            pltpu.VMEM((10, CHIPS, PADDED, 128), F32),
            pltpu.SemaphoreType.DMA((CHIPS,)),
            pltpu.VMEM(WEIGHTS, BF16),
            pltpu.SemaphoreType.DMA,
            pltpu.VMEM((4, 128, CHIPS * PADDED), BF16),
            pltpu.SemaphoreType.DMA,
        ],
        compiler_params=params(51),
        cost_estimate=CONV_COST,
    )(place, x, *blocks)


def sigmoid(v):
    return 1.0 / (1.0 + jnp.exp(-v))


def middle_kernel(got, proj, cot, projected, send, grad):
    parts = []
    for yh in range(2):
        total = got[yh * 4].astype(F32)
        for x in range(1, 4):
            total = total + got[yh * 4 + x].astype(F32)
        parts.append(total)
    pre = jnp.concatenate(parts, 1).astype(BF16).astype(F32)
    sig = sigmoid(pre)
    acts = (pre * sig).astype(BF16)
    slope = sig + pre * sig * (1.0 - sig)
    weight = proj[...]
    out_pre = jnp.dot(acts, weight, preferred_element_type=F32)
    osig = sigmoid(out_pre)
    projected[...] = (out_pre * osig).astype(BF16)
    dout = (cot[...].astype(F32) * (osig + out_pre * osig * (1.0 - osig))).astype(BF16)
    dacts = lax.dot_general(
        dout, weight, (((1,), (1,)), ((), ())), preferred_element_type=F32
    )
    dpre = (dacts * slope).astype(BF16)
    for yh in range(2):
        for x in range(4):
            send[yh * 4 + x] = dpre[:, yh * 512 : (yh + 1) * 512]
    grad[...] = lax.dot_general(
        acts, dout, (((0,), (0,)), ((), ())), preferred_element_type=F32
    )


def middle(got, proj, cot):
    return pl.pallas_call(
        middle_kernel,
        out_shape=(
            jax.ShapeDtypeStruct((CELLS, 256), BF16),
            jax.ShapeDtypeStruct((CHIPS, CELLS, 512), BF16),
            jax.ShapeDtypeStruct((1024, 256), F32),
        ),
        in_specs=[VMEM] * 3,
        out_specs=(VMEM,) * 3,
        compiler_params=params(48),
    )(got, proj, cot)


SPREAD = [pltpu.VMEM((9, CHIPS + 2 * HALO, PADDED, 128), BF16), pltpu.VMEM((CHIPS, PADDED, 128), BF16)]


def spread_point(got, point, j):
    point[j, :CELLS] = got[j, :, :128]
    point[j, CELLS:] = jnp.zeros((PADDED - CELLS, 128), BF16)


def spread_branch(got, moved, column, g, j):
    d = DILATIONS[g]
    v = got[j, :, (g + 1) * 128 : (g + 2) * 128]
    wide = v.astype(F32)
    minus = jnp.where(column < WIDTH - d, pltpu.roll(wide, CELLS - d, 0), 0.0)
    plus = jnp.where(column >= d, pltpu.roll(wide, d, 0), 0.0)
    for kx, part in enumerate((minus.astype(BF16), v, plus.astype(BF16))):
        moved[3 * g + kx, HALO + j, :CELLS] = part
        moved[3 * g + kx, HALO + j, CELLS:] = jnp.zeros((PADDED - CELLS, 128), BF16)


def spread_edges(moved, g):
    for n in range(3 * g, 3 * g + 3):
        moved[n, :HALO] = jnp.zeros((HALO, PADDED, 128), BF16)
        moved[n, HALO + CHIPS :] = jnp.zeros((HALO, PADDED, 128), BF16)


def spread(got, moved, point):
    column = cell_column(CELLS)
    for g in range(3):
        spread_edges(moved, g)

    def step(j, _):
        spread_point(got, point, j)
        for g in range(3):
            spread_branch(got, moved, column, g, j)
        return 0

    lax.fori_loop(0, CHIPS, step, 0)


def spread_columns(moved, point, tap, first, count):
    _, g, ky, kx = tap
    if g < 0:
        v = point[pl.ds(first, count)]
    else:
        v = moved[3 * g + kx + 1, pl.ds(HALO + first - ky * (g + 1), count)]
    return v.reshape(count * PADDED, 128)


def kernel_grad_kernel(got, xt, keep, send, again, sent, xs, x_sem, g_sem, out_sem, moved, point):
    load = pltpu.make_async_copy(xt, xs, x_sem)
    load.start()
    copy_got = pltpu.make_async_copy(got, again, g_sem)
    copy_got.start()
    column = cell_column(CELLS)
    stores = []
    ready = -1
    for index, pair in enumerate(PAIRS):
        for g in range(ready + 1, max(tap[1] for tap in pair) + 1):
            spread_edges(moved, g)
            for j in range(CHIPS):
                if g == 0:
                    spread_point(got, point, j)
                spread_branch(got, moved, column, g, j)
            ready = g
        if index == 0:
            load.wait()
        left = xs[...].reshape(K, CHIPS * PADDED)
        right = jnp.concatenate([spread_columns(moved, point, tap, 0, CHIPS) for tap in pair], 1)
        part = jnp.dot(left, right, preferred_element_type=F32).astype(BF16)
        for half, tap in enumerate(pair):
            cols = pl.ds(tap[0] * 128, 128)
            block = part[:, half * 128 : (half + 1) * 128].reshape(2, 2, 8, 16, 128)
            for yh in range(2):
                keep[:, yh, :, cols] = block[0, yh]
                sent[:, yh, :, cols] = block[1, yh]
            view = (slice(None), slice(None), slice(None), cols)
            stores.append(pltpu.make_async_copy(sent.at[view], send.at[view], out_sem.at[tap[0]]))
            stores[-1].start()
    for copy in stores:
        copy.wait()
    copy_got.wait()


def kernel_grad(got, xt):
    return pl.pallas_call(
        kernel_grad_kernel,
        out_shape=(jax.ShapeDtypeStruct((8, 2, 16, COLS), BF16),) * 2
        + (jax.ShapeDtypeStruct((CHIPS, CELLS, 512), BF16),),
        in_specs=[VMEM, ANY],
        out_specs=(VMEM, ANY, ANY),
        scratch_shapes=[
            pltpu.VMEM((8, 2, 16, COLS), BF16),
            pltpu.VMEM((4, 128, CHIPS * PADDED), BF16),
            pltpu.SemaphoreType.DMA,
            pltpu.SemaphoreType.DMA,
            pltpu.SemaphoreType.DMA((TAPS,)),
        ]
        + SPREAD,
        compiler_params=params(48),
        cost_estimate=CONV_COST,
    )(got, xt)


def add_cores_kernel(mine, other, out):
    out[...] = (mine[...].astype(F32) + other[...].astype(F32)).astype(BF16)


def add_cores(mine, other):
    spec = pl.BlockSpec((2, 2, 16, COLS), lambda i: (i, 0, 0, 0))
    return pl.pallas_call(
        add_cores_kernel,
        grid=(4,),
        out_shape=jax.ShapeDtypeStruct((8, 2, 16, COLS), BF16),
        in_specs=[spec] * 2,
        out_specs=spec,
        compiler_params=params(16),
    )(mine, other)


def sum_samples_kernel(got, out):
    for yh in range(2):
        total = got[yh].astype(F32)
        for rep in range(1, 8):
            total = total + got[2 * rep + yh].astype(F32)
        out[yh] = total.astype(BF16)


def sum_samples(got):
    return pl.pallas_call(
        sum_samples_kernel,
        out_shape=jax.ShapeDtypeStruct((2, 16, COLS), BF16),
        in_specs=[VMEM],
        out_specs=VMEM,
        compiler_params=params(24),
    )(got)


def feature_grad_kernel(got, kept, out, moved, point, wt, w_sem):
    load = pltpu.make_async_copy(kept, wt, w_sem)
    load.start()
    spread(got, moved, point)
    load.wait()
    taps = [tap for pair in PAIRS for tap in pair]

    def step(i, _):
        left = jnp.concatenate([spread_columns(moved, point, tap, 2 * i, 2) for tap in taps], 1)
        right = weights_of(wt, [tap[0] for tap in taps])
        part = jnp.dot(left, right, preferred_element_type=F32).astype(BF16)
        for sub in range(2):
            out[2 * i + sub] = part[sub * PADDED : sub * PADDED + CELLS]
        return 0

    lax.fori_loop(0, CHIPS // 2, step, 0)


def feature_grad(got, kept):
    return pl.pallas_call(
        feature_grad_kernel,
        out_shape=jax.ShapeDtypeStruct((CHIPS, CELLS, K), BF16),
        in_specs=[VMEM, ANY],
        out_specs=VMEM,
        scratch_shapes=SPREAD + [pltpu.VMEM(WEIGHTS, BF16), pltpu.SemaphoreType.DMA],
        compiler_params=params(56),
        cost_estimate=CONV_COST,
    )(got, kept)


def pack_sums_kernel(mine, other, proj, out):
    for n, block in enumerate((mine, other)):
        for yh in range(2):
            out[n, yh, :, :COLS] = block[yh]
            for half in range(2):
                row = half * 64 + n * 32 + yh * 16
                lane = COLS + half * 256
                out[n, yh, :, lane : lane + 256] = proj[row : row + 16, :].astype(BF16)


def pack_sums(mine, other, proj):
    return pl.pallas_call(
        pack_sums_kernel,
        out_shape=jax.ShapeDtypeStruct((2, 2, 16, COLS + 512), BF16),
        in_specs=[VMEM] * 3,
        out_specs=VMEM,
        compiler_params=params(16),
    )(mine, other, proj)


def side_of(refs, d, l):
    return refs[2 + l] if d == 2 else refs[(0, 1, 2, 4)[d]].at[l]


def place_grads_kernel(place, *refs):
    point, atrous = refs[5], refs[6]
    z, yl = place[0], place[3]
    for d in range(4):
        for l in range(2):
            rep = 2 * lax.rem(z + 4 - d, 4) + lax.rem(yl + l, 2)
            rows = pl.ds(pl.multiple_of(rep * 16, 16), 16)
            for yh in range(2):
                cols = slice(yh * 128, (yh + 1) * 128)
                for t in range(TAPS):
                    part = side_of(refs, d, l)[yh, :, t * 128 : (t + 1) * 128].astype(F32) * 0.125
                    if t == 0:
                        point[rows, cols] = part
                    else:
                        atrous[t - 1, rows, cols] = part


def place_grads(place, blocks):
    return pl.pallas_call(
        place_grads_kernel,
        out_shape=(
            jax.ShapeDtypeStruct((128, 256), F32),
            jax.ShapeDtypeStruct((27, 128, 256), F32),
        ),
        in_specs=[SMEM] + [VMEM] * 5,
        out_specs=(VMEM,) * 2,
        compiler_params=params(40),
    )(place, *blocks)


def proj_half_kernel(place, *refs):
    out = refs[5]
    for d in range(4):
        z = lax.rem(place[0] + 4 - d, 4)
        row = gray(z) * 256 + (z >> 1) * 128
        for n in range(2):
            for yh in range(2):
                for half in range(2):
                    at = pl.multiple_of(row + half * 64 + n * 32 + yh * 16, 16)
                    lane = COLS + half * 256
                    out[pl.ds(at, 16), :] = side_of(refs, d, n)[yh, :, lane : lane + 256]


def proj_half(place, blocks):
    return pl.pallas_call(
        proj_half_kernel,
        out_shape=jax.ShapeDtypeStruct((512, 256), BF16),
        in_specs=[SMEM] + [VMEM] * 5,
        out_specs=VMEM,
        compiler_params=params(24),
    )(place, *blocks)


def join_proj_kernel(place, mine, other, out):
    c = place[2]
    for half, block in enumerate((mine, other)):
        yh = c if half == 0 else 1 - c
        for branch in range(4):
            part = block[branch * 128 : (branch + 1) * 128, :].astype(F32) * 0.125
            rows = pl.multiple_of(branch * 256 + yh * 128, 128)
            out[pl.ds(rows, 128), :] = part


def join_proj(place, mine, other):
    return pl.pallas_call(
        join_proj_kernel,
        out_shape=jax.ShapeDtypeStruct((1024, 256), F32),
        in_specs=[SMEM, VMEM, VMEM],
        out_specs=VMEM,
        compiler_params=params(16),
    )(place, mine, other)


def join_features_kernel(got, out):
    for x in range(4):
        total = (got[x].astype(F32) + got[4 + x].astype(F32)).astype(BF16)
        for yh in range(2):
            out[:, (yh * 4 + x) * 256 : (yh * 4 + x + 1) * 256] = total[:, yh * 256 : (yh + 1) * 256]


def join_features(got):
    return pl.pallas_call(
        join_features_kernel,
        out_shape=jax.ShapeDtypeStruct((CELLS, 2048), BF16),
        in_specs=[VMEM],
        out_specs=VMEM,
        compiler_params=params(16),
    )(got)


def turn(n, d):
    return [(i, (i + d) % n) for i in range(n)]


def swap(v, axis):
    return lax.ppermute(v, axis, turn(2, 1))


BESIDE = [(i, i ^ 1) for i in range(4)]
ACROSS = [(i, 3 - i) for i in range(4)]


def gray(i):
    return (i ^ (i >> 1)) & 1


def halved(v, axis, pairs, bit):
    half = v.shape[0] // 2
    mine = lax.dynamic_slice_in_dim(v, bit * half, half, 0)
    theirs = lax.dynamic_slice_in_dim(v, (1 - bit) * half, half, 0)
    return mine + lax.ppermute(theirs.astype(BF16), axis, pairs).astype(F32)


def added(v, axis, pairs):
    return v + lax.ppermute(v.astype(BF16), axis, pairs).astype(F32)


def shards(features, atrous_weight, point_weight, proj_weight, cotangent):
    place = jnp.stack([lax.axis_index(a) for a in ("z", "x", "c", "yl", "yh")]).astype(jnp.int32)

    atrous_t = jnp.transpose(atrous_weight, (0, 2, 1))
    z = lax.axis_index("z")
    taps = lax.dynamic_slice_in_dim(atrous_t, jnp.maximum(QUARTER * z - 1, 0), QUARTER, 0)
    with_point = jnp.concatenate([jnp.transpose(point_weight, (1, 0))[None], taps[: QUARTER - 1]], 0)
    parts = split_weights(place, jnp.where(z == 0, with_point, taps))
    from_x = [parts[0]] + [lax.ppermute(parts[d], "x", turn(4, d)) for d in (1, 2, 3)]
    quarter = stack_columns(place, from_x)
    below, above = (lax.ppermute(quarter, "z", turn(4, d)) for d in (1, 3))
    opposite = [lax.ppermute(above[:2], "z", turn(4, 3)), lax.ppermute(below[2:], "z", turn(4, 1))]
    quarters = [quarter, below, *opposite, above]
    blocks = quarters + [swap(v, "c") for v in quarters]

    x_send = split_features(features.reshape(CELLS, 2048))
    x_send, quarter = lax.optimization_barrier((x_send, quarter))
    x = lax.all_to_all(x_send, ("yh", "x"), 0, 0, tiled=True)

    partial, wt, xt = forward(place, x, blocks)
    got = lax.all_to_all(partial, ("yh", "x"), 0, 0, tiled=True)
    proj = proj_weight.reshape(4, 2, 128, 256).transpose(1, 0, 2, 3).reshape(1024, 256)
    projected, d_send, proj_part = middle(got, proj, cotangent.reshape(CELLS, 256))
    dpre = lax.all_to_all(d_send, ("yh", "x"), 0, 0, tiled=True)

    core, layer = lax.axis_index("c"), lax.axis_index("z")
    share = halved(proj_part, "c", turn(2, 1), core)
    share = halved(share, "z", BESIDE, gray(layer))
    share = halved(share, "z", ACROSS, layer >> 1)
    dpre, share = lax.optimization_barrier((dpre, share))
    share = added(share, "yh", turn(2, 1))

    keep, send, dpre = kernel_grad(dpre, xt)
    send, share = lax.optimization_barrier((send, share))
    other = swap(send, "c")
    share = added(share, "yl", turn(2, 1))
    other, share = lax.optimization_barrier((other, share))
    g_part = add_cores(keep, other)
    g_got = lax.all_to_all(g_part.reshape(16, 16, COLS), ("z", "yl", "yh"), 0, 0, tiled=True)

    dpre, _ = lax.optimization_barrier((dpre, g_part))
    back = feature_grad(dpre, wt)
    share, _ = lax.optimization_barrier((share, back))
    share = added(share, "x", BESIDE)
    share = added(share, "x", ACROSS)

    g_got, back, share = lax.optimization_barrier((g_got, back, share))
    g_sum = sum_samples(g_got)
    swapped = swap(g_sum, "yl")
    back, swapped = lax.optimization_barrier((back, swapped))
    pair = pack_sums(g_sum, swapped, share)
    below, above = lax.ppermute(pair, "z", turn(4, 1)), lax.ppermute(pair, "z", turn(4, 3))
    opposite = [lax.ppermute(above[0], "z", turn(4, 3)), lax.ppermute(below[1], "z", turn(4, 1))]
    pairs = [pair, below, *opposite, above]
    input_grad = join_features(lax.all_to_all(back, ("yh", "x"), 0, 0, tiled=True))
    half = proj_half(place, pairs)
    grad_point, grad_atrous = place_grads(place, pairs)
    grad_proj = join_proj(place, half, swap(half, "c"))

    return (
        projected.reshape(1, 3, WIDTH, 256),
        input_grad.reshape(1, 3, WIDTH, 2048),
        grad_point,
        grad_atrous,
        grad_proj,
    )


def solution(mesh):
    fine = Mesh(mesh.devices.reshape(4, 2, 2, 4, 2), ("z", "yl", "yh", "x", "c"))
    rep, sp = ("z", "yl"), ("yh", "x", "c")
    in_specs = (
        P(rep, sp, None, None),
        P(None, None, sp),
        P(None, sp),
        P(),
        P(rep, sp, None, None),
    )
    out_specs = (
        P(rep, sp, None, None),
        P(rep, sp, None, None),
        P(sp, None),
        P(None, sp, None),
        P(),
    )
    return jax.shard_map(shards, mesh=fine, in_specs=in_specs, out_specs=out_specs, check_vma=False)
```

```python
import jax
import jax.numpy as jnp
from jax import lax
from jax.experimental import pallas as pl
from jax.experimental.pallas import tpu as pltpu
from jax.sharding import Mesh
from jax.sharding import PartitionSpec as P

DILATIONS = (6, 12, 18)
CHIPS = 8
CELLS = 216
PADDED = 224
WIDTH = 72
HALO = 3
K = 512
TAPS = 28
COLS = TAPS * 128
QUARTER = TAPS // 4
BF16 = jnp.bfloat16
F32 = jnp.float32
VMEM = pl.BlockSpec(memory_space=pltpu.VMEM)
SMEM = pl.BlockSpec(memory_space=pltpu.SMEM)
ANY = pl.BlockSpec(memory_space=pl.ANY)


def tap_of(g, ky, kx):
    return 1 + 9 * g + 3 * (ky + 1) + (kx + 1)


def tap_pairs():
    def tap(g, ky, kx):
        return (tap_of(g, ky, kx), g, ky, kx)

    sides = [[(tap(g, ky, -1), tap(g, ky, 1)) for ky in (0, -1, 1)] for g in range(3)]
    pairs = [((0, -1, 0, 0), tap(0, 0, 0))] + sides[0] + sides[1]
    pairs += [(tap(1, 0, 0), tap(2, 0, 0))]
    pairs += [(tap(0, ky, 0), tap(1, ky, 0)) for ky in (-1, 1)]
    pairs += sides[2] + [(tap(2, -1, 0), tap(2, 1, 0))]
    return pairs


PAIRS = tap_pairs()


def params(mib):
    return pltpu.CompilerParams(vmem_limit_bytes=mib << 20)


def cost(flops, nbytes):
    return pl.CostEstimate(flops=flops, bytes_accessed=nbytes, transcendentals=0)


CONV_COST = cost(2 * 1728 * K * COLS, 8 << 20)


def cell_column(rows):
    row = lax.broadcasted_iota(jnp.int32, (rows, 128), 0)
    return jnp.where(row >= 144, row - 144, jnp.where(row >= 72, row - 72, row))


def split_features_kernel(x, out):
    for col in range(4):
        for yh in range(2):
            part = x[:, (yh * 4 + col) * 256 : (yh * 4 + col + 1) * 256]
            for dest in range(2):
                out[dest * 4 + col, :CELLS, yh * 256 : (yh + 1) * 256] = part
    for chip in range(CHIPS):
        out[chip, CELLS:] = jnp.zeros((PADDED - CELLS, K), BF16)


def split_features(x):
    return pl.pallas_call(
        split_features_kernel,
        out_shape=jax.ShapeDtypeStruct((CHIPS, PADDED, K), BF16),
        in_specs=[VMEM],
        out_specs=VMEM,
        compiler_params=params(16),
        cost_estimate=cost(0, 3 << 20),
    )(x)


def split_weights_kernel(place, taps, out0, out1, out2, out3):
    for d, out in enumerate((out0, out1, out2, out3)):
        col = lax.rem(place[1] + d, 4)
        for yh in range(2):
            lanes = pl.ds(pl.multiple_of((yh * 4 + col) * 256, 256), 256)
            for t in range(QUARTER):
                out[t, :, yh * 256 : (yh + 1) * 256] = taps[t, :, lanes]


def split_weights(place, taps):
    return pl.pallas_call(
        split_weights_kernel,
        out_shape=(jax.ShapeDtypeStruct((QUARTER, 16, K), BF16),) * 4,
        in_specs=[SMEM, VMEM],
        out_specs=(VMEM,) * 4,
        compiler_params=params(16),
        cost_estimate=cost(0, 1 << 20),
    )(place, taps)


WEIGHTS = (2, 4, 4, QUARTER, 16, K)


def weights_of(wt, taps):
    rows = []
    for t in taps:
        rows += [wt[c, t // QUARTER, x, t % QUARTER] for x in range(4) for c in range(2)]
    return jnp.concatenate(rows, 0)


def stack_columns_kernel(place, b0, b1, b2, b3, out):
    for d, block in enumerate((b0, b1, b2, b3)):
        out[lax.rem(place[1] + 4 - d, 4)] = block[...]


def stack_columns(place, blocks):
    return pl.pallas_call(
        stack_columns_kernel,
        out_shape=jax.ShapeDtypeStruct((4, QUARTER, 16, K), BF16),
        in_specs=[SMEM] + [VMEM] * 4,
        out_specs=VMEM,
        compiler_params=params(16),
        cost_estimate=cost(0, 1 << 20),
    )(place, *blocks)


def forward_kernel(place, x, *refs):
    blocks, (out, kept, xt, done, acc, out_sem, wt, w_sem, turned, x_sem) = refs[:10], refs[10:]
    for n, block in enumerate(blocks):
        c = place[2] if n < 5 else 1 - place[2]
        d, begin = ((0, 0), (1, 0), (2, 0), (2, 2), (3, 0))[n % 5]
        wt[c, lax.rem(place[0] + 4 - d, 4), begin : begin + block.shape[0]] = block[...]
    keep = pltpu.make_async_copy(wt, kept, w_sem)
    keep.start()
    flat = x[...].reshape(CHIPS * PADDED, K)
    for n in range(7):
        for yh in range(2):
            for core in range(2):
                lane = (yh * 2 + core) * 128
                away = jnp.where(place[2] == core, 0, 1)
                block = flat[n * 256 : (n + 1) * 256, lane : lane + 128]
                turned[2 * away + yh, :, n * 256 : (n + 1) * 256] = block.T
    turn_out = pltpu.make_async_copy(turned, xt, x_sem)
    turn_out.start()

    def span(g, ky):
        return max(0, ky * (g + 1)), CHIPS + min(0, ky * (g + 1))

    for pair in PAIRS:
        begin = min(span(g, ky)[0] for _, g, ky, _ in pair)
        end = max(span(g, ky)[1] for _, g, ky, _ in pair)
        rows = x[begin:end].reshape((end - begin) * PADDED, K)
        right = weights_of(wt, [tap[0] for tap in pair])
        y = lax.dot_general(rows, right, (((1,), (1,)), ((), ())), preferred_element_type=F32)
        y = y.reshape(end - begin, PADDED, 256)
        for half, (_, g, ky, kx) in enumerate(pair):
            which = 3 if g < 0 else (g if kx == 0 else 4 + 2 * g + (kx + 1) // 2)
            lo, hi = span(g, ky)
            part = y[lo - begin : hi - begin, :, half * 128 : (half + 1) * 128]
            to = slice(lo - ky * (g + 1), hi - ky * (g + 1))
            if ky == 0:
                acc[which, to] = part
            else:
                acc[which, to] += part

    column = cell_column(PADDED)

    def finish(j, _):
        parts = [acc[3, j]]
        for g, d in enumerate(DILATIONS):
            minus = pltpu.roll(acc[4 + 2 * g, j], d, 0)
            plus = pltpu.roll(acc[5 + 2 * g, j], PADDED - d, 0)
            parts.append(
                acc[g, j]
                + jnp.where(column >= d, minus, 0.0)
                + jnp.where(column < WIDTH - d, plus, 0.0)
            )
        done[j] = jnp.concatenate(parts, 1).astype(BF16)
        pltpu.make_async_copy(done.at[j], out.at[j], out_sem.at[j]).start()
        return 0

    lax.fori_loop(0, CHIPS, finish, 0)
    for j in range(CHIPS):
        pltpu.make_async_copy(done.at[j], out.at[j], out_sem.at[j]).wait()
    keep.wait()
    turn_out.wait()


def forward(place, x, blocks):
    return pl.pallas_call(
        forward_kernel,
        out_shape=(
            jax.ShapeDtypeStruct((CHIPS, PADDED, 512), BF16),
            jax.ShapeDtypeStruct(WEIGHTS, BF16),
            jax.ShapeDtypeStruct((4, 128, CHIPS * PADDED), BF16),
        ),
        in_specs=[SMEM] + [VMEM] * 11,
        out_specs=(ANY,) * 3,
        scratch_shapes=[
            pltpu.VMEM((CHIPS, PADDED, 512), BF16),
            pltpu.VMEM((10, CHIPS, PADDED, 128), F32),
            pltpu.SemaphoreType.DMA((CHIPS,)),
            pltpu.VMEM(WEIGHTS, BF16),
            pltpu.SemaphoreType.DMA,
            pltpu.VMEM((4, 128, CHIPS * PADDED), BF16),
            pltpu.SemaphoreType.DMA,
        ],
        compiler_params=params(51),
        cost_estimate=CONV_COST,
    )(place, x, *blocks)


def sigmoid(v):
    return 1.0 / (1.0 + jnp.exp(-v))


def middle_kernel(got, proj, cot, projected, send, grad):
    parts = []
    for yh in range(2):
        total = got[yh * 4].astype(F32)
        for x in range(1, 4):
            total = total + got[yh * 4 + x].astype(F32)
        parts.append(total[:CELLS])
    pre = jnp.concatenate(parts, 1).astype(BF16).astype(F32)
    sig = sigmoid(pre)
    acts = (pre * sig).astype(BF16)
    slope = sig + pre * sig * (1.0 - sig)
    weight = proj[...]
    out_pre = jnp.dot(acts, weight, preferred_element_type=F32)
    osig = sigmoid(out_pre)
    projected[...] = (out_pre * osig).astype(BF16)
    dout = (cot[...].astype(F32) * (osig + out_pre * osig * (1.0 - osig))).astype(BF16)
    dacts = lax.dot_general(
        dout, weight, (((1,), (1,)), ((), ())), preferred_element_type=F32
    )
    dpre = (dacts * slope).astype(BF16)
    for yh in range(2):
        for x in range(4):
            send[yh * 4 + x, :CELLS] = dpre[:, yh * 512 : (yh + 1) * 512]
            send[yh * 4 + x, CELLS:] = jnp.zeros((PADDED - CELLS, 512), BF16)
    grad[...] = lax.dot_general(
        acts, dout, (((0,), (0,)), ((), ())), preferred_element_type=F32
    )


def middle(got, proj, cot):
    return pl.pallas_call(
        middle_kernel,
        out_shape=(
            jax.ShapeDtypeStruct((CELLS, 256), BF16),
            jax.ShapeDtypeStruct((CHIPS, PADDED, 512), BF16),
            jax.ShapeDtypeStruct((1024, 256), F32),
        ),
        in_specs=[VMEM] * 3,
        out_specs=(VMEM,) * 3,
        compiler_params=params(48),
    )(got, proj, cot)


SPREAD = [pltpu.VMEM((9, CHIPS + 2 * HALO, PADDED, 128), BF16), pltpu.VMEM((CHIPS, PADDED, 128), BF16)]


def spread_point(got, point, j):
    point[j] = got[j, :, :128]


def spread_branch(got, moved, column, g, j):
    d = DILATIONS[g]
    v = got[j, :, (g + 1) * 128 : (g + 2) * 128]
    wide = v.astype(F32)
    minus = jnp.where(column < WIDTH - d, pltpu.roll(wide, PADDED - d, 0), 0.0)
    plus = jnp.where((column >= d) & (column < WIDTH), pltpu.roll(wide, d, 0), 0.0)
    for kx, part in enumerate((minus.astype(BF16), v, plus.astype(BF16))):
        moved[3 * g + kx, HALO + j] = part


def spread_edges(moved, g):
    for n in range(3 * g, 3 * g + 3):
        moved[n, :HALO] = jnp.zeros((HALO, PADDED, 128), BF16)
        moved[n, HALO + CHIPS :] = jnp.zeros((HALO, PADDED, 128), BF16)


def spread(got, moved, point):
    column = cell_column(PADDED)
    for g in range(3):
        spread_edges(moved, g)

    def step(j, _):
        spread_point(got, point, j)
        for g in range(3):
            spread_branch(got, moved, column, g, j)
        return 0

    lax.fori_loop(0, CHIPS, step, 0)


def spread_columns(moved, point, tap, first, count):
    _, g, ky, kx = tap
    if g < 0:
        v = point[pl.ds(first, count)]
    else:
        v = moved[3 * g + kx + 1, pl.ds(HALO + first - ky * (g + 1), count)]
    return v.reshape(count * PADDED, 128)


def kernel_grad_kernel(got, xt, keep, send, again, sent, xs, x_sem, g_sem, out_sem, moved, point):
    load = pltpu.make_async_copy(xt, xs, x_sem)
    load.start()
    copy_got = pltpu.make_async_copy(got, again, g_sem)
    copy_got.start()
    column = cell_column(PADDED)
    stores = []
    ready = -1
    for index, pair in enumerate(PAIRS):
        for g in range(ready + 1, max(tap[1] for tap in pair) + 1):
            spread_edges(moved, g)
            for j in range(CHIPS):
                if g == 0:
                    spread_point(got, point, j)
                spread_branch(got, moved, column, g, j)
            ready = g
        if index == 0:
            load.wait()
        left = xs[...].reshape(K, CHIPS * PADDED)
        right = jnp.concatenate([spread_columns(moved, point, tap, 0, CHIPS) for tap in pair], 1)
        part = jnp.dot(left, right, preferred_element_type=F32).astype(BF16)
        for half, tap in enumerate(pair):
            cols = pl.ds(tap[0] * 128, 128)
            block = part[:, half * 128 : (half + 1) * 128].reshape(2, 2, 8, 16, 128)
            for yh in range(2):
                keep[:, yh, :, cols] = block[0, yh]
                sent[:, yh, :, cols] = block[1, yh]
            view = (slice(None), slice(None), slice(None), cols)
            stores.append(pltpu.make_async_copy(sent.at[view], send.at[view], out_sem.at[tap[0]]))
            stores[-1].start()
    for copy in stores:
        copy.wait()
    copy_got.wait()


def kernel_grad(got, xt):
    return pl.pallas_call(
        kernel_grad_kernel,
        out_shape=(jax.ShapeDtypeStruct((8, 2, 16, COLS), BF16),) * 2
        + (jax.ShapeDtypeStruct((CHIPS, PADDED, 512), BF16),),
        in_specs=[VMEM, ANY],
        out_specs=(VMEM, ANY, ANY),
        scratch_shapes=[
            pltpu.VMEM((8, 2, 16, COLS), BF16),
            pltpu.VMEM((4, 128, CHIPS * PADDED), BF16),
            pltpu.SemaphoreType.DMA,
            pltpu.SemaphoreType.DMA,
            pltpu.SemaphoreType.DMA((TAPS,)),
        ]
        + SPREAD,
        compiler_params=params(52),
        cost_estimate=CONV_COST,
    )(got, xt)


def add_cores_kernel(mine, other, out):
    out[...] = (mine[...].astype(F32) + other[...].astype(F32)).astype(BF16)


def add_cores(mine, other):
    spec = pl.BlockSpec((2, 2, 16, COLS), lambda i: (i, 0, 0, 0))
    return pl.pallas_call(
        add_cores_kernel,
        grid=(4,),
        out_shape=jax.ShapeDtypeStruct((8, 2, 16, COLS), BF16),
        in_specs=[spec] * 2,
        out_specs=spec,
        compiler_params=params(16),
    )(mine, other)


def sum_samples_kernel(got, out):
    for yh in range(2):
        total = got[yh].astype(F32)
        for rep in range(1, 8):
            total = total + got[2 * rep + yh].astype(F32)
        out[yh] = total.astype(BF16)


def sum_samples(got):
    return pl.pallas_call(
        sum_samples_kernel,
        out_shape=jax.ShapeDtypeStruct((2, 16, COLS), BF16),
        in_specs=[VMEM],
        out_specs=VMEM,
        compiler_params=params(24),
    )(got)


def feature_grad_kernel(got, kept, out, moved, point, wt, w_sem):
    load = pltpu.make_async_copy(kept, wt, w_sem)
    load.start()
    spread(got, moved, point)
    load.wait()
    taps = [tap for pair in PAIRS for tap in pair]

    def step(i, _):
        left = jnp.concatenate([spread_columns(moved, point, tap, 2 * i, 2) for tap in taps], 1)
        right = weights_of(wt, [tap[0] for tap in taps])
        part = jnp.dot(left, right, preferred_element_type=F32).astype(BF16)
        for sub in range(2):
            out[2 * i + sub] = part[sub * PADDED : sub * PADDED + CELLS]
        return 0

    lax.fori_loop(0, CHIPS // 2, step, 0)


def feature_grad(got, kept):
    return pl.pallas_call(
        feature_grad_kernel,
        out_shape=jax.ShapeDtypeStruct((CHIPS, CELLS, K), BF16),
        in_specs=[VMEM, ANY],
        out_specs=VMEM,
        scratch_shapes=SPREAD + [pltpu.VMEM(WEIGHTS, BF16), pltpu.SemaphoreType.DMA],
        compiler_params=params(56),
        cost_estimate=CONV_COST,
    )(got, kept)


def pack_sums_kernel(mine, other, proj, out):
    for n, block in enumerate((mine, other)):
        for yh in range(2):
            out[n, yh, :, :COLS] = block[yh]
            for half in range(2):
                row = half * 64 + n * 32 + yh * 16
                lane = COLS + half * 256
                out[n, yh, :, lane : lane + 256] = proj[row : row + 16, :].astype(BF16)


def pack_sums(mine, other, proj):
    return pl.pallas_call(
        pack_sums_kernel,
        out_shape=jax.ShapeDtypeStruct((2, 2, 16, COLS + 512), BF16),
        in_specs=[VMEM] * 3,
        out_specs=VMEM,
        compiler_params=params(16),
    )(mine, other, proj)


def side_of(refs, d, l):
    return refs[2 + l] if d == 2 else refs[(0, 1, 2, 4)[d]].at[l]


def place_grads_kernel(place, *refs):
    point, atrous = refs[5], refs[6]
    z, yl = place[0], place[3]
    for d in range(4):
        for l in range(2):
            rep = 2 * lax.rem(z + 4 - d, 4) + lax.rem(yl + l, 2)
            rows = pl.ds(pl.multiple_of(rep * 16, 16), 16)
            for yh in range(2):
                cols = slice(yh * 128, (yh + 1) * 128)
                for t in range(TAPS):
                    part = side_of(refs, d, l)[yh, :, t * 128 : (t + 1) * 128].astype(F32) * 0.125
                    if t == 0:
                        point[rows, cols] = part
                    else:
                        atrous[t - 1, rows, cols] = part


def place_grads(place, blocks):
    return pl.pallas_call(
        place_grads_kernel,
        out_shape=(
            jax.ShapeDtypeStruct((128, 256), F32),
            jax.ShapeDtypeStruct((27, 128, 256), F32),
        ),
        in_specs=[SMEM] + [VMEM] * 5,
        out_specs=(VMEM,) * 2,
        compiler_params=params(40),
    )(place, *blocks)


def proj_half_kernel(place, *refs):
    out = refs[5]
    for d in range(4):
        z = lax.rem(place[0] + 4 - d, 4)
        row = gray(z) * 256 + (z >> 1) * 128
        for n in range(2):
            for yh in range(2):
                for half in range(2):
                    at = pl.multiple_of(row + half * 64 + n * 32 + yh * 16, 16)
                    lane = COLS + half * 256
                    out[pl.ds(at, 16), :] = side_of(refs, d, n)[yh, :, lane : lane + 256]


def proj_half(place, blocks):
    return pl.pallas_call(
        proj_half_kernel,
        out_shape=jax.ShapeDtypeStruct((512, 256), BF16),
        in_specs=[SMEM] + [VMEM] * 5,
        out_specs=VMEM,
        compiler_params=params(24),
    )(place, *blocks)


def join_proj_kernel(place, mine, other, out):
    c = place[2]
    for half, block in enumerate((mine, other)):
        yh = c if half == 0 else 1 - c
        for branch in range(4):
            part = block[branch * 128 : (branch + 1) * 128, :].astype(F32) * 0.125
            rows = pl.multiple_of(branch * 256 + yh * 128, 128)
            out[pl.ds(rows, 128), :] = part


def join_proj(place, mine, other):
    return pl.pallas_call(
        join_proj_kernel,
        out_shape=jax.ShapeDtypeStruct((1024, 256), F32),
        in_specs=[SMEM, VMEM, VMEM],
        out_specs=VMEM,
        compiler_params=params(16),
    )(place, mine, other)


def join_features_kernel(got, out):
    for x in range(4):
        total = (got[x].astype(F32) + got[4 + x].astype(F32)).astype(BF16)
        for yh in range(2):
            out[:, (yh * 4 + x) * 256 : (yh * 4 + x + 1) * 256] = total[:, yh * 256 : (yh + 1) * 256]


def join_features(got):
    return pl.pallas_call(
        join_features_kernel,
        out_shape=jax.ShapeDtypeStruct((CELLS, 2048), BF16),
        in_specs=[VMEM],
        out_specs=VMEM,
        compiler_params=params(16),
    )(got)


def turn(n, d):
    return [(i, (i + d) % n) for i in range(n)]


def swap(v, axis):
    return lax.ppermute(v, axis, turn(2, 1))


BESIDE = [(i, i ^ 1) for i in range(4)]
ACROSS = [(i, 3 - i) for i in range(4)]


def gray(i):
    return (i ^ (i >> 1)) & 1


def halved(v, axis, pairs, bit):
    half = v.shape[0] // 2
    mine = lax.dynamic_slice_in_dim(v, bit * half, half, 0)
    theirs = lax.dynamic_slice_in_dim(v, (1 - bit) * half, half, 0)
    return mine + lax.ppermute(theirs.astype(BF16), axis, pairs).astype(F32)


def added(v, axis, pairs):
    return v + lax.ppermute(v.astype(BF16), axis, pairs).astype(F32)


def shards(features, atrous_weight, point_weight, proj_weight, cotangent):
    place = jnp.stack([lax.axis_index(a) for a in ("z", "x", "c", "yl", "yh")]).astype(jnp.int32)

    atrous_t = jnp.transpose(atrous_weight, (0, 2, 1))
    z = lax.axis_index("z")
    taps = lax.dynamic_slice_in_dim(atrous_t, jnp.maximum(QUARTER * z - 1, 0), QUARTER, 0)
    with_point = jnp.concatenate([jnp.transpose(point_weight, (1, 0))[None], taps[: QUARTER - 1]], 0)
    parts = split_weights(place, jnp.where(z == 0, with_point, taps))
    from_x = [parts[0]] + [lax.ppermute(parts[d], "x", turn(4, d)) for d in (1, 2, 3)]
    quarter = stack_columns(place, from_x)
    below, above = (lax.ppermute(quarter, "z", turn(4, d)) for d in (1, 3))
    opposite = [lax.ppermute(above[:2], "z", turn(4, 3)), lax.ppermute(below[2:], "z", turn(4, 1))]
    quarters = [quarter, below, *opposite, above]
    blocks = quarters + [swap(v, "c") for v in quarters]

    x_send = split_features(features.reshape(CELLS, 2048))
    x_send, quarter = lax.optimization_barrier((x_send, quarter))
    x = lax.all_to_all(x_send, ("yh", "x"), 0, 0, tiled=True)

    partial, wt, xt = forward(place, x, blocks)
    got = lax.all_to_all(partial, ("yh", "x"), 0, 0, tiled=True)
    proj = proj_weight.reshape(4, 2, 128, 256).transpose(1, 0, 2, 3).reshape(1024, 256)
    projected, d_send, proj_part = middle(got, proj, cotangent.reshape(CELLS, 256))
    dpre = lax.all_to_all(d_send, ("yh", "x"), 0, 0, tiled=True)

    core, layer = lax.axis_index("c"), lax.axis_index("z")
    share = halved(proj_part, "c", turn(2, 1), core)
    share = halved(share, "z", BESIDE, gray(layer))
    share = halved(share, "z", ACROSS, layer >> 1)
    dpre, share = lax.optimization_barrier((dpre, share))
    share = added(share, "yh", turn(2, 1))

    keep, send, dpre = kernel_grad(dpre, xt)
    send, share = lax.optimization_barrier((send, share))
    other = swap(send, "c")
    share = added(share, "yl", turn(2, 1))
    other, share = lax.optimization_barrier((other, share))
    g_part = add_cores(keep, other)
    g_got = lax.all_to_all(g_part.reshape(16, 16, COLS), ("z", "yl", "yh"), 0, 0, tiled=True)

    dpre, _ = lax.optimization_barrier((dpre, g_part))
    back = feature_grad(dpre, wt)
    share, _ = lax.optimization_barrier((share, back))
    share = added(share, "x", BESIDE)
    share = added(share, "x", ACROSS)

    g_got, back, share = lax.optimization_barrier((g_got, back, share))
    g_sum = sum_samples(g_got)
    swapped = swap(g_sum, "yl")
    back, swapped = lax.optimization_barrier((back, swapped))
    pair = pack_sums(g_sum, swapped, share)
    below, above = lax.ppermute(pair, "z", turn(4, 1)), lax.ppermute(pair, "z", turn(4, 3))
    opposite = [lax.ppermute(above[0], "z", turn(4, 3)), lax.ppermute(below[1], "z", turn(4, 1))]
    pairs = [pair, below, *opposite, above]
    input_grad = join_features(lax.all_to_all(back, ("yh", "x"), 0, 0, tiled=True))
    half = proj_half(place, pairs)
    grad_point, grad_atrous = place_grads(place, pairs)
    grad_proj = join_proj(place, half, swap(half, "c"))

    return (
        projected.reshape(1, 3, WIDTH, 256),
        input_grad.reshape(1, 3, WIDTH, 2048),
        grad_point,
        grad_atrous,
        grad_proj,
    )


def solution(mesh):
    fine = Mesh(mesh.devices.reshape(4, 2, 2, 4, 2), ("z", "yl", "yh", "x", "c"))
    rep, sp = ("z", "yl"), ("yh", "x", "c")
    in_specs = (
        P(rep, sp, None, None),
        P(None, None, sp),
        P(None, sp),
        P(),
        P(rep, sp, None, None),
    )
    out_specs = (
        P(rep, sp, None, None),
        P(rep, sp, None, None),
        P(sp, None),
        P(None, sp, None),
        P(),
    )
    return jax.shard_map(shards, mesh=fine, in_specs=in_specs, out_specs=out_specs, check_vma=False)
```
